128 devices in a mesh: grp: 64 (over z_hi, y, x, core), seq: 2 (over z_lo).
Axes of the slice: x: 4, y: 4, z: 4 (z_hi: 2, z_lo: 2; z = z_hi * 2 + z_lo), core: 2. Of those that a mesh axis runs over, the one named last changes fastest.
Arguments:
- tokens: bfloat16 [32768, 768], P(('grp', 'seq')), may hold values from -6 to 6
- w_qkv: bfloat16 [768, 2304], P(('grp', 'seq')), may hold values from -0.21875 to 0.21875
- w_out: bfloat16 [768, 768], P(('grp', 'seq')), may hold values from -2.5 to 2.5
- w_up: bfloat16 [768, 3072], P(('grp', 'seq')), may hold values from -0.21875 to 0.21875
- w_down: bfloat16 [3072, 768], P(('grp', 'seq')), may hold values from -0.109375 to 0.109375
- gain_attn: bfloat16 [768], P(('grp', 'seq')), may hold values from 0.099609375 to 1.8984375
- gain_ffn: bfloat16 [768], P(('grp', 'seq')), may hold values from 0.099609375 to 1.8984375
- conv_taps: bfloat16 [3, 2304], P(None, ('grp', 'seq')), may hold values from -1 to 1
- cotangent: bfloat16 [32768, 768], P(('grp', 'seq')), may hold values from -6 to 6
Outputs:
- output: bfloat16 [32768, 768], P(('grp', 'seq'))
- grad_tokens: bfloat16 [32768, 768], P(('grp', 'seq'))
- grad_w_qkv: float32 [768, 2304], P(('grp', 'seq'))
- grad_w_out: float32 [768, 768], P(('grp', 'seq'))
- grad_w_up: float32 [768, 3072], P(('grp', 'seq'))
- grad_w_down: float32 [3072, 768], P(('grp', 'seq'))
- grad_gain_attn: float32 [768], P(('grp', 'seq'))
- grad_gain_ffn: float32 [768], P(('grp', 'seq'))
- grad_conv_taps: float32 [3, 2304], P(None, ('grp', 'seq'))
The draws below stay inside these ranges and needn't reach their ends.
All inputs are finite; a program needn't handle non-finite values.
Results may differ from the reference program's by a relative error of at most 0.017.
Values may be sent and summed in bfloat16 or wider, within the bound.
A program may use at most 128 MiB of HBM per device.

```python
import jax
import jax.numpy as jnp
from jax import lax

D = 768
HEADS = 12
HEAD_DIM = 64
FF = 3072
TAPS = 3
LENGTH = 512
TOKENS = 32768


def level_of(key, extent, cuts, smallest, top_value):
    level, own = 1.0, jax.random.fold_in(key, 6)
    for dim, blocks in cuts:
        draws = jnp.exp(jax.random.uniform(jax.random.fold_in(own, dim), (blocks,), jnp.float32, smallest / len(cuts), top_value / len(cuts)))
        level = level * jnp.repeat(draws, extent[dim] // blocks).reshape([-1 if axis == dim else 1 for axis in range(len(extent))])
    return level


def bell_draw(own_key, shape, scale, bound, shards=(), dtype=jnp.bfloat16):
    loudness = level_of(own_key, shape, shards, -0.22, 0.18) if shards else 1.0
    array = jax.random.normal(own_key, shape, jnp.float32) * scale * loudness
    return jnp.minimum(jnp.maximum(array, -bound), bound).astype(dtype)


def setup_inputs(seed: int = 0) -> dict:
    key_of = jax.random.split(jax.random.key(seed), 10)
    return {
        "tokens": bell_draw(key_of[0], (TOKENS, D), 1.0, 6.0, ((0, 128),)),
        "w_qkv": bell_draw(key_of[1], (D, 3 * D), D ** -0.5, 0.21875, ((0, 128),)),
        "w_out": bell_draw(key_of[2], (D, D), (max(D * 4 // LENGTH, 1)) ** -0.5, 2.5, ((0, 128),)),
        "w_up": bell_draw(key_of[3], (D, FF), D ** -0.5, 0.21875, ((0, 128),)),
        "w_down": bell_draw(key_of[4], (FF, D), FF ** -0.5, 0.109375, ((0, 128),)),
        "gain_attn": jnp.clip(1.0 + 0.18 * jax.random.normal(key_of[5], (D,), jnp.float32), 0.099609375, 1.8984375).astype(jnp.bfloat16),
        "gain_ffn": jnp.clip(1.0 + 0.18 * jax.random.normal(key_of[6], (D,), jnp.float32), 0.099609375, 1.8984375).astype(jnp.bfloat16),
        "conv_taps": jnp.clip(jax.random.uniform(key_of[7], (TAPS, 3 * D), jnp.float32, -1.0, 1.0) * level_of(key_of[7], (TAPS, 3 * D), ((1, 128),), -0.4, 0.0), -1.0, 1.0).astype(jnp.bfloat16),
        "cotangent": bell_draw(key_of[8], (TOKENS, D), 1.0, 6.0, ((0, 128),)),
    }


@jax.custom_vjp
def low(v):
    return lax.optimization_barrier(v.astype(jnp.bfloat16)).astype(jnp.float32)

@jax.custom_vjp
def low_back(v):
    return v

def low_keep(v):
    return (low(v), None)

def low_pass(kept, grad):
    return (grad,)

def back_keep(v):
    return (v, None)

def back_low(kept, grad):
    return (low(grad),)
low.defvjp(low_keep, low_pass)
low_back.defvjp(back_keep, back_low)
HIGH = lax.Precision.HIGHEST
epsilon = 1e-05

def layer_norm(values, gain):
    mean = lax.optimization_barrier(jnp.mean(values, axis=-1, keepdims=True))
    centred = values - mean
    variance = lax.optimization_barrier(jnp.mean(centred * centred, axis=-1, keepdims=True))
    return centred * lax.rsqrt(variance + epsilon) * gain

def causal_conv(values, taps):
    first = jnp.concatenate([jnp.zeros_like(values[:1]), values[:-1]], axis=0)
    second = jnp.concatenate([jnp.zeros_like(values[:2]), values[:-2]], axis=0)
    return taps[0] * values + taps[1] * first + taps[2] * second

def head_attention(operands):
    query, key, value = operands
    scale = HEAD_DIM ** (-0.5)
    scores = low_back(jnp.dot(query, key.T, precision=HIGH) * scale)
    rows = lax.broadcasted_iota(jnp.int32, scores.shape, 0)
    columns = lax.broadcasted_iota(jnp.int32, scores.shape, 1)
    masked = jnp.where(columns <= rows, scores, -1e+30)
    probs = low(jax.nn.softmax(masked, axis=-1))
    return jnp.dot(probs, value, precision=HIGH)

def split_heads(block):
    return block.reshape(block.shape[0], HEADS, HEAD_DIM).transpose(1, 0, 2)

def sequence_forward(inputs, w_qkv, w_out, w_up, w_down, gain_attn, gain_ffn, conv_taps):
    length = inputs.shape[0]
    hidden_one = low(layer_norm(inputs, gain_attn))
    qkv = low_back(low(jnp.dot(hidden_one, w_qkv, precision=HIGH)))
    mixed = low(causal_conv(qkv, conv_taps))
    query = split_heads(mixed[:, :D])
    key = split_heads(mixed[:, D:2 * D])
    value = split_heads(mixed[:, 2 * D:])
    heads = lax.map(jax.checkpoint(head_attention), (query, key, value))
    attended = heads.transpose(1, 0, 2).reshape(length, D)
    attended = low_back(low(attended))
    resid = inputs + low_back(jnp.dot(attended, w_out, precision=HIGH))
    hidden_two = low(layer_norm(resid, gain_ffn))
    up = low_back(jnp.dot(hidden_two, w_up, precision=HIGH))
    act = low(jnp.square(jax.nn.relu(up)))
    return resid + low_back(jnp.dot(act, w_down, precision=HIGH))

def reference(tokens, w_qkv, w_out, w_up, w_down, gain_attn, gain_ffn, conv_taps, cotangent):
    floats = [a.astype(jnp.float32) for a in (tokens, w_qkv, w_out, w_up, w_down, gain_attn, gain_ffn, conv_taps)]

    def forward(inputs, wq, wo, wu, wd, ga, gf, taps):
        count = inputs.shape[0] // LENGTH
        blocks = inputs.reshape(count, LENGTH, D)

        def one_sequence(block):
            return sequence_forward(block, wq, wo, wu, wd, ga, gf, taps)
        results = lax.map(jax.checkpoint(one_sequence), blocks)
        return results.reshape(inputs.shape[0], D)
    output, pullback = jax.vjp(forward, *floats)
    grads = pullback(cotangent.astype(jnp.float32))
    return (output.astype(jnp.bfloat16), grads[0].astype(jnp.bfloat16), grads[1], grads[2], grads[3], grads[4], grads[5], grads[6], grads[7])
```

```python
import functools

import jax
import jax.numpy as jnp
from jax import lax
from jax.experimental import pallas as pl
from jax.experimental.pallas import tpu as pltpu
from jax.sharding import PartitionSpec as P

MESH = pl.DeviceIdType.MESH
F32 = jnp.float32
BF16 = jnp.bfloat16
EPS = 1e-05
D = 768
ROWS = 256
EXT = 512
PAIRS = 6
TILES = 18
BLOCK = (48, 384)
GRID = (2, 2, 2, 4, 2, 2)
VEC = 80
ORDERS = (("x", "y", "z"), ("y", "z", "x"), ("z", "x", "y"))
BACK = (("z", "y", "x"), ("x", "z", "y"), ("y", "x", "z"))
LIMIT = 60 * 2**20


class Place:
    def __init__(self, send_sem, recv_sem):
        grp, seq = lax.axis_index("grp"), lax.axis_index("seq")
        self.c = lax.rem(grp, 2)
        self.x = lax.rem(lax.div(grp, 2), 4)
        self.y = lax.rem(lax.div(grp, 8), 4)
        self.z = lax.div(grp, 32) * 2 + seq
        self.zl = seq
        self.index = grp * 2 + seq
        self.send_sem, self.recv_sem = send_sem, recv_sem
        self.used = 0
        self.sent = []

    def device(self, **new):
        at = {"x": self.x, "y": self.y, "z": self.z, "c": self.c}
        at.update(new)
        grp = ((lax.div(at["z"], 2) * 4 + at["y"]) * 4 + at["x"]) * 2 + at["c"]
        return (grp, lax.rem(at["z"], 2))

    def along(self, axis, delta):
        return lax.rem(getattr(self, axis) + delta, 4)

    def flip(self, value, bit):
        return value + bit * (1 - 2 * lax.rem(value, 2))

    def member(self, d):
        x, c, z = self.flip(self.x, d // 4), self.flip(self.c, (d // 2) % 2), self.flip(self.z, d % 2)
        number = lax.rem(x, 2) * 4 + c * 2 + lax.rem(z, 2)
        return self.device(x=x, c=c, z=z), number

    def greet(self):
        barrier = pltpu.get_barrier_semaphore()
        partners = [self.device(**{a: self.along(a, d)}) for a in "xyz" for d in (1, 2, 3)]
        partners += [self.member(d)[0] for d in (2, 3, 5, 6, 7)]
        for partner in partners:
            pl.semaphore_signal(barrier, inc=1, device_id=partner, device_id_type=MESH)
        pl.semaphore_wait(barrier, len(partners))

    def slot(self):
        self.used += 1
        return self.used - 1

    def copy(self, src, dst, device, slot):
        return pltpu.make_async_remote_copy(
            src_ref=src,
            dst_ref=dst,
            send_sem=self.send_sem.at[slot],
            recv_sem=self.recv_sem.at[slot],
            device_id=device,
            device_id_type=MESH,
        )

    def send(self, src, dst, device, slot):
        self.copy(src, dst, device, slot).start()
        self.sent.append((src, device, slot))

    def arrive(self, dst, slot):
        self.copy(dst, dst, self.device(), slot).wait_recv()

    def drain(self):
        for src, device, slot in self.sent:
            self.copy(src, src, device, slot).wait_send()
        self.sent = []


def slab(ref, lead=(), c=None, **at):
    index = list(lead) + [slice(None) if c is None else c]
    for axis in "zyx":
        value = at.get(axis)
        half = isinstance(value, tuple)
        if axis == "y":
            index.append(pl.ds(2 * value[1], 2) if half else slice(None) if value is None else value)
        elif half:
            index += [value[1], slice(None)]
        elif value is None:
            index += [slice(None), slice(None)]
        else:
            index += [lax.div(value, 2), lax.rem(value, 2)]
    return ref.at[tuple(index)]


def total_of(place, vec, incoming):
    for stage, axis in enumerate("cxyz"):
        steps = (1,) if axis == "c" else (1, 2, 3)
        slots = [place.slot() for _ in steps]
        for k, step in enumerate(steps):
            device = place.device(c=1 - place.c) if axis == "c" else place.device(**{axis: place.along(axis, step)})
            place.send(vec.at[stage], incoming.at[stage, k], device, slots[k])
        total = vec[stage]
        for k, step in enumerate(steps):
            place.arrive(incoming.at[stage, k], slots[k])
            total = total + incoming[stage, k]
        vec[stage + 1] = total
        yield


def spread(index, count, width):
    row = lax.broadcasted_iota(jnp.int32, (128, width), 0)
    column = lax.broadcasted_iota(jnp.int32, (128, width), 1)
    return jnp.where((column == count * index + row) & (row < count), 1.0, 0.0)


def gather_kernel(tok, wq, wo, wu, wd, ga, gf, taps, w_out, vec_out, prev, to_peer, from_peer, pile, down_s, down, few, vec, incoming, send_sem, recv_sem):
    place = Place(send_sem, recv_sem)
    c, zl = place.c, place.zl
    for number in range(8):
        source = wq[:, number * 384:(number + 1) * 384] if number < 6 else wo[:, (number - 6) * 384:(number - 5) * 384]
        to_peer[number, 0, 0:6, :] = source.astype(F32)
        to_peer[number, 1, 0:6, :] = wu[:, number * 384:(number + 1) * 384].astype(F32)
    left, right = wd[:, 0:384].astype(F32), wd[:, 384:768].astype(F32)
    down_s[...] = jnp.where(zl == 0, right, left)
    down[pl.ds(pl.multiple_of(zl * 24, 8), 24), :] = jnp.where(zl == 0, left, right)
    few[...] = jnp.zeros_like(few)
    few[0:1, 0:6] = ga[...].astype(F32)
    few[1:2, 0:6] = gf[...].astype(F32)
    few[2:5, 0:18] = taps[...].astype(F32)
    low = few[...].astype(BF16)
    gains = jnp.dot(low, spread(place.index, 6, D).astype(BF16), preferred_element_type=F32)
    tapped = jnp.dot(low, spread(place.index, 18, 3 * D).astype(BF16), preferred_element_type=F32)
    vec[0] = jnp.zeros((VEC, 128), F32)
    for r in range(6):
        vec[0, r:r + 1, :] = gains[0:1, r * 128:(r + 1) * 128]
        vec[0, 6 + r:7 + r, :] = gains[1:2, r * 128:(r + 1) * 128]
    for j in range(3):
        for t in range(TILES):
            row = 12 + TILES * j + t
            vec[0, row:row + 1, :] = tapped[2 + j:3 + j, t * 128:(t + 1) * 128]

    place.greet()
    other = place.device(z=place.flip(place.z, 1))
    trade = [place.slot() for _ in range(8)]
    _, mine = place.member(0)
    for d in range(1, 8):
        device, number = place.member(d)
        place.send(to_peer.at[number], from_peer.at[mine], device, trade[d])
    place.send(down_s, down.at[pl.ds(pl.multiple_of(zl * 24, 8), 24)], other, trade[0])
    token_slot = place.slot()

    @pl.when(zl == 0)
    def _():
        place.copy(tok, prev, other, token_slot).start()

    @pl.when(zl == 1)
    def _():
        place.arrive(prev, token_slot)

    @pl.when(zl == 0)
    def _():
        prev[...] = jnp.zeros_like(prev)

    sums = total_of(place, vec, incoming)
    from_peer[mine] = to_peer[mine]
    for d in range(1, 8):
        _, number = place.member(d)
        place.arrive(from_peer.at[number], trade[d])
    place.arrive(down.at[pl.ds(pl.multiple_of((1 - zl) * 24, 8), 24)], trade[0])
    for number in range(8):
        for k in range(2):
            pile[k, 6 * number:6 * number + 8, :] = from_peer[number, k]
    at = (c, lax.div(place.z, 2), zl, place.y, lax.div(place.x, 2), lax.rem(place.x, 2))
    for k in range(2):
        w_out[(k,) + at] = pile[k, 0:48, :].astype(BF16)
    w_out[(2,) + at] = down[...].astype(BF16)

    here = {"x": place.x, "y": place.y, "z": place.z}
    sibling = place.device(c=1 - c)
    passed = []

    def pass_on(part, spot):
        slot = place.slot()
        place.send(slab(w_out, (part,), c, **spot), slab(w_out, (part,), c, **spot), sibling, slot)
        passed.append((part, spot, slot))

    for stage in range(2):
        waits = []
        for part in range(3):
            axis, done = ORDERS[part][stage], ORDERS[part][:stage]
            spot = {a: here[a] for a in "xyz" if a not in done}
            for step in (1, 2, 3):
                slot = place.slot()
                piece = slab(w_out, (part,), c, **spot)
                place.send(piece, piece, place.device(**{axis: place.along(axis, step)}), slot)
                waits.append((part, {**spot, axis: place.along(axis, 4 - step)}, slot))
        next(sums)
        for part, spot, slot in waits:
            place.arrive(slab(w_out, (part,), c, **spot), slot)
    first = [[place.slot() for _ in range(4)] for _ in range(3)]
    for part in range(3):
        axis = ORDERS[part][2]
        piece = slab(w_out, (part,), c, **{axis: here[axis]})
        place.send(piece, piece, place.device(**{axis: place.along(axis, 1)}), first[part][0])
        place.send(piece, piece, place.device(**{axis: place.along(axis, 3)}), first[part][1])
        pass_on(part, {axis: here[axis]})
    next(sums)
    for side in range(2):
        for part in range(3):
            axis, whole = ORDERS[part][2], ORDERS[part][0]
            came = {axis: place.along(axis, 3 if side == 0 else 1)}
            place.arrive(slab(w_out, (part,), c, **came), first[part][side])
            piece = slab(w_out, (part,), c, **came, **{whole: ("half", side)})
            place.send(piece, piece, place.device(**{axis: place.along(axis, 1 if side == 0 else 3)}), first[part][2 + side])
            pass_on(part, came)
    next(sums)
    for side in range(2):
        for part in range(3):
            axis, whole = ORDERS[part][2], ORDERS[part][0]
            came = {axis: place.along(axis, 2), whole: ("half", side)}
            place.arrive(slab(w_out, (part,), c, **came), first[part][2 + side])
            pass_on(part, came)
    vec_out[...] = vec[4]
    for part, spot, slot in passed:
        place.arrive(slab(w_out, (part,), 1 - c, **spot), slot)
    place.drain()

    @pl.when(zl == 0)
    def _():
        place.copy(tok, tok, other, token_slot).wait_send()


def gather(tok, wq, wo, wu, wd, ga, gf, taps):
    vmem = pl.BlockSpec(memory_space=pltpu.VMEM)
    return pl.pallas_call(
        gather_kernel,
        out_shape=(
            jax.ShapeDtypeStruct((3,) + GRID + BLOCK, BF16),
            jax.ShapeDtypeStruct((VEC, 128), F32),
            jax.ShapeDtypeStruct((ROWS, D), BF16),
        ),
        in_specs=[vmem] * 8,
        out_specs=(vmem,) * 3,
        scratch_shapes=[
            pltpu.VMEM((8, 2, 8, 384), F32),
            pltpu.VMEM((8, 2, 8, 384), F32),
            pltpu.VMEM((2, 56, 384), F32),
            pltpu.VMEM((24, 384), F32),
            pltpu.VMEM((48, 384), F32),
            pltpu.VMEM((8, 128), F32),
            pltpu.VMEM((5, VEC, 128), F32),
            pltpu.VMEM((4, 3, VEC, 128), F32),
            pltpu.SemaphoreType.DMA((80,)),
            pltpu.SemaphoreType.DMA((80,)),
        ],
        compiler_params=pltpu.CompilerParams(collective_id=0, has_side_effects=True, vmem_limit_bytes=LIMIT),
    )(tok, wq, wo, wu, wd, ga, gf, taps)


def nt(left, right):
    return lax.dot_general(left, right, (((1,), (1,)), ((), ())), preferred_element_type=F32)


def tn(left, right):
    return lax.dot_general(left, right, (((0,), (0,)), ((), ())), preferred_element_type=F32)


def nn(left, right):
    return jnp.dot(left, right, preferred_element_type=F32)


def columns(ref, part, jp):
    halves = [ref[part, lax.rem(jp, 2), :, zl, :, :, lax.div(jp, 2)].reshape(D, 384) for zl in range(2)]
    return jnp.concatenate(halves, axis=1)


def put_columns(ref, part, jp, value):
    for zl in range(2):
        ref[part, lax.rem(jp, 2), :, zl, :, :, lax.div(jp, 2)] = (
            value[:, zl * 384:(zl + 1) * 384].astype(BF16).reshape(2, 4, 2, 48, 384)
        )


def row_pieces():
    return [(y, xh, xl, c) for y in range(2) for xh in range(2) for xl in range(2) for c in range(2)]


def rows(ref, jp):
    zh, y0 = lax.div(jp, 2), lax.rem(jp, 2) * 2
    halves = [
        jnp.concatenate([ref[2, c, zh, zl, y0 + y, xh, xl] for y, xh, xl, c in row_pieces()], axis=0) for zl in range(2)
    ]
    return jnp.concatenate(halves, axis=1)


def put_rows(ref, jp, value):
    zh, y0 = lax.div(jp, 2), lax.rem(jp, 2) * 2
    low = value.astype(BF16)
    for zl in range(2):
        for k, (y, xh, xl, c) in enumerate(row_pieces()):
            ref[2, c, zh, zl, y0 + y, xh, xl] = low[48 * k:48 * k + 48, zl * 384:(zl + 1) * 384]


def normalize(values):
    mean = jnp.mean(values, axis=-1, keepdims=True)
    centred = values - mean
    inverse = lax.rsqrt(jnp.mean(centred * centred, axis=-1, keepdims=True) + EPS)
    return centred * inverse, inverse


def norm_back(grad, normed, inverse):
    first = jnp.mean(grad, axis=-1, keepdims=True)
    second = jnp.mean(grad * normed, axis=-1, keepdims=True)
    return inverse * (grad - first - normed * second)


def shifted(values, steps):
    count = values.shape[0]
    row = lax.broadcasted_iota(jnp.int32, values.shape, 0)
    rolled = pltpu.roll(values, steps % count, 0)
    return jnp.where(row >= steps if steps > 0 else row < count + steps, rolled, 0.0)


def layer_kernel(tok, prev, cot, w, vec, out, partial, contrib, g, gvec, h1, n1, inv1, raw, mixed, bias, probs, att, h2, gh2, gatt, gqkv, gh1, acc):
    rank = lax.axis_index("seq")
    gain_one = jnp.concatenate([vec[r:r + 1, :] for r in range(6)], axis=1)
    gain_two = jnp.concatenate([vec[r:r + 1, :] for r in range(6, 12)], axis=1)
    gvec[...] = jnp.zeros_like(gvec)
    for half in range(2):
        values = (prev if half == 0 else tok)[...].astype(F32)
        normed, inverse = normalize(values)
        here = pl.ds(half * ROWS, ROWS)
        n1[here, :] = normed
        inv1[here, :] = inverse
        h1[here, :] = (normed * gain_one).astype(BF16)

    def tap(j, t):
        return vec[pl.ds(12 + TILES * j + t, 1), :]

    @pl.loop(0, 3)
    def _(jp):
        block = nn(h1[...], columns(w, 0, jp)).astype(BF16)
        for k in range(6):
            t = 6 * jp + k
            tile = block[:, 128 * k:128 * (k + 1)]
            raw[t] = tile
            value = tile.astype(F32)
            conv = tap(0, t) * value + tap(1, t) * shifted(value, 1) + tap(2, t) * shifted(value, 2)
            mixed[t] = conv.astype(BF16)

    row = lax.broadcasted_iota(jnp.int32, (ROWS, EXT), 0)
    column = lax.broadcasted_iota(jnp.int32, (ROWS, EXT), 1)
    behind = jnp.where(column < ROWS, (1 - rank) * EXT, column - ROWS)
    bias[...] = jnp.where(behind <= row, 0.0, -1e30)
    first = lax.broadcasted_iota(jnp.int32, (ROWS, 128), 1) < 64

    def both(value):
        zero = jnp.zeros_like(value)
        return jnp.concatenate([jnp.where(first, value, zero), jnp.where(first, zero, value)], axis=0)

    def pick(value):
        return jnp.where(first, value[:ROWS], value[ROWS:])

    @pl.loop(0, PAIRS)
    def _(p):
        query = both(mixed[p, ROWS:, :])
        key, value = mixed[PAIRS + p], mixed[2 * PAIRS + p]
        scores = nt(query, key) * 0.125 + jnp.concatenate([bias[...], bias[...]], axis=0)
        weights = jnp.exp(scores - jnp.max(scores, axis=-1, keepdims=True))
        exact = weights * (1.0 / jnp.sum(weights, axis=-1, keepdims=True))
        probs[p] = exact
        att[p] = pick(nn(exact.astype(BF16), value)).astype(BF16)

    attended = jnp.concatenate([att[p] for p in range(PAIRS)], axis=1)
    resid = tok[...].astype(F32) + nn(attended, columns(w, 0, 3))
    normed_two, inverse_two = normalize(resid)
    h2[...] = (normed_two * gain_two).astype(BF16)
    acc[...] = resid
    gh2[...] = jnp.zeros_like(gh2)

    @pl.loop(0, 4)
    def _(jp):
        up = columns(w, 1, jp)
        down = rows(w, jp)
        rect = jnp.maximum(nn(h2[...], up), 0.0)
        act = (rect * rect).astype(BF16)
        acc[...] += nn(act, down)
        gact = nt(cot[...], down)
        put_rows(g, jp, tn(act, cot[...]))
        gup = (gact * 2.0 * rect).astype(BF16)
        put_columns(g, 1, jp, tn(h2[...], gup))
        gh2[...] += nt(gup, up)

    out[...] = acc[...].astype(BF16)
    grad_two = gh2[...]
    summed = jnp.sum(grad_two * normed_two, axis=0, keepdims=True)
    for r in range(6):
        gvec[6 + r:7 + r, :] = summed[:, 128 * r:128 * (r + 1)]
    grad_resid = cot[...].astype(F32) + norm_back(grad_two * gain_two, normed_two, inverse_two)
    acc[...] = grad_resid
    gproj = grad_resid.astype(BF16)
    put_columns(g, 0, 3, tn(attended, gproj))
    gback = nt(gproj, columns(w, 0, 3)).astype(BF16)
    for p in range(PAIRS):
        gatt[p] = gback[:, 128 * p:128 * (p + 1)]

    @pl.loop(0, PAIRS)
    def _(p):
        query = both(mixed[p, ROWS:, :])
        key, value = mixed[PAIRS + p], mixed[2 * PAIRS + p]
        grad = both(gatt[p])
        exact = probs[p]
        gvalue = tn(exact.astype(BF16), grad)
        gprobs = nt(grad, value)
        centred = gprobs - jnp.sum(gprobs * exact, axis=-1, keepdims=True)
        gscores = (exact * centred).astype(BF16)
        gquery = pick(nn(gscores, key)) * 0.125
        gkey = tn(gscores, query) * 0.125
        for k, tile in enumerate((jnp.concatenate([jnp.zeros_like(gquery), gquery], axis=0), gkey, gvalue)):
            t = PAIRS * k + p
            back = tap(0, t) * tile + tap(1, t) * shifted(tile, -1) + tap(2, t) * shifted(tile, -2)
            gqkv[t] = back.astype(BF16)
            value_in = raw[t].astype(F32)
            for j in range(3):
                delayed = value_in if j == 0 else shifted(value_in, j)
                gvec[pl.ds(12 + TILES * j + t, 1), :] = jnp.sum(tile * delayed, axis=0, keepdims=True)

    gh1[...] = jnp.zeros_like(gh1)

    @pl.loop(0, 3)
    def _(jp):
        grad = jnp.concatenate([gqkv[6 * jp + k] for k in range(6)], axis=1)
        put_columns(g, 0, jp, tn(h1[...], grad))
        gh1[...] += nt(grad, columns(w, 0, jp))

    total = jnp.zeros((1, D), F32)
    for half in range(2):
        here = pl.ds(half * ROWS, ROWS)
        grad_one = gh1[here, :]
        total = total + jnp.sum(grad_one * n1[here, :], axis=0, keepdims=True)
        back = norm_back(grad_one * gain_one, n1[here, :], inv1[here, :])
        if half == 0:
            contrib[...] = back.astype(BF16)
        else:
            partial[...] = acc[...] + back
    for r in range(6):
        gvec[r:r + 1, :] = total[:, 128 * r:128 * (r + 1)]


def layer(tok, prev, cot, w, vec):
    vmem = pl.BlockSpec(memory_space=pltpu.VMEM)
    return pl.pallas_call(
        layer_kernel,
        out_shape=(
            jax.ShapeDtypeStruct((ROWS, D), BF16),
            jax.ShapeDtypeStruct((ROWS, D), F32),
            jax.ShapeDtypeStruct((ROWS, D), BF16),
            jax.ShapeDtypeStruct((3,) + GRID + BLOCK, BF16),
            jax.ShapeDtypeStruct((VEC, 128), F32),
        ),
        in_specs=[vmem] * 5,
        out_specs=(vmem,) * 5,
        scratch_shapes=[
            pltpu.VMEM((EXT, D), BF16),
            pltpu.VMEM((EXT, D), F32),
            pltpu.VMEM((EXT, 1), F32),
            pltpu.VMEM((TILES, EXT, 128), BF16),
            pltpu.VMEM((TILES, EXT, 128), BF16),
            pltpu.VMEM((ROWS, EXT), F32),
            pltpu.VMEM((PAIRS, EXT, EXT), F32),
            pltpu.VMEM((PAIRS, ROWS, 128), BF16),
            pltpu.VMEM((ROWS, D), BF16),
            pltpu.VMEM((ROWS, D), F32),
            pltpu.VMEM((PAIRS, ROWS, 128), BF16),
            pltpu.VMEM((TILES, EXT, 128), BF16),
            pltpu.VMEM((EXT, D), F32),
            pltpu.VMEM((ROWS, D), F32),
        ],
        compiler_params=pltpu.CompilerParams(vmem_limit_bytes=LIMIT),
    )(tok, prev, cot, w, vec)


def kept(axes):
    grid = []
    for axis in "zyx":
        if axis not in axes:
            grid += {"z": [2, 2], "y": [4], "x": [2, 2]}[axis]
    return tuple(grid)


def flat(grid):
    count = 1
    for n in grid:
        count *= n
    return count


def unflat(k, grid):
    index = []
    for n in reversed(grid):
        index.insert(0, lax.rem(k, n))
        k = lax.div(k, n)
    return index


def reduce_kernel(partial, contrib, gvec, g_in, gtok, gq, go, gu, gd, gga, ggf, gtap, g, from_core, *scratch):
    lands, (got, vec, incoming, pieces, arrived, down, sums, load_sem, send_sem, recv_sem) = scratch[:9], scratch[9:]
    load = pltpu.make_async_copy(g_in, g, load_sem)
    load.start()
    place = Place(send_sem, recv_sem)
    c, zl = place.c, place.zl
    place.greet()
    load.wait()
    here = {"x": place.x, "y": place.y, "z": place.z}
    sibling = place.device(c=1 - c)
    other = place.device(z=place.flip(place.z, 1))
    token_slot = place.slot()

    @pl.when(zl == 1)
    def _():
        place.copy(contrib, got, other, token_slot).start()

    core = [place.slot() for _ in range(3)]
    for part in range(3):
        place.send(slab(g, (part,), 1 - c), from_core.at[part], sibling, core[part])
    vec[0] = gvec[...]
    small = total_of(place, vec, incoming)
    next(small)
    for part in range(3):
        place.arrive(from_core.at[part], core[part])

        @pl.loop(0, 64)
        def _(k):
            at = unflat(k, (2, 2, 4, 2, 2))
            spot = (part, c, *at)
            g[spot] = (g[spot].astype(F32) + from_core[(part, *at)].astype(F32)).astype(BF16)

    stages = [lands[3 * stage:3 * stage + 3] for stage in range(3)]
    for stage in range(3):
        waits = []
        for part in range(3):
            axis, done = BACK[part][stage], BACK[part][:stage]
            spot = {a: here[a] for a in done}
            for step in (1, 2, 3):
                slot = place.slot()
                there = place.along(axis, step)
                place.send(slab(g, (part,), c, **{**spot, axis: there}), stages[stage][part].at[step - 1], place.device(**{axis: there}), slot)
                waits.append(slot)
        next(small)
        for part in range(3):
            axis, done = BACK[part][stage], BACK[part][:stage]
            for step in (1, 2, 3):
                place.arrive(stages[stage][part].at[step - 1], waits[part * 3 + step - 1])
            spot = {a: here[a] for a in done + (axis,)}
            grid = kept(done + (axis,))
            land = stages[stage][part]

            def add(at):
                index, rest = [part, c], list(at)
                for a in "zyx":
                    if a in spot:
                        index += [spot[a]] if a == "y" else [lax.div(spot[a], 2), lax.rem(spot[a], 2)]
                    elif a == "y":
                        index.append(rest.pop(0))
                    else:
                        index += [rest.pop(0), rest.pop(0)]
                index = tuple(index)
                total = g[index].astype(F32)
                for step in range(3):
                    total = total + land[(step, *at)].astype(F32)
                if stage < 2:
                    g[index] = total.astype(BF16)
                else:
                    sums[part] = total

            if stage == 2:
                add(())
            else:
                pl.loop(0, flat(grid))(lambda k: add(unflat(k, grid)))
    _, mine = place.member(0)
    for number in range(8):
        for k in range(2):
            pieces[number, k, 0:6, :] = sums[k, 6 * number:6 * number + 6, :]
            pieces[number, k, 6:8, :] = jnp.zeros((2, 384), F32)
    trade = [place.slot() for _ in range(8)]
    for d in range(1, 8):
        device, number = place.member(d)
        place.send(pieces.at[number], arrived.at[mine], device, trade[d])
    place.send(sums.at[2, pl.ds(pl.multiple_of((1 - zl) * 24, 8), 24)], down, other, trade[0])
    arrived[mine] = pieces[mine]
    summed = vec[4]
    gains = [jnp.concatenate([summed[r:r + 1] for r in range(6 * k, 6 * k + 6)], axis=1) for k in range(2)]
    tapped = [jnp.concatenate([summed[r:r + 1] for r in range(12 + TILES * j, 12 + TILES * j + TILES)], axis=1) for j in range(3)]
    gain_rows = jnp.concatenate(gains + [jnp.zeros((6, D), F32)], axis=0)
    tap_rows = jnp.concatenate(tapped + [jnp.zeros((5, 3 * D), F32)], axis=0)
    high = functools.partial(
        lax.dot_general,
        dimension_numbers=(((1,), (1,)), ((), ())),
        preferred_element_type=F32,
        precision=lax.Precision.HIGHEST,
    )
    gain_own = high(gain_rows, spread(place.index, 6, D))
    gga[...] = gain_own[0:1, 0:6]
    ggf[...] = gain_own[1:2, 0:6]
    gtap[...] = high(tap_rows, spread(place.index, 18, 3 * D))[0:3, 0:18]

    @pl.when(zl == 0)
    def _():
        place.arrive(got, token_slot)

    @pl.when(zl == 1)
    def _():
        got[...] = jnp.zeros_like(got)

    gtok[...] = (partial[...] + got[...].astype(F32)).astype(BF16)
    for d in range(1, 8):
        _, number = place.member(d)
        place.arrive(arrived.at[number], trade[d])
    place.arrive(down, trade[0])
    for number in range(8):
        if number < 6:
            gq[:, 384 * number:384 * (number + 1)] = arrived[number, 0, 0:6, :]
        else:
            go[:, 384 * (number - 6):384 * (number - 5)] = arrived[number, 0, 0:6, :]
        gu[:, 384 * number:384 * (number + 1)] = arrived[number, 1, 0:6, :]
    own = sums[2, pl.ds(pl.multiple_of(zl * 24, 8), 24), :]
    gd[:, 0:384] = jnp.where(zl == 0, own, down[...])
    gd[:, 384:768] = jnp.where(zl == 0, down[...], own)
    place.drain()

    @pl.when(zl == 1)
    def _():
        place.copy(contrib, contrib, other, token_slot).wait_send()


def reduce(partial, contrib, gvec, g):
    vmem = pl.BlockSpec(memory_space=pltpu.VMEM)
    lands = []
    for stage in range(3):
        for part in range(3):
            grid = kept(BACK[part][:stage + 1])
            lands.append(pltpu.VMEM((3,) + grid + BLOCK, BF16))
    return pl.pallas_call(
        reduce_kernel,
        out_shape=(
            jax.ShapeDtypeStruct((ROWS, D), BF16),
            jax.ShapeDtypeStruct((6, 2304), F32),
            jax.ShapeDtypeStruct((6, 768), F32),
            jax.ShapeDtypeStruct((6, 3072), F32),
            jax.ShapeDtypeStruct((24, 768), F32),
            jax.ShapeDtypeStruct((1, 6), F32),
            jax.ShapeDtypeStruct((1, 6), F32),
            jax.ShapeDtypeStruct((3, 18), F32),
        ),
        in_specs=[vmem] * 3 + [pl.BlockSpec(memory_space=pl.ANY)],
        out_specs=(vmem,) * 8,
        scratch_shapes=[
            pltpu.VMEM((3,) + GRID + BLOCK, BF16),
            pltpu.VMEM((3,) + GRID[1:] + BLOCK, BF16),
            *lands,
            pltpu.VMEM((ROWS, D), BF16),
            pltpu.VMEM((5, VEC, 128), F32),
            pltpu.VMEM((4, 3, VEC, 128), F32),
            pltpu.VMEM((8, 2, 8, 384), F32),
            pltpu.VMEM((8, 2, 8, 384), F32),
            pltpu.VMEM((24, 384), F32),
            pltpu.VMEM((3,) + BLOCK, F32),
            pltpu.SemaphoreType.DMA,
            pltpu.SemaphoreType.DMA((64,)),
            pltpu.SemaphoreType.DMA((64,)),
        ],
        compiler_params=pltpu.CompilerParams(collective_id=1, has_side_effects=True, vmem_limit_bytes=LIMIT),
    )(partial, contrib, gvec, g)


def per_device(tokens, w_qkv, w_out, w_up, w_down, gain_attn, gain_ffn, conv_taps, cotangent):
    w, vec, prev = gather(
        tokens, w_qkv, w_out, w_up, w_down, gain_attn.reshape(1, 6), gain_ffn.reshape(1, 6), conv_taps
    )
    out, partial, contrib, g, gvec = layer(tokens, prev, cotangent, w, vec)
    gtok, gq, go, gu, gd, gga, ggf, gtap = reduce(partial, contrib, gvec, g)
    return out, gtok, gq, go, gu, gd, gga.reshape(6), ggf.reshape(6), gtap


def solution(mesh):
    both = ("grp", "seq")
    row, one, column = P(both, None), P(both), P(None, both)
    return jax.shard_map(
        per_device,
        mesh=mesh,
        in_specs=(row, row, row, row, row, one, one, column, row),
        out_specs=(row, row, row, row, row, row, one, one, column),
        check_vma=False,
    )
```

```python
import functools

import jax
import jax.numpy as jnp
from jax import lax
from jax.experimental import pallas as pl
from jax.experimental.pallas import tpu as pltpu
from jax.sharding import PartitionSpec as P

MESH = pl.DeviceIdType.MESH
F32 = jnp.float32
BF16 = jnp.bfloat16
EPS = 1e-05
D = 768
ROWS = 256
EXT = 512
PAIRS = 6
TILES = 18
BLOCK = (48, 384)
GRID = (2, 2, 2, 4, 2, 2)
VEC = 80
ORDERS = (("x", "y", "z"), ("y", "z", "x"), ("z", "x", "y"))
BACK = (("z", "y", "x"), ("x", "z", "y"), ("y", "x", "z"))
LIMIT = 60 * 2**20


class Place:
    def __init__(self, send_sem, recv_sem):
        grp, seq = lax.axis_index("grp"), lax.axis_index("seq")
        self.c = lax.rem(grp, 2)
        self.x = lax.rem(lax.div(grp, 2), 4)
        self.y = lax.rem(lax.div(grp, 8), 4)
        self.z = lax.div(grp, 32) * 2 + seq
        self.zl = seq
        self.index = grp * 2 + seq
        self.send_sem, self.recv_sem = send_sem, recv_sem
        self.used = 0
        self.sent = []

    def device(self, **new):
        at = {"x": self.x, "y": self.y, "z": self.z, "c": self.c}
        at.update(new)
        grp = ((lax.div(at["z"], 2) * 4 + at["y"]) * 4 + at["x"]) * 2 + at["c"]
        return (grp, lax.rem(at["z"], 2))

    def along(self, axis, delta):
        return lax.rem(getattr(self, axis) + delta, 4)

    def flip(self, value, bit):
        return value + bit * (1 - 2 * lax.rem(value, 2))

    def member(self, d):
        x, c, z = self.flip(self.x, d // 4), self.flip(self.c, (d // 2) % 2), self.flip(self.z, d % 2)
        number = lax.rem(x, 2) * 4 + c * 2 + lax.rem(z, 2)
        return self.device(x=x, c=c, z=z), number

    def greet(self):
        barrier = pltpu.get_barrier_semaphore()
        partners = [self.device(**{a: self.along(a, d)}) for a in "xyz" for d in (1, 2, 3)]
        partners += [self.member(d)[0] for d in (2, 3, 5, 7)]
        partners += [self.device(x=self.along("x", d), c=1 - self.c) for d in (1, 2, 3)]
        for partner in partners:
            pl.semaphore_signal(barrier, inc=1, device_id=partner, device_id_type=MESH)
        return lambda: pl.semaphore_wait(barrier, len(partners))

    def slot(self):
        self.used += 1
        return self.used - 1

    def copy(self, src, dst, device, slot):
        return pltpu.make_async_remote_copy(
            src_ref=src,
            dst_ref=dst,
            send_sem=self.send_sem.at[slot],
            recv_sem=self.recv_sem.at[slot],
            device_id=device,
            device_id_type=MESH,
        )

    def send(self, src, dst, device, slot):
        self.copy(src, dst, device, slot).start()
        self.sent.append((src, device, slot))

    def arrive(self, dst, slot):
        self.copy(dst, dst, self.device(), slot).wait_recv()

    def drain(self):
        for src, device, slot in self.sent:
            self.copy(src, src, device, slot).wait_send()
        self.sent = []


def spot(lead, c=None, tail=(), **at):
    index = list(lead) + [slice(None) if c is None else c]
    for axis in "zyx":
        value = at.get(axis)
        half = isinstance(value, tuple)
        if axis == "y":
            index.append(pl.ds(2 * value[1], 2) if half else slice(None) if value is None else value)
        elif half:
            index += [value[1], slice(None)]
        elif value is None:
            index += [slice(None), slice(None)]
        else:
            index += [lax.div(value, 2), lax.rem(value, 2)]
    return tuple(index) + tail


def strip(sub):
    return (pl.ds(16 * sub, 16), slice(None))


def spread(index, count, width):
    row = lax.broadcasted_iota(jnp.int32, (128, width), 0)
    column = lax.broadcasted_iota(jnp.int32, (128, width), 1)
    return jnp.where((column == count * index + row) & (row < count), 1.0, 0.0)


def gather_strip(place, w, part, sub):
    order, c, tail = ORDERS[sub], place.c, strip(sub)
    here = {"x": place.x, "y": place.y, "z": place.z}
    sibling = place.device(c=1 - c)
    passed = []

    def piece(core, **at):
        return w.at[spot((part,), core, tail, **at)]

    def pass_on(**at):
        slot = place.slot()
        place.send(piece(c, **at), piece(c, **at), sibling, slot)
        passed.append((at, slot))

    for stage in range(2):
        axis, done = order[stage], order[:stage]
        own = {a: here[a] for a in "xyz" if a not in done}
        waits = []
        for step in (1, 2, 3):
            slot = place.slot()
            place.send(piece(c, **own), piece(c, **own), place.device(**{axis: place.along(axis, step)}), slot)
            waits.append(({**own, axis: place.along(axis, 4 - step)}, slot))
        yield
        for at, slot in waits:
            place.arrive(piece(c, **at), slot)
    axis, whole = order[2], order[0]
    slots = [place.slot() for _ in range(4)]
    toward = [place.device(**{axis: place.along(axis, 1)}), place.device(**{axis: place.along(axis, 3)})]
    for side in range(2):
        own = piece(c, **{axis: here[axis]})
        place.send(own, own, toward[side], slots[side])
    pass_on(**{axis: here[axis]})
    yield
    for side in range(2):
        came = {axis: place.along(axis, 3 if side == 0 else 1)}
        place.arrive(piece(c, **came), slots[side])
        half = piece(c, **came, **{whole: ("half", side)})
        place.send(half, half, toward[side], slots[2 + side])
        pass_on(**came)
    yield
    for side in range(2):
        came = {axis: place.along(axis, 2), whole: ("half", side)}
        place.arrive(piece(c, **came), slots[2 + side])
        pass_on(**came)
    yield
    for at, slot in passed:
        place.arrive(piece(1 - c, **at), slot)


HALF = {"z": "y", "x": "z", "y": "x"}
HALVES = {"z": (2, 2, 2), "x": (2, 4), "y": (2, 2, 2)}


def half_of(axis, h):
    return {"z": (pl.ds(2 * h, 2),), "x": (h,), "y": (slice(None), slice(None), h)}[axis]


def scatter_strip(place, w, part, sub, from_core, lands, sums):
    order, c, tail = BACK[sub], place.c, strip(sub)
    here = {"x": place.x, "y": place.y, "z": place.z}
    relay, low, high, second, third = lands

    def at(**where):
        return spot((part,), c, tail, **where)

    slot = place.slot()
    landed = (part,) + (slice(None),) * 5 + tail
    place.send(w.at[spot((part,), 1 - c, tail)], from_core.at[landed], place.device(c=1 - c), slot)
    yield
    place.arrive(from_core.at[landed], slot)
    w[at()] = w[at()] + from_core[landed]
    axis = order[0]
    up, down, across = place.along(axis, 1), place.along(axis, 3), place.along(axis, 2)
    whole = HALF[axis]
    above, below = place.device(**{axis: up}), place.device(**{axis: down})
    slots = [place.slot() for _ in range(6)]
    place.send(w.at[at(**{axis: across, whole: ("half", 0)})], relay.at[0], above, slots[0])
    place.send(w.at[at(**{axis: across, whole: ("half", 1)})], relay.at[1], below, slots[1])
    place.send(w.at[at(**{axis: up, whole: ("half", 1)})], low.at[half_of(axis, 1)], above, slots[2])
    place.send(w.at[at(**{axis: down, whole: ("half", 0)})], high.at[half_of(axis, 0)], below, slots[3])
    yield
    for side, (coordinate, device, land) in enumerate(((up, above, low), (down, below, high))):
        place.arrive(relay.at[side], slots[side])
        index = at(**{axis: coordinate, whole: ("half", side)})
        w[index] = w[index] + relay[side]
        place.send(w.at[index], land.at[half_of(axis, side)], device, slots[4 + side])
    yield
    place.arrive(low.at[half_of(axis, 1)], slots[2])
    place.arrive(high.at[half_of(axis, 0)], slots[3])
    place.arrive(low.at[half_of(axis, 0)], slots[4])
    place.arrive(high.at[half_of(axis, 1)], slots[5])
    index = at(**{axis: here[axis]})
    w[index] = (w[index].astype(F32) + low[...].astype(F32) + high[...].astype(F32)).astype(BF16)
    for stage, land in ((1, second), (2, third)):
        axis, done = order[stage], order[:stage]
        own = {a: here[a] for a in done}
        slots = [place.slot() for _ in range(3)]
        for step in (1, 2, 3):
            there = place.along(axis, step)
            place.send(w.at[at(**own, **{axis: there})], land.at[step - 1], place.device(**{axis: there}), slots[step - 1])
        yield
        for step in range(3):
            place.arrive(land.at[step], slots[step])
        index = at(**own, **{axis: here[axis]})
        total = w[index].astype(F32)
        for step in range(3):
            total = total + land[step].astype(F32)
        if stage == 1:
            w[index] = total.astype(BF16)
        else:
            sums[part, 16 * sub:16 * sub + 16, :] = total


def advance(steps):
    for step in steps:
        next(step, None)


def remainder(value, count):
    value = value.astype(F32)
    whole = jnp.floor((value + 0.5) * (1.0 / count))
    return value - whole * count, whole


def gather_vectors(place, few, tiles, landed, vec):
    slots = [place.slot() for _ in range(7)]
    sublane = lax.broadcasted_iota(jnp.int32, (8, 128), 0)
    mine = place.c * 4 + place.x
    own = jnp.where(sublane == mine, few[...], 0.0)
    here = tiles.at[place.z, place.y]
    landed[7] = own
    yield
    for k in range(7):
        core, step = (k + 1) // 4, (k + 1) % 4
        target = place.device(x=place.along("x", step), c=place.c + core * (1 - 2 * place.c))
        place.send(landed.at[7], landed.at[k], target, slots[k])
    yield
    total = own
    for k in range(7):
        place.arrive(landed.at[k], slots[k])
        total = total + landed[k]
    tiles[place.z, place.y] = total
    slots = [place.slot() for _ in range(6)]
    for step in (1, 2, 3):
        place.send(here, here, place.device(y=place.along("y", step)), slots[step - 1])
    yield
    for step in (1, 2, 3):
        place.arrive(tiles.at[place.z, place.along("y", 4 - step)], slots[step - 1])
    for step in (1, 2, 3):
        place.send(tiles.at[place.z], tiles.at[place.z], place.device(z=place.along("z", step)), slots[2 + step])
    yield
    for step in (1, 2, 3):
        place.arrive(tiles.at[place.along("z", 4 - step)], slots[2 + step])
    table = tiles[...].reshape(128, 128).astype(BF16)
    row = lax.broadcasted_iota(jnp.int32, (128, 1), 0)
    z, y, core, x = row // 32, (row // 8) % 4, (row // 4) % 2, row % 4
    device = ((z // 2) * 64 + y * 16 + x * 4 + core * 2 + z % 2).astype(F32)
    for count, width, firsts in ((6, D, (0, 6)), (18, 3 * D, (12, 30, 48))):
        part, owner = remainder(lax.broadcasted_iota(jnp.int32, (1, width), 1), count)
        lane = lax.broadcasted_iota(jnp.int32, (128, 1), 0).astype(F32)
        for first in firsts:
            choose = jnp.where(lane - first == part, 1.0, 0.0).astype(BF16)
            spread_out = nn(table, choose)
            vector = jnp.sum(jnp.where(device == owner, spread_out, 0.0), axis=0, keepdims=True)
            base = first if count == 6 else first
            for k in range(width // 128):
                vec[base + k:base + k + 1, :] = vector[:, 128 * k:128 * (k + 1)]


def sum_vectors(place, vec, incoming):
    for stage, axis in enumerate("cxyz"):
        steps = (1,) if axis == "c" else (1, 2, 3)
        slots = [place.slot() for _ in steps]
        for k, step in enumerate(steps):
            device = place.device(c=1 - place.c) if axis == "c" else place.device(**{axis: place.along(axis, step)})
            place.send(vec.at[stage], incoming.at[stage, k], device, slots[k])
        yield
        total = vec[stage]
        for k, step in enumerate(steps):
            place.arrive(incoming.at[stage, k], slots[k])
            total = total + incoming[stage, k]
        vec[stage + 1] = total


def nt(left, right):
    return lax.dot_general(left, right, (((1,), (1,)), ((), ())), preferred_element_type=F32)


def tn(left, right):
    return lax.dot_general(left, right, (((0,), (0,)), ((), ())), preferred_element_type=F32)


def nn(left, right):
    return jnp.dot(left, right, preferred_element_type=F32)


def columns(ref, part, jp):
    halves = [ref[part, lax.rem(jp, 2), :, zl, :, :, lax.div(jp, 2)].reshape(D, 384) for zl in range(2)]
    return jnp.concatenate(halves, axis=1)


def put_columns(ref, part, jp, value):
    for zl in range(2):
        ref[part, lax.rem(jp, 2), :, zl, :, :, lax.div(jp, 2)] = (
            value[:, zl * 384:(zl + 1) * 384].astype(BF16).reshape(2, 4, 2, 48, 384)
        )


def row_pieces():
    return [(y, xh, xl, c) for y in range(2) for xh in range(2) for xl in range(2) for c in range(2)]


def rows(ref, jp):
    zh, y0 = lax.div(jp, 2), lax.rem(jp, 2) * 2
    halves = [
        jnp.concatenate([ref[2, c, zh, zl, y0 + y, xh, xl] for y, xh, xl, c in row_pieces()], axis=0) for zl in range(2)
    ]
    return jnp.concatenate(halves, axis=1)


def put_rows(ref, jp, value):
    zh, y0 = lax.div(jp, 2), lax.rem(jp, 2) * 2
    low = value.astype(BF16)
    for zl in range(2):
        for k, (y, xh, xl, c) in enumerate(row_pieces()):
            ref[2, c, zh, zl, y0 + y, xh, xl] = low[48 * k:48 * k + 48, zl * 384:(zl + 1) * 384]


def normalize(values):
    mean = jnp.mean(values, axis=-1, keepdims=True)
    centred = values - mean
    inverse = lax.rsqrt(jnp.mean(centred * centred, axis=-1, keepdims=True) + EPS)
    return centred * inverse, inverse


def norm_back(grad, normed, inverse):
    first = jnp.mean(grad, axis=-1, keepdims=True)
    second = jnp.mean(grad * normed, axis=-1, keepdims=True)
    return inverse * (grad - first - normed * second)


def shifted(values, steps):
    count = values.shape[0]
    row = lax.broadcasted_iota(jnp.int32, values.shape, 0)
    rolled = pltpu.roll(values, steps % count, 0)
    return jnp.where(row >= steps if steps > 0 else row < count + steps, rolled, 0.0)


def layer_kernel(tok, cot, wq, wo, wu, wd, ga, gf, taps, out, gtok, gq, go, gu, gd, gga, ggf, gtap, *scratch):
    (w, from_core, to_peer, from_peer, pile, down_s, down, few, tiles, few_landed, vec, prev, h1, n1, inv1, raw, mixed, bias,
     probs, att, h2, gh2, gatt, gqkv, gh1, acc, contrib, got, gvec, incoming, sums) = scratch[:31]
    lands, (send_sem, recv_sem) = scratch[31:-2], scratch[-2:]
    place = Place(send_sem, recv_sem)
    c, zl, rank = place.c, place.zl, place.zl
    ready = place.greet()
    for number in range(8):
        source = wq[:, number * 384:(number + 1) * 384] if number < 6 else wo[:, (number - 6) * 384:(number - 5) * 384]
        to_peer[number, 0, 0:6, :] = source.astype(F32)
        to_peer[number, 1, 0:6, :] = wu[:, number * 384:(number + 1) * 384].astype(F32)
    left, right = wd[:, 0:384].astype(F32), wd[:, 384:768].astype(F32)
    down_s[...] = jnp.where(zl == 0, right, left)
    down[pl.ds(pl.multiple_of(zl * 24, 8), 24), :] = jnp.where(zl == 0, left, right)
    few[...] = jnp.zeros_like(few)
    few[0:1, 0:6] = ga[...].astype(F32)
    few[0:1, 6:12] = gf[...].astype(F32)
    for j in range(3):
        few[0:1, 12 + 18 * j:30 + 18 * j] = taps[j:j + 1, :].astype(F32)
    few[...] = jnp.broadcast_to(few[0:1, :], (8, 128))
    vectors = gather_vectors(place, few, tiles, few_landed, vec)
    next(vectors)
    ready()

    other = place.device(z=place.flip(place.z, 1))
    trade = [place.slot() for _ in range(8)]
    _, mine = place.member(0)
    for d in range(1, 8):
        device, number = place.member(d)
        place.send(to_peer.at[number], from_peer.at[mine], device, trade[d])
    place.send(down_s, down.at[pl.ds(pl.multiple_of(zl * 24, 8), 24)], other, trade[0])
    next(vectors)
    from_peer[mine] = to_peer[mine]

    def normalize_half(half):
        normed, inverse = normalize((prev if half == 0 else tok)[...].astype(F32))
        here = pl.ds(half * ROWS, ROWS)
        n1[here, :] = normed
        inv1[here, :] = inverse

    for d in range(1, 8):
        _, number = place.member(d)
        place.arrive(from_peer.at[number], trade[d])
    place.arrive(down.at[pl.ds(pl.multiple_of((1 - zl) * 24, 8), 24)], trade[0])
    at = (c, lax.div(place.z, 2), zl, place.y, lax.div(place.x, 2), lax.rem(place.x, 2))
    for k in range(2):
        for number in range(8):
            pile[k, 6 * number:6 * number + 8, :] = from_peer[number, k]
        w[(k,) + at] = pile[k, 0:48, :].astype(BF16)
    w[(2,) + at] = down[...].astype(BF16)
    phase = [[gather_strip(place, w, part, sub) for sub in range(3)] for part in range(3)]
    advance(phase[0])
    next(vectors)
    token_slot, back_slot = place.slot(), place.slot()
    advance(phase[0])

    @pl.when(zl == 0)
    def _():
        place.copy(tok, prev, other, token_slot).start()

    next(vectors)
    advance(phase[1])
    normalize_half(1)
    advance(phase[0])
    next(vectors, None)
    advance(phase[1])
    advance(phase[2])
    advance(phase[0])
    advance(phase[1])
    advance(phase[2])

    @pl.when(zl == 1)
    def _():
        place.arrive(prev, token_slot)

    @pl.when(zl == 0)
    def _():
        prev[...] = jnp.zeros_like(prev)

    normalize_half(0)
    gain_one = jnp.concatenate([vec[r:r + 1, :] for r in range(6)], axis=1)
    gain_two = jnp.concatenate([vec[r:r + 1, :] for r in range(6, 12)], axis=1)
    h1[...] = (n1[...] * gain_one).astype(BF16)
    row = lax.broadcasted_iota(jnp.int32, (ROWS, EXT), 0)
    column = lax.broadcasted_iota(jnp.int32, (ROWS, EXT), 1)
    behind = jnp.where(column < ROWS, (1 - rank) * EXT, column - ROWS)
    bias[...] = jnp.where(behind <= row, 0.0, -1e30)
    first = lax.broadcasted_iota(jnp.int32, (ROWS, 128), 1) < 64
    gvec[0] = jnp.zeros((VEC, 128), F32)
    advance(phase[0])
    advance(phase[0])

    def tap(j, t):
        return vec[pl.ds(12 + TILES * j + t, 1), :]

    @pl.loop(0, 3)
    def _(jp):
        block = nn(h1[...], columns(w, 0, jp)).astype(BF16)
        for k in range(6):
            t = 6 * jp + k
            tile = block[:, 128 * k:128 * (k + 1)]
            raw[t] = tile
            value = tile.astype(F32)
            conv = tap(0, t) * value + tap(1, t) * shifted(value, 1) + tap(2, t) * shifted(value, 2)
            mixed[t] = conv.astype(BF16)

    def both(value):
        zero = jnp.zeros_like(value)
        return jnp.concatenate([jnp.where(first, value, zero), jnp.where(first, zero, value)], axis=0)

    def pick(value):
        return jnp.where(first, value[:ROWS], value[ROWS:])

    def attend(p):
        query = both(mixed[p, ROWS:, :])
        key, value = mixed[PAIRS + p], mixed[2 * PAIRS + p]
        scores = nt(query, key) * 0.125 + jnp.concatenate([bias[...], bias[...]], axis=0)
        weights = jnp.exp(scores - jnp.max(scores, axis=-1, keepdims=True))
        exact = weights * (1.0 / jnp.sum(weights, axis=-1, keepdims=True))
        probs[p] = exact
        att[p] = pick(nn(exact.astype(BF16), value)).astype(BF16)

    advance(phase[1])
    advance(phase[2])
    for p in range(PAIRS):
        attend(p)
        if p in (1, 3):
            advance(phase[1])
        if p in (2, 4):
            advance(phase[2])

    attended = jnp.concatenate([att[p] for p in range(PAIRS)], axis=1)
    resid = tok[...].astype(F32) + nn(attended, columns(w, 0, 3))
    normed_two, inverse_two = normalize(resid)
    h2[...] = (normed_two * gain_two).astype(BF16)
    acc[...] = resid
    gh2[...] = jnp.zeros_like(gh2)
    for _ in range(6):
        advance(phase[1])
        advance(phase[2])
    place.drain()

    @pl.when(zl == 0)
    def _():
        place.copy(tok, tok, other, token_slot).wait_send()

    @pl.loop(0, 4)
    def _(jp):
        up = columns(w, 1, jp)
        low = rows(w, jp)
        rect = jnp.maximum(nn(h2[...], up), 0.0)
        act = (rect * rect).astype(BF16)
        acc[...] += nn(act, low)
        gact = nt(cot[...], low)
        gup = (gact * 2.0 * rect).astype(BF16)
        gh2[...] += nt(gup, up)
        put_rows(w, jp, tn(act, cot[...]))
        put_columns(w, 1, jp, tn(h2[...], gup))

    sent = {part: [scatter_strip(place, w, part, sub, from_core, lands[15 * part + 5 * sub:15 * part + 5 * sub + 5], sums) for sub in range(3)] for part in range(3)}
    advance(sent[2])
    advance(sent[1])
    out[...] = acc[...].astype(BF16)
    grad_two = gh2[...]
    summed = jnp.sum(grad_two * normed_two, axis=0, keepdims=True)
    for r in range(6):
        gvec[0, 6 + r:7 + r, :] = summed[:, 128 * r:128 * (r + 1)]
    grad_resid = cot[...].astype(F32) + norm_back(grad_two * gain_two, normed_two, inverse_two)
    acc[...] = grad_resid
    gproj = grad_resid.astype(BF16)
    gback = nt(gproj, columns(w, 0, 3)).astype(BF16)
    for p in range(PAIRS):
        gatt[p] = gback[:, 128 * p:128 * (p + 1)]
    advance(sent[2])
    put_columns(w, 0, 3, tn(attended, gproj))

    def attend_back(p):
        query = both(mixed[p, ROWS:, :])
        key, value = mixed[PAIRS + p], mixed[2 * PAIRS + p]
        grad = both(gatt[p])
        exact = probs[p]
        gvalue = tn(exact.astype(BF16), grad)
        gprobs = nt(grad, value)
        centred = gprobs - jnp.sum(gprobs * exact, axis=-1, keepdims=True)
        gscores = (exact * centred).astype(BF16)
        gquery = pick(nn(gscores, key)) * 0.125
        gkey = tn(gscores, query) * 0.125
        for k, tile in enumerate((jnp.concatenate([jnp.zeros_like(gquery), gquery], axis=0), gkey, gvalue)):
            t = PAIRS * k + p
            back = tap(0, t) * tile + tap(1, t) * shifted(tile, -1) + tap(2, t) * shifted(tile, -2)
            gqkv[t] = back.astype(BF16)
            value_in = raw[t].astype(F32)
            for j in range(3):
                delayed = value_in if j == 0 else shifted(value_in, j)
                gvec[0, pl.ds(12 + TILES * j + t, 1), :] = jnp.sum(tile * delayed, axis=0, keepdims=True)

    for p in range(PAIRS):
        attend_back(p)
        advance(sent[1] if p % 2 == 0 else sent[2])

    gh1[...] = jnp.zeros_like(gh1)

    @pl.loop(0, 3)
    def _(jp):
        grad = jnp.concatenate([gqkv[6 * jp + k] for k in range(6)], axis=1)
        gh1[...] += nt(grad, columns(w, 0, jp))
        put_columns(w, 0, jp, tn(h1[...], grad))

    advance(sent[0])
    total = jnp.zeros((1, D), F32)
    for half in range(2):
        here = pl.ds(half * ROWS, ROWS)
        grad_one = gh1[here, :]
        total = total + jnp.sum(grad_one * n1[here, :], axis=0, keepdims=True)
        back = norm_back(grad_one * gain_one, n1[here, :], inv1[here, :])
        if half == 0:
            contrib[...] = back.astype(BF16)

            @pl.when(zl == 1)
            def _():
                place.copy(contrib, got, other, back_slot).start()
        else:
            acc[...] += back
    for r in range(6):
        gvec[0, r:r + 1, :] = total[:, 128 * r:128 * (r + 1)]
    advance(sent[0])
    for _ in range(6):
        advance(sent[1])
        advance(sent[2])
    small = sum_vectors(place, gvec, incoming)
    for _ in range(5):
        next(small, None)
        advance(sent[0])

    for number in range(8):
        for k in range(2):
            to_peer[number, k, 0:6, :] = sums[k, 6 * number:6 * number + 6, :]
    trade = [place.slot() for _ in range(8)]
    back_from = pile.at[0, pl.ds(0, 24)]
    arrived = from_core_free = from_peer
    for d in range(1, 8):
        device, number = place.member(d)
        place.send(to_peer.at[number], arrived.at[mine], device, trade[d])
    place.send(sums.at[2, pl.ds(pl.multiple_of((1 - zl) * 24, 8), 24)], back_from, other, trade[0])
    arrived[mine] = to_peer[mine]
    summed = gvec[4]
    gains = [jnp.concatenate([summed[r:r + 1] for r in range(6 * k, 6 * k + 6)], axis=1) for k in range(2)]
    tapped = [jnp.concatenate([summed[r:r + 1] for r in range(12 + TILES * j, 12 + TILES * j + TILES)], axis=1) for j in range(3)]
    gain_rows = jnp.concatenate(gains + [jnp.zeros((6, D), F32)], axis=0)
    tap_rows = jnp.concatenate(tapped + [jnp.zeros((5, 3 * D), F32)], axis=0)
    exactly = functools.partial(
        lax.dot_general,
        dimension_numbers=(((1,), (1,)), ((), ())),
        preferred_element_type=F32,
        precision=lax.Precision.HIGHEST,
    )
    gain_own = exactly(gain_rows, spread(place.index, 6, D))
    gga[...] = gain_own[0:1, 0:6]
    ggf[...] = gain_own[1:2, 0:6]
    gtap[...] = exactly(tap_rows, spread(place.index, 18, 3 * D))[0:3, 0:18]

    @pl.when(zl == 0)
    def _():
        place.arrive(got, back_slot)

    @pl.when(zl == 1)
    def _():
        got[...] = jnp.zeros_like(got)

    gtok[...] = (acc[...] + got[...].astype(F32)).astype(BF16)
    for d in range(1, 8):
        _, number = place.member(d)
        place.arrive(arrived.at[number], trade[d])
    place.arrive(back_from, trade[0])
    for number in range(8):
        if number < 6:
            gq[:, 384 * number:384 * (number + 1)] = arrived[number, 0, 0:6, :]
        else:
            go[:, 384 * (number - 6):384 * (number - 5)] = arrived[number, 0, 0:6, :]
        gu[:, 384 * number:384 * (number + 1)] = arrived[number, 1, 0:6, :]
    own = sums[2, pl.ds(pl.multiple_of(zl * 24, 8), 24), :]
    theirs = pile[0, 0:24, :]
    gd[:, 0:384] = jnp.where(zl == 0, own, theirs)
    gd[:, 384:768] = jnp.where(zl == 0, theirs, own)
    place.drain()

    @pl.when(zl == 1)
    def _():
        place.copy(contrib, contrib, other, back_slot).wait_send()


def kept(axes):
    grid = []
    for axis in "zyx":
        if axis not in axes:
            grid += {"z": [2, 2], "y": [4], "x": [2, 2]}[axis]
    return tuple(grid)


RESULTS = (
    ((ROWS, D), BF16),
    ((ROWS, D), BF16),
    ((6, 2304), F32),
    ((6, 768), F32),
    ((6, 3072), F32),
    ((24, 768), F32),
    ((1, 6), F32),
    ((1, 6), F32),
    ((3, 18), F32),
)


def layer(*args):
    vmem = pl.BlockSpec(memory_space=pltpu.VMEM)
    lands = []
    for _ in range(3):
        for sub in range(3):
            order = BACK[sub]
            grids = [(2,) + HALVES[order[0]], kept(order[:1]), kept(order[:1]), (3,) + kept(order[:2]), (3,)]
            lands += [pltpu.VMEM(grid + (16, 384), BF16) for grid in grids]
    return pl.pallas_call(
        layer_kernel,
        out_shape=tuple(jax.ShapeDtypeStruct(*result) for result in RESULTS),
        in_specs=[vmem] * 9,
        out_specs=(vmem,) * 9,
        scratch_shapes=[
            pltpu.VMEM((3,) + GRID + BLOCK, BF16),
            pltpu.VMEM((3,) + GRID[1:] + BLOCK, BF16),
            pltpu.VMEM((8, 2, 8, 384), F32),
            pltpu.VMEM((8, 2, 8, 384), F32),
            pltpu.VMEM((2, 56, 384), F32),
            pltpu.VMEM((24, 384), F32),
            pltpu.VMEM((48, 384), F32),
            pltpu.VMEM((8, 128), F32),
            pltpu.VMEM((4, 4, 8, 128), F32),
            pltpu.VMEM((8, 8, 128), F32),
            pltpu.VMEM((VEC, 128), F32),
            pltpu.VMEM((ROWS, D), BF16),
            pltpu.VMEM((EXT, D), BF16),
            pltpu.VMEM((EXT, D), F32),
            pltpu.VMEM((EXT, 1), F32),
            pltpu.VMEM((TILES, EXT, 128), BF16),
            pltpu.VMEM((TILES, EXT, 128), BF16),
            pltpu.VMEM((ROWS, EXT), F32),
            pltpu.VMEM((PAIRS, EXT, EXT), F32),
            pltpu.VMEM((PAIRS, ROWS, 128), BF16),
            pltpu.VMEM((ROWS, D), BF16),
            pltpu.VMEM((ROWS, D), F32),
            pltpu.VMEM((PAIRS, ROWS, 128), BF16),
            pltpu.VMEM((TILES, EXT, 128), BF16),
            pltpu.VMEM((EXT, D), F32),
            pltpu.VMEM((ROWS, D), F32),
            pltpu.VMEM((ROWS, D), BF16),
            pltpu.VMEM((ROWS, D), BF16),
            pltpu.VMEM((5, VEC, 128), F32),
            pltpu.VMEM((4, 3, VEC, 128), F32),
            pltpu.VMEM((3,) + BLOCK, F32),
            *lands,
            pltpu.SemaphoreType.DMA((340,)),
            pltpu.SemaphoreType.DMA((340,)),
        ],
        compiler_params=pltpu.CompilerParams(collective_id=0, has_side_effects=True, vmem_limit_bytes=LIMIT),
    )(*args)


def copy_kernel(*refs):
    count = len(RESULTS)
    copies = [pltpu.make_async_copy(refs[k], refs[count + k], refs[-1].at[k]) for k in range(count)]
    for copy in copies:
        copy.start()
    for copy in copies:
        copy.wait()


def copied(*args):
    anywhere = pl.BlockSpec(memory_space=pl.ANY)
    return pl.pallas_call(
        copy_kernel,
        out_shape=tuple(jax.ShapeDtypeStruct(*result) for result in RESULTS),
        in_specs=[anywhere] * len(RESULTS),
        out_specs=(anywhere,) * len(RESULTS),
        scratch_shapes=[pltpu.SemaphoreType.DMA((len(RESULTS),))],
    )(*args)


def per_device(tokens, w_qkv, w_out, w_up, w_down, gain_attn, gain_ffn, conv_taps, cotangent):
    results = copied(*layer(
        tokens, cotangent, w_qkv, w_out, w_up, w_down, gain_attn.reshape(1, 6), gain_ffn.reshape(1, 6), conv_taps
    ))
    return results[:6] + (results[6].reshape(6), results[7].reshape(6), results[8])


def solution(mesh):
    both = ("grp", "seq")
    row, one, column = P(both, None), P(both), P(None, both)
    return jax.shard_map(
        per_device,
        mesh=mesh,
        in_specs=(row, row, row, row, row, one, one, column, row),
        out_specs=(row, row, row, row, row, row, one, one, column),
        check_vma=False,
    )
```

```python
import functools

import jax
import jax.numpy as jnp
from jax import lax
from jax.experimental import pallas as pl
from jax.experimental.pallas import tpu as pltpu
from jax.sharding import PartitionSpec as P

MESH = pl.DeviceIdType.MESH
F32 = jnp.float32
BF16 = jnp.bfloat16
EPS = 1e-05
D = 768
ROWS = 256
EXT = 512
PAIRS = 6
TILES = 18
BLOCK = (48, 384)
GRID = (2, 2, 2, 4, 2, 2)
VEC = 80
ORDERS = (("x", "y", "z"), ("y", "z", "x"), ("z", "x", "y"))
BACK = (("z", "y", "x"), ("x", "z", "y"), ("y", "x", "z"))
LIMIT = 60 * 2**20
READY = tuple(range(18, 24)) + tuple(t for p in range(6) for t in (p, 6 + p, 12 + p))
CHUNKS = ((0, 256), (256, 128))

LEAN_IN = (False, True, True)
LEAN_OUT = (True, True, True)


class Place:
    def __init__(self, send_sem, recv_sem):
        grp, seq = lax.axis_index("grp"), lax.axis_index("seq")
        self.c = lax.rem(grp, 2)
        self.x = lax.rem(lax.div(grp, 2), 4)
        self.y = lax.rem(lax.div(grp, 8), 4)
        self.z = lax.div(grp, 32) * 2 + seq
        self.zl = seq
        self.index = grp * 2 + seq
        self.send_sem, self.recv_sem = send_sem, recv_sem
        self.sends = self.receives = 0
        self.owed = []

    def device(self, **new):
        at = {"x": self.x, "y": self.y, "z": self.z, "c": self.c}
        at.update(new)
        grp = ((lax.div(at["z"], 2) * 4 + at["y"]) * 4 + at["x"]) * 2 + at["c"]
        return (grp, lax.rem(at["z"], 2))

    def along(self, axis, delta):
        return lax.rem(getattr(self, axis) + delta, 4)

    def flip(self, value, bit):
        return value + bit * (1 - 2 * lax.rem(value, 2))

    def member(self, d):
        x, c, z = self.flip(self.x, d // 4), self.flip(self.c, (d // 2) % 2), self.flip(self.z, d % 2)
        number = lax.rem(x, 2) * 4 + c * 2 + lax.rem(z, 2)
        return self.device(x=x, c=c, z=z), number

    def greet(self):
        barrier = pltpu.get_barrier_semaphore()
        partners = [self.device(**{a: self.along(a, d)}) for a in "xyz" for d in (1, 2, 3)]
        partners += [self.member(d)[0] for d in (2, 3, 5, 6, 7)]
        for partner in partners:
            pl.semaphore_signal(barrier, inc=1, device_id=partner, device_id_type=MESH)
        return lambda: pl.semaphore_wait(barrier, len(partners))

    def slot(self, count=1):
        self.receives += count
        return self.receives - count

    def outbox(self, *wholes):
        self.sends += 1
        self.owed.append((self.sends - 1, wholes))
        return self.sends - 1

    def copy(self, src, dst, device, out, slot):
        return pltpu.make_async_remote_copy(
            src_ref=src,
            dst_ref=dst,
            send_sem=self.send_sem.at[out],
            recv_sem=self.recv_sem.at[slot],
            device_id=device,
            device_id_type=MESH,
        )

    def send(self, src, dst, device, out, slot):
        self.copy(src, dst, device, out, slot).start()

    def arrive(self, whole, slot):
        self.copy(whole, whole, self.device(), 0, slot).wait_recv()

    def drain(self):
        for out, wholes in self.owed:
            for whole in wholes:
                self.copy(whole, whole, self.device(), out, 0).wait_send()
        self.owed = []


def spot(lead, c=None, tail=(), **at):
    index = list(lead) + [slice(None) if c is None else c]
    for axis in "zyx":
        value = at.get(axis)
        half = isinstance(value, tuple)
        if axis == "y":
            index.append(pl.ds(2 * value[1], 2) if half else slice(None) if value is None else value)
        elif half:
            index += [value[1], slice(None)]
        elif value is None:
            index += [slice(None), slice(None)]
        else:
            index += [lax.div(value, 2), lax.rem(value, 2)]
    return tuple(index) + tail


def strip(sub):
    return (pl.ds(16 * sub, 16), slice(None))


def spread(index, count, width):
    row = lax.broadcasted_iota(jnp.int32, (128, width), 0)
    column = lax.broadcasted_iota(jnp.int32, (128, width), 1)
    return jnp.where((column == count * index + row) & (row < count), 1.0, 0.0)


def gather_phase(place, w, part, lean):
    c = place.c
    here = {"x": place.x, "y": place.y, "z": place.z}
    sibling = place.device(c=1 - c)
    blocks = {3: w.at[part, 0, 0, 0, 0:3, 0, 0], 12: w.at[part, 0, 0, 0, 0:3], 16: w.at[part, 0, 0, 0], 48: w.at[part, 0, :, :, 0:3], 64: w.at[part, 0]}
    passing, passed = place.outbox(blocks[64]), place.slot()

    def piece(sub, **at):
        return w.at[spot((part,), c, strip(sub), **at)]

    def pass_on(sub, **at):
        place.send(piece(sub, **at), piece(sub, **at), sibling, passing, passed)

    for stage, count in ((0, 3), (1, 12)):
        out, slot = place.outbox(blocks[count]), place.slot()
        for sub in range(3):
            axis, done = ORDERS[sub][stage], ORDERS[sub][:stage]
            own = piece(sub, **{a: here[a] for a in "xyz" if a not in done})
            for step in (1, 2, 3):
                place.send(own, own, place.device(**{axis: place.along(axis, step)}), out, slot)
        yield
        place.arrive(blocks[count], slot)
    out, sides, last = place.outbox(blocks[48]), place.slot(6), place.slot()

    def toward(axis, side):
        return place.device(**{axis: place.along(axis, 3 if side else 1)})

    for sub in range(3):
        axis = ORDERS[sub][2]
        own = piece(sub, **{axis: here[axis]})
        for side in range(2):
            place.send(own, own, toward(axis, side), out, sides + 2 * sub + side)
    for sub in range(3):
        axis = ORDERS[sub][2]
        pass_on(sub, **{axis: here[axis]})
    yield
    for side in range(2):
        for sub in range(3):
            axis, whole = ORDERS[sub][2], ORDERS[sub][0]
            came = {axis: place.along(axis, 1 if side else 3)}
            place.arrive(piece(sub, **came), sides + 2 * sub + side)
            down_only = lean and axis == "z"
            if not down_only or side == 1:
                half = piece(sub, **came) if down_only else piece(sub, **came, **{whole: ("half", side)})
                place.send(half, half, toward(axis, side), out, last)
            pass_on(sub, **came)
    yield
    place.arrive(blocks[16], last)
    for sub in range(3):
        axis = ORDERS[sub][2]
        pass_on(sub, **{axis: place.along(axis, 2)})
    yield
    place.arrive(blocks[64], passed)


HALF = {"z": "y", "x": "z", "y": "x"}
HALVES = {"z": (2, 2, 2), "x": (2, 4), "y": (2, 2, 2)}


def half_of(axis, h):
    return {"z": (pl.ds(2 * h, 2),), "x": (h,), "y": (slice(None), slice(None), h)}[axis]


def scatter_phase(place, g, lead, tails, arrivals, landed, lands, finish, relayed, lean):
    c = place.c
    here = {"x": place.x, "y": place.y, "z": place.z}
    tail = (slice(None), tails[0][1])
    corner = lead + (0, 0, 0)
    blocks = {
        3: g.at[corner + (pl.ds(0, 3), 0, 0) + tail],
        12: g.at[corner + (pl.ds(0, 3), slice(None), slice(None)) + tail],
        48: g.at[lead + (0, slice(None), slice(None), pl.ds(0, 3), slice(None), slice(None)) + tail],
    }

    def at(sub, **where):
        return spot(lead, c, tails[sub], **where)

    for index, slot in arrivals:
        place.arrive(landed.at[index], slot)
        g[lead + (c,) + index] = g[lead + (c,) + index] + landed[index]
    out = place.outbox(blocks[48])

    def ways(sub):
        axis = BACK[sub][0]
        way = [(t, place.device(**{axis: t})) for t in (place.along(axis, 1), place.along(axis, 3))]
        return axis, HALF[axis], way, (0, 0) if lean and axis == "z" else (0, 1)

    if relayed:
        relays, sides = place.slot(6), place.slot(3)
        for sub in range(3):
            axis, whole, way, course = ways(sub)
            across = place.along(axis, 2)
            for k in range(2):
                src = g.at[at(sub, **{axis: across, whole: ("half", k)})]
                place.send(src, lands[sub][0].at[k], way[course[k]][1], out, relays + 2 * sub + k)
        for sub in range(3):
            axis, whole, way, course = ways(sub)
            for k in range(2):
                toward = 1 - course[k]
                coordinate, device = way[toward]
                src = g.at[at(sub, **{axis: coordinate, whole: ("half", k)})]
                place.send(src, lands[sub][1].at[(toward,) + half_of(axis, k)], device, out, sides + sub)
        yield
        for sub in range(3):
            axis, whole, way, course = ways(sub)
            relay, side = lands[sub][:2]
            for k in range(2):
                coordinate, device = way[course[k]]
                place.arrive(relay.at[k], relays + 2 * sub + k)
                index = at(sub, **{axis: coordinate, whole: ("half", k)})
                g[index] = g[index] + relay[k]
                place.send(g.at[index], side.at[(course[k],) + half_of(axis, k)], device, out, sides + sub)
        yield
    else:
        sides = place.slot(3)
        for step in (2, 1, 3):
            for sub in range(3):
                axis = BACK[sub][0]
                there = place.along(axis, step)
                src = g.at[at(sub, **{axis: there})]
                place.send(src, lands[sub][1].at[step - 1], place.device(**{axis: there}), out, sides + sub)
        yield
    out, slot = place.outbox(blocks[12]), place.slot()
    for sub in range(3):
        axis, second = BACK[sub][0], BACK[sub][1]
        side = lands[sub][1]
        place.arrive(side, sides + sub)
        index = at(sub, **{axis: here[axis]})
        total = g[index].astype(F32)
        for k in range(side.shape[0]):
            total = total + side[k].astype(F32)
        g[index] = total.astype(BF16)
        for step in (1, 2, 3):
            there = place.along(second, step)
            src = g.at[at(sub, **{axis: here[axis], second: there})]
            place.send(src, lands[sub][2].at[step - 1], place.device(**{second: there}), out, slot)
    yield
    place.arrive(blocks[12], slot)
    out, slot = place.outbox(blocks[3]), place.slot()
    for sub in range(3):
        own = {a: here[a] for a in BACK[sub][:2]}
        third = BACK[sub][2]
        index = at(sub, **own)
        total = g[index].astype(F32)
        for step in range(3):
            total = total + lands[sub][2][step].astype(F32)
        g[index] = total.astype(BF16)
        for step in (1, 2, 3):
            there = place.along(third, step)
            src = g.at[at(sub, **own, **{third: there})]
            place.send(src, lands[sub][3].at[step - 1], place.device(**{third: there}), out, slot)
    yield
    place.arrive(blocks[3], slot)
    for sub in range(3):
        total = g[at(sub, **here)].astype(F32)
        for step in range(3):
            total = total + lands[sub][3][step].astype(F32)
        finish(sub, total)


def advance(*steps):
    for step in steps:
        next(step, None)


def remainder(value, count):
    value = value.astype(F32)
    whole = jnp.floor((value + 0.5) * (1.0 / count))
    return value - whole * count, whole


def gather_vectors(place, few, tiles, landed, vec):
    sublane = lax.broadcasted_iota(jnp.int32, (8, 128), 0)
    mine = place.c * 4 + place.x
    landed[3] = jnp.where(sublane == mine, few[...], 0.0)
    yield
    out, slot = place.outbox(landed.at[0:3]), place.slot()
    for step in (1, 2, 3):
        place.send(landed.at[3], landed.at[step - 1], place.device(x=place.along("x", step)), out, slot)
    yield
    place.arrive(landed.at[0:3], slot)
    landed[4] = landed[0] + landed[1] + landed[2] + landed[3]
    out, slot = place.outbox(landed.at[4]), place.slot()
    place.send(landed.at[4], landed.at[5], place.device(c=1 - place.c), out, slot)
    yield
    place.arrive(landed.at[5], slot)
    tiles[place.z, place.y] = landed[4] + landed[5]
    here = tiles.at[place.z, place.y]
    out, slot = place.outbox(landed.at[0:3]), place.slot()
    for step in (1, 2, 3):
        place.send(here, here, place.device(y=place.along("y", step)), out, slot)
    yield
    place.arrive(landed.at[0:3], slot)
    out, slot = place.outbox(tiles.at[0:3]), place.slot()
    for step in (1, 2, 3):
        place.send(tiles.at[place.z], tiles.at[place.z], place.device(z=place.along("z", step)), out, slot)
    yield
    place.arrive(tiles.at[0:3], slot)
    table = tiles[...].reshape(128, 128).astype(BF16)
    row = lax.broadcasted_iota(jnp.int32, (128, 1), 0)
    z, y, core, x = row // 32, (row // 8) % 4, (row // 4) % 2, row % 4
    device = ((z // 2) * 64 + y * 16 + x * 4 + core * 2 + z % 2).astype(F32)
    for count, width, firsts in ((6, D, (0, 6)), (18, 3 * D, (12, 30, 48))):
        part, owner = remainder(lax.broadcasted_iota(jnp.int32, (1, width), 1), count)
        lane = lax.broadcasted_iota(jnp.int32, (128, 1), 0).astype(F32)
        for first in firsts:
            choose = jnp.where(lane - first == part, 1.0, 0.0).astype(BF16)
            spread_out = nn(table, choose)
            vector = jnp.sum(jnp.where(device == owner, spread_out, 0.0), axis=0, keepdims=True)
            base = first if count == 6 else first
            for k in range(width // 128):
                vec[base + k:base + k + 1, :] = vector[:, 128 * k:128 * (k + 1)]


def sum_vectors(place, vec, incoming):
    for stage, axis in enumerate("cxyz"):
        steps = (1,) if axis == "c" else (1, 2, 3)
        whole = incoming.at[stage, 0:len(steps)]
        out, slot = place.outbox(whole), place.slot()
        for k, step in enumerate(steps):
            device = place.device(c=1 - place.c) if axis == "c" else place.device(**{axis: place.along(axis, step)})
            place.send(vec.at[stage], incoming.at[stage, k], device, out, slot)
        yield
        place.arrive(whole, slot)
        total = vec[stage]
        for k in range(len(steps)):
            total = total + incoming[stage, k]
        vec[stage + 1] = total


def nt(left, right):
    return lax.dot_general(left, right, (((1,), (1,)), ((), ())), preferred_element_type=F32)


def tn(left, right):
    return lax.dot_general(left, right, (((0,), (0,)), ((), ())), preferred_element_type=F32)


def nn(left, right):
    return jnp.dot(left, right, preferred_element_type=F32)


def columns(ref, part, jp):
    halves = [ref[part, lax.rem(jp, 2), :, zl, :, :, lax.div(jp, 2)].reshape(D, 384) for zl in range(2)]
    return jnp.concatenate(halves, axis=1)


def tile_at(t):
    j, q = READY.index(t) % 8, READY.index(t) // 8
    xl, c, zl = j // 4, j // 2 % 2, j % 2
    every = slice(None)
    return (c, every, zl, every, every, xl, every, pl.ds(128 * q, 128))


def tiles_of(w, wanted):
    return jnp.concatenate([w[(0,) + tile_at(t)].reshape(D, 128) for t in wanted], axis=1)


def put_tiles(g, wanted, value):
    low = value.astype(BF16)
    for k, t in enumerate(wanted):
        g[tile_at(t)] = low[:, 128 * k:128 * (k + 1)].reshape(2, 4, 2, 48, 128)


def put_columns(ref, part, jp, value):
    for zl in range(2):
        ref[part, lax.rem(jp, 2), :, zl, :, :, lax.div(jp, 2)] = (
            value[:, zl * 384:(zl + 1) * 384].astype(BF16).reshape(2, 4, 2, 48, 384)
        )


def row_pieces():
    return [(y, xh, xl, c) for y in range(2) for xh in range(2) for xl in range(2) for c in range(2)]


def rows(ref, jp):
    zh, y0 = lax.div(jp, 2), lax.rem(jp, 2) * 2
    halves = [
        jnp.concatenate([ref[2, c, zh, zl, y0 + y, xh, xl] for y, xh, xl, c in row_pieces()], axis=0) for zl in range(2)
    ]
    return jnp.concatenate(halves, axis=1)


def put_rows(ref, jp, value):
    zh, y0 = lax.div(jp, 2), lax.rem(jp, 2) * 2
    low = value.astype(BF16)
    for zl in range(2):
        for k, (y, xh, xl, c) in enumerate(row_pieces()):
            ref[2, c, zh, zl, y0 + y, xh, xl] = low[48 * k:48 * k + 48, zl * 384:(zl + 1) * 384]


def normalize(values):
    mean = jnp.mean(values, axis=-1, keepdims=True)
    centred = values - mean
    inverse = lax.rsqrt(jnp.mean(centred * centred, axis=-1, keepdims=True) + EPS)
    return centred * inverse, inverse


def norm_back(grad, normed, inverse):
    first = jnp.mean(grad, axis=-1, keepdims=True)
    second = jnp.mean(grad * normed, axis=-1, keepdims=True)
    return inverse * (grad - first - normed * second)


def shifted(values, steps):
    count = values.shape[0]
    row = lax.broadcasted_iota(jnp.int32, values.shape, 0)
    rolled = pltpu.roll(values, steps % count, 0)
    return jnp.where(row >= steps if steps > 0 else row < count + steps, rolled, 0.0)


def layer_kernel(tok, cot, wq, wo, wu, wd, ga, gf, taps, out, gtok, gq, go, gu, gd, gga, ggf, gtap, *scratch):
    (w, g0, h1t, h2t, from_core, to_peer, from_peer, pile, down_s, down, few, tiles, few_landed, vec, prev, h1, raw, mixed, bias,
     probs, att, h2, act, gup, gh2, gatt, acc, contrib, got, gvec, incoming, sums) = scratch[:32]
    lands, (send_sem, recv_sem) = scratch[32:-2], scratch[-2:]
    place = Place(send_sem, recv_sem)
    c, zl, rank = place.c, place.zl, place.zl
    ready = place.greet()
    for number in range(8):
        for q in range(3):
            t = READY[8 * q + number]
            source = wq[:, t * 128:(t + 1) * 128] if t < 18 else wo[:, (t - 18) * 128:(t - 17) * 128]
            to_peer[0, number, 0:6, q * 128:(q + 1) * 128] = source.astype(F32)
        to_peer[1, number, 0:6, :] = wu[:, number * 384:(number + 1) * 384].astype(F32)
    left, right = wd[:, 0:384].astype(F32), wd[:, 384:768].astype(F32)
    down_s[...] = jnp.where(zl == 0, right, left)
    down[pl.ds(pl.multiple_of(zl * 24, 8), 24), :] = jnp.where(zl == 0, left, right)
    few[...] = jnp.zeros_like(few)
    few[0:1, 0:6] = ga[...].astype(F32)
    few[0:1, 6:12] = gf[...].astype(F32)
    for j in range(3):
        few[0:1, 12 + 18 * j:30 + 18 * j] = taps[j:j + 1, :].astype(F32)
    few[...] = jnp.broadcast_to(few[0:1, :], (8, 128))
    vectors = gather_vectors(place, few, tiles, few_landed, vec)
    advance(vectors)
    ready()

    other = place.device(z=place.flip(place.z, 1))
    trades, trade_down, token_slot, back_slot = place.slot(2), place.slot(), place.slot(), place.slot()
    out_trades, out_down = [place.outbox(from_peer.at[0, 0:7]) for _ in range(2)], place.outbox(down_s)
    out_tokens = place.outbox()
    _, mine = place.member(0)
    def trade(k):
        for d in range(1, 8):
            device, number = place.member(d)
            place.send(to_peer.at[k, number], from_peer.at[k, mine], device, out_trades[k], trades + k)

    trade(0)
    trade(1)
    place.send(down_s, down.at[pl.ds(pl.multiple_of(zl * 24, 8), 24)], other, out_down, trade_down)
    next(vectors)

    for k in range(2):
        from_peer[k, mine] = to_peer[k, mine]

    def normalize_half(half):
        return normalize((prev if half == 0 else tok)[...].astype(F32))

    place.arrive(down_s, trade_down)
    at = (c, lax.div(place.z, 2), zl, place.y, lax.div(place.x, 2), lax.rem(place.x, 2))
    for k in range(2):
        place.arrive(from_peer.at[k, 0:7], trades + k)
        for number in range(8):
            pile[k, 6 * number:6 * number + 8, :] = from_peer[k, number]
        w[(k,) + at] = pile[k, 0:48, :].astype(BF16)
    w[(2,) + at] = down[...].astype(BF16)
    phase = [gather_phase(place, w, part, LEAN_IN[part]) for part in range(3)]
    advance(vectors)
    for _ in range(3):
        advance(*phase)
        advance(vectors)

    @pl.when(zl == 0)
    def _():
        place.send(tok, prev, other, out_tokens, token_slot)

    advance(*phase)

    @pl.when(zl == 1)
    def _():
        place.arrive(prev, token_slot)

    @pl.when(zl == 0)
    def _():
        prev[...] = jnp.zeros_like(prev)

    gain_one = jnp.concatenate([vec[r:r + 1, :] for r in range(6)], axis=1)
    gain_two = jnp.concatenate([vec[r:r + 1, :] for r in range(6, 12)], axis=1)
    for half in range(2):
        h1[half * ROWS:(half + 1) * ROWS, :] = (normalize_half(half)[0] * gain_one).astype(BF16)
    h1t[...] = h1[...].T
    row = lax.broadcasted_iota(jnp.int32, (ROWS, EXT), 0)
    column = lax.broadcasted_iota(jnp.int32, (ROWS, EXT), 1)
    behind = jnp.where(column < ROWS, (1 - rank) * EXT, column - ROWS)
    bias[...] = jnp.where(behind <= row, 0.0, -1e30)
    first = lax.broadcasted_iota(jnp.int32, (ROWS, 128), 1) < 64
    gvec[0] = jnp.zeros((VEC, 128), F32)
    advance(*phase)
    advance(phase[0])

    def tap(j, t):
        return vec[pl.ds(12 + TILES * j + t, 1), :]

    for jp in range(3):
        block = nn(h1[...], tiles_of(w, range(6 * jp, 6 * jp + 6))).astype(BF16)
        for k in range(6):
            t = 6 * jp + k
            tile = block[:, 128 * k:128 * (k + 1)]
            raw[t] = tile
            value = tile.astype(F32)
            conv = tap(0, t) * value + tap(1, t) * shifted(value, 1) + tap(2, t) * shifted(value, 2)
            mixed[t] = conv.astype(BF16)

    def both(value):
        zero = jnp.zeros_like(value)
        return jnp.concatenate([jnp.where(first, value, zero), jnp.where(first, zero, value)], axis=0)

    def pick(value):
        return jnp.where(first, value[:ROWS], value[ROWS:])

    def attend(p):
        query = both(mixed[p, ROWS:, :])
        key, value = mixed[PAIRS + p], mixed[2 * PAIRS + p]
        scores = nt(query, key) * 0.125 + jnp.concatenate([bias[...], bias[...]], axis=0)
        weights = jnp.exp(scores - jnp.max(scores, axis=-1, keepdims=True))
        exact = weights * (1.0 / jnp.sum(weights, axis=-1, keepdims=True))
        probs[p] = exact
        att[p] = pick(nn(exact.astype(BF16), value)).astype(BF16)

    for p in range(PAIRS):
        attend(p)

    attended = jnp.concatenate([att[p] for p in range(PAIRS)], axis=1)
    resid = tok[...].astype(F32) + nn(attended, tiles_of(w, range(18, 24)))
    normed_two, inverse_two = normalize(resid)
    h2[...] = (normed_two * gain_two).astype(BF16)
    h2t[...] = h2[...].T
    acc[...] = resid
    advance(phase[1], phase[1], phase[1])

    @pl.loop(0, 4)
    def _(jp):
        rect = jnp.maximum(nn(h2[...], columns(w, 1, jp)), 0.0)
        act[jp] = (rect * rect).astype(BF16)
        gup[jp] = rect.astype(BF16)

    for _ in range(6):
        advance(phase[2])
    place.drain()

    @pl.when(zl == 0)
    def _():
        place.copy(tok, tok, other, out_tokens, 0).wait_send()

    sibling = place.device(c=1 - c)
    across = [place.slot(3), place.slot(2), place.slot(4)]
    out_across = [place.outbox(w.at[part, 0]) for part in range(3)]
    every = slice(None)

    @pl.loop(0, 4)
    def _(jp):
        low = rows(w, jp)
        gup[jp] = (nt(cot[...], low) * 2.0 * gup[jp].astype(F32)).astype(BF16)
        acc[...] += nn(act[jp], low)
        put_rows(w, jp, tn(act[jp], cot[...]))
        some = (lax.div(jp, 2), slice(None), pl.ds(lax.rem(jp, 2) * 2, 2))
        place.send(w.at[(2, 1 - c) + some], from_core.at[(2,) + some], sibling, out_across[2], across[2] + jp)

    gh2[...] = jnp.zeros_like(gh2)

    def widen(jp):
        gh2[...] += nt(gup[jp], columns(w, 1, jp))
        put_columns(w, 1, jp, nn(h2t[...], gup[jp]))

        @pl.when(lax.rem(jp, 2) == 1 - c)
        def _():
            xl = lax.div(jp, 2)
            src, dst = w.at[1, 1 - c, :, :, :, :, xl], from_core.at[1, :, :, :, :, xl]
            place.send(src, dst, sibling, out_across[1], across[1] + xl)

    strips = [strip(sub) for sub in range(3)]

    def finish(part):
        def store(sub, total):
            sums[part, 16 * sub:16 * sub + 16, :] = total
        return store

    def finish_chunk(first, width):
        def store(sub, total):
            sums[0, 16 * sub:16 * sub + 16, first:first + width] = total
        return store

    def land(k):
        return [lands[12 * k + 4 * sub:12 * k + 4 * sub + 4] for sub in range(3)]

    def cross(k):
        cut = (1 - c,) + (every,) * 6 + (pl.ds(*CHUNKS[k]),)
        place.send(g0.at[cut], from_core.at[(0,) + cut[1:]], sibling, out_across[0], across[0] + k)

    up_ready = [((every,) * 4 + (xl,), across[1] + xl) for xl in range(2)]
    down_ready = [((jp // 2, every, pl.ds(jp % 2 * 2, 2)), across[2] + jp) for jp in range(4)]
    ups = scatter_phase(place, w, (1,), strips, up_ready, from_core.at[1], land(2), finish(1), True, LEAN_OUT[1])
    downs = scatter_phase(place, w, (2,), strips, down_ready, from_core.at[2], land(3), finish(2), True, LEAN_OUT[2])
    chunks = []
    for k, (start, width) in enumerate(CHUNKS):
        cut = (pl.ds(start, width),)
        came = [((every,) * 6 + cut, across[0] + k)]
        tails = [(pl.ds(16 * sub, 16),) + cut for sub in range(3)]
        chunks.append(scatter_phase(place, g0, (), tails, came, from_core.at[0], land(k), finish_chunk(start, width), k == 0, LEAN_OUT[0]))
    pl.loop(0, 2)(widen)
    advance(downs)
    pl.loop(2, 4)(widen)
    out[...] = acc[...].astype(BF16)
    grad_two = gh2[...]
    summed = jnp.sum(grad_two * normed_two, axis=0, keepdims=True)
    for r in range(6):
        gvec[0, 6 + r:7 + r, :] = summed[:, 128 * r:128 * (r + 1)]
    grad_resid = cot[...].astype(F32) + norm_back(grad_two * gain_two, normed_two, inverse_two)
    acc[...] = grad_resid
    gproj = grad_resid.astype(BF16)
    gback = nt(gproj, tiles_of(w, range(18, 24))).astype(BF16)
    for p in range(PAIRS):
        gatt[p] = gback[:, 128 * p:128 * (p + 1)]
    advance(ups)
    put_tiles(g0, range(18, 24), tn(attended, gproj))

    def attend_back(p):
        query = both(mixed[p, ROWS:, :])
        key, value = mixed[PAIRS + p], mixed[2 * PAIRS + p]
        grad = both(gatt[p])
        exact = probs[p]
        gvalue = tn(exact.astype(BF16), grad)
        gprobs = nt(grad, value)
        centred = gprobs - jnp.sum(gprobs * exact, axis=-1, keepdims=True)
        gscores = (exact * centred).astype(BF16)
        gquery = pick(nn(gscores, key)) * 0.125
        gkey = tn(gscores, query) * 0.125
        for k, tile in enumerate((jnp.concatenate([jnp.zeros_like(gquery), gquery], axis=0), gkey, gvalue)):
            t = PAIRS * k + p
            back = tap(0, t) * tile + tap(1, t) * shifted(tile, -1) + tap(2, t) * shifted(tile, -2)
            mixed[t] = back.astype(BF16)
            value_in = raw[t].astype(F32)
            for j in range(3):
                delayed = value_in if j == 0 else shifted(value_in, j)
                gvec[0, pl.ds(12 + TILES * j + t, 1), :] = jnp.sum(tile * delayed, axis=0, keepdims=True)

    def weigh(wanted):
        put_tiles(g0, wanted, nn(h1t[...], jnp.concatenate([mixed[t] for t in wanted], axis=1)))

    attend_back(0)
    attend_back(1)
    attend_back(2)
    attend_back(3)
    weigh(READY[6:16])
    cross(0)
    attend_back(4)
    attend_back(5)
    weigh(READY[16:24])
    cross(1)
    advance(downs)
    advance(chunks[0])

    out_back = place.outbox()

    def through_norm(half):
        here = pl.ds(half * ROWS, ROWS)
        grad_one = jnp.zeros((ROWS, D), F32)
        for jp in range(3):
            grad = jnp.concatenate([mixed[6 * jp + k, here, :] for k in range(6)], axis=1)
            grad_one = grad_one + nt(grad, tiles_of(w, range(6 * jp, 6 * jp + 6)))
        normed, inverse = normalize_half(half)
        return jnp.sum(grad_one * normed, axis=0, keepdims=True), norm_back(grad_one * gain_one, normed, inverse)

    total, back = through_norm(0)
    contrib[...] = back.astype(BF16)

    @pl.when(zl == 1)
    def _():
        place.send(contrib, got, other, out_back, back_slot)

    advance(ups)
    advance(chunks[1])
    gain, back = through_norm(1)
    acc[...] += back
    total = total + gain
    for r in range(6):
        gvec[0, r:r + 1, :] = total[:, 128 * r:128 * (r + 1)]
    small = sum_vectors(place, gvec, incoming)
    advance(small)
    advance(chunks[0], downs, ups, chunks[1])
    advance(small)
    advance(chunks[0], downs, ups, chunks[1])
    advance(small)
    advance(chunks[0], downs, ups)

    trades, trade_down = place.slot(2), place.slot()
    back_from, arrived = pile.at[0, pl.ds(0, 24)], from_peer
    out_trades, out_down = [place.outbox(from_peer.at[0, 0:7]) for _ in range(2)], place.outbox(back_from)

    def hand_back(k):
        for number in range(8):
            to_peer[k, number, 0:6, :] = sums[k, 6 * number:6 * number + 6, :]
        for d in range(1, 8):
            device, number = place.member(d)
            place.send(to_peer.at[k, number], arrived.at[k, mine], device, out_trades[k], trades + k)
        arrived[k, mine] = to_peer[k, mine]

    hand_back(1)
    place.send(sums.at[2, pl.ds(pl.multiple_of((1 - zl) * 24, 8), 24)], back_from, other, out_down, trade_down)
    advance(chunks[1], chunks[0])
    hand_back(0)
    advance(small, small, small)
    summed = gvec[4]
    gains = [jnp.concatenate([summed[r:r + 1] for r in range(6 * k, 6 * k + 6)], axis=1) for k in range(2)]
    tapped = [jnp.concatenate([summed[r:r + 1] for r in range(12 + TILES * j, 12 + TILES * j + TILES)], axis=1) for j in range(3)]
    gain_rows = jnp.concatenate(gains + [jnp.zeros((6, D), F32)], axis=0)
    tap_rows = jnp.concatenate(tapped + [jnp.zeros((5, 3 * D), F32)], axis=0)
    exactly = functools.partial(
        lax.dot_general,
        dimension_numbers=(((1,), (1,)), ((), ())),
        preferred_element_type=F32,
        precision=lax.Precision.HIGHEST,
    )
    gain_own = exactly(gain_rows, spread(place.index, 6, D))
    gga[...] = gain_own[0:1, 0:6]
    ggf[...] = gain_own[1:2, 0:6]
    gtap[...] = exactly(tap_rows, spread(place.index, 18, 3 * D))[0:3, 0:18]

    @pl.when(zl == 0)
    def _():
        place.arrive(got, back_slot)

    @pl.when(zl == 1)
    def _():
        got[...] = jnp.zeros_like(got)

    gtok[...] = (acc[...] + got[...].astype(F32)).astype(BF16)
    for k in range(2):
        place.arrive(arrived.at[k, 0:7], trades + k)
    place.arrive(back_from, trade_down)
    for number in range(8):
        for q in range(3):
            t = READY[8 * q + number]
            tile = arrived[0, number, 0:6, 128 * q:128 * (q + 1)]
            if t < 18:
                gq[:, 128 * t:128 * (t + 1)] = tile
            else:
                go[:, 128 * (t - 18):128 * (t - 17)] = tile
        gu[:, 384 * number:384 * (number + 1)] = arrived[1, number, 0:6, :]
    own = sums[2, pl.ds(pl.multiple_of(zl * 24, 8), 24), :]
    theirs = pile[0, 0:24, :]
    gd[:, 0:384] = jnp.where(zl == 0, own, theirs)
    gd[:, 384:768] = jnp.where(zl == 0, theirs, own)
    place.drain()

    @pl.when(zl == 1)
    def _():
        place.copy(contrib, contrib, other, out_back, 0).wait_send()


def kept(axes):
    grid = []
    for axis in "zyx":
        if axis not in axes:
            grid += {"z": [2, 2], "y": [4], "x": [2, 2]}[axis]
    return tuple(grid)


RESULTS = (
    ((ROWS, D), BF16),
    ((ROWS, D), BF16),
    ((6, 2304), F32),
    ((6, 768), F32),
    ((6, 3072), F32),
    ((24, 768), F32),
    ((1, 6), F32),
    ((1, 6), F32),
    ((3, 18), F32),
)


def layer(*args):
    vmem = pl.BlockSpec(memory_space=pltpu.VMEM)
    lands = []
    for k in range(4):
        for sub in range(3):
            order = BACK[sub]
            grids = [(2,) + HALVES[order[0]], (2,) + kept(order[:1]), (3,) + kept(order[:2]), (3,)]
            if k == 1:
                grids[:2] = [(1,), (3,) + kept(order[:1])]
            lands += [pltpu.VMEM(grid + (16, CHUNKS[k][1] if k < 2 else 384), BF16) for grid in grids]
    return pl.pallas_call(
        layer_kernel,
        out_shape=tuple(jax.ShapeDtypeStruct(*result) for result in RESULTS),
        in_specs=[vmem] * 9,
        out_specs=(vmem,) * 9,
        scratch_shapes=[
            pltpu.VMEM((3,) + GRID + BLOCK, BF16),
            pltpu.VMEM(GRID + BLOCK, BF16),
            pltpu.VMEM((D, EXT), BF16),
            pltpu.VMEM((D, ROWS), BF16),
            pltpu.VMEM((3,) + GRID[1:] + BLOCK, BF16),
            pltpu.VMEM((2, 8, 8, 384), F32),
            pltpu.VMEM((2, 8, 8, 384), F32),
            pltpu.VMEM((2, 56, 384), F32),
            pltpu.VMEM((24, 384), F32),
            pltpu.VMEM((48, 384), F32),
            pltpu.VMEM((8, 128), F32),
            pltpu.VMEM((4, 4, 8, 128), F32),
            pltpu.VMEM((8, 8, 128), F32),
            pltpu.VMEM((VEC, 128), F32),
            pltpu.VMEM((ROWS, D), BF16),
            pltpu.VMEM((EXT, D), BF16),
            pltpu.VMEM((TILES, EXT, 128), BF16),
            pltpu.VMEM((TILES, EXT, 128), BF16),
            pltpu.VMEM((ROWS, EXT), F32),
            pltpu.VMEM((PAIRS, EXT, EXT), F32),
            pltpu.VMEM((PAIRS, ROWS, 128), BF16),
            pltpu.VMEM((ROWS, D), BF16),
            pltpu.VMEM((4, ROWS, D), BF16),
            pltpu.VMEM((4, ROWS, D), BF16),
            pltpu.VMEM((ROWS, D), F32),
            pltpu.VMEM((PAIRS, ROWS, 128), BF16),
            pltpu.VMEM((ROWS, D), F32),
            pltpu.VMEM((ROWS, D), BF16),
            pltpu.VMEM((ROWS, D), BF16),
            pltpu.VMEM((5, VEC, 128), F32),
            pltpu.VMEM((4, 3, VEC, 128), F32),
            pltpu.VMEM((3,) + BLOCK, F32),
            *lands,
            pltpu.SemaphoreType.DMA((64,)),
            pltpu.SemaphoreType.DMA((120,)),
        ],
        compiler_params=pltpu.CompilerParams(collective_id=0, has_side_effects=True, vmem_limit_bytes=LIMIT),
    )(*args)


def copy_kernel(*refs):
    for source, target in zip(refs[:len(RESULTS)], refs[len(RESULTS):]):
        target[...] = source[...]


def copied(*args):
    vmem = pl.BlockSpec(memory_space=pltpu.VMEM)
    return pl.pallas_call(
        copy_kernel,
        out_shape=tuple(jax.ShapeDtypeStruct(*result) for result in RESULTS),
        in_specs=[vmem] * len(RESULTS),
        out_specs=(vmem,) * len(RESULTS),
    )(*args)


def per_device(tokens, w_qkv, w_out, w_up, w_down, gain_attn, gain_ffn, conv_taps, cotangent):
    results = copied(*layer(
        tokens, cotangent, w_qkv, w_out, w_up, w_down, gain_attn.reshape(1, 6), gain_ffn.reshape(1, 6), conv_taps
    ))
    return results[:6] + (results[6].reshape(6), results[7].reshape(6), results[8])


def solution(mesh):
    both = ("grp", "seq")
    row, one, column = P(both, None), P(both), P(None, both)
    return jax.shard_map(
        per_device,
        mesh=mesh,
        in_specs=(row, row, row, row, row, one, one, column, row),
        out_specs=(row, row, row, row, row, row, one, one, column),
        check_vma=False,
    )
```

```python
import functools

import jax
import jax.numpy as jnp
from jax import lax
from jax.experimental import pallas as pl
from jax.experimental.pallas import tpu as pltpu
from jax.sharding import PartitionSpec as P

MESH = pl.DeviceIdType.MESH
F32 = jnp.float32
BF16 = jnp.bfloat16
EPS = 1e-05
D = 768
ROWS = 256
EXT = 512
PAIRS = 6
TILES = 18
BLOCK = (48, 384)
GRID = (2, 2, 2, 4, 2, 2)
VEC = 80
ORDERS = (("x", "y", "z"), ("y", "z", "x"), ("z", "x", "y"))
BACK = (("z", "y", "x"), ("x", "z", "y"), ("y", "x", "z"))
LIMIT = 60 * 2**20
READY = tuple(range(18, 24)) + tuple(t for p in range(6) for t in (p, 6 + p, 12 + p))
CHUNKS = ((0, 256), (256, 128))

LEAN_IN = (False, True, True)
LEAN_OUT = (True, True, True)


class Place:
    def __init__(self, send_sem, recv_sem):
        grp, seq = lax.axis_index("grp"), lax.axis_index("seq")
        self.c = lax.rem(grp, 2)
        self.x = lax.rem(lax.div(grp, 2), 4)
        self.y = lax.rem(lax.div(grp, 8), 4)
        self.z = lax.div(grp, 32) * 2 + seq
        self.zl = seq
        self.index = grp * 2 + seq
        self.send_sem, self.recv_sem = send_sem, recv_sem
        self.sends = self.receives = 0
        self.owed = []

    def device(self, **new):
        at = {"x": self.x, "y": self.y, "z": self.z, "c": self.c}
        at.update(new)
        grp = ((lax.div(at["z"], 2) * 4 + at["y"]) * 4 + at["x"]) * 2 + at["c"]
        return (grp, lax.rem(at["z"], 2))

    def along(self, axis, delta):
        return lax.rem(getattr(self, axis) + delta, 4)

    def flip(self, value, bit):
        return value + bit * (1 - 2 * lax.rem(value, 2))

    def member(self, d):
        x, c, z = self.flip(self.x, d // 4), self.flip(self.c, (d // 2) % 2), self.flip(self.z, d % 2)
        number = lax.rem(x, 2) * 4 + c * 2 + lax.rem(z, 2)
        return self.device(x=x, c=c, z=z), number

    def greet(self):
        barrier = pltpu.get_barrier_semaphore()
        partners = [self.device(**{a: self.along(a, d)}) for a in "xyz" for d in (1, 2, 3)]
        partners += [self.member(d)[0] for d in (2, 3, 5, 6, 7)]
        for partner in partners:
            pl.semaphore_signal(barrier, inc=1, device_id=partner, device_id_type=MESH)
        return lambda: pl.semaphore_wait(barrier, len(partners))

    def slot(self, count=1):
        self.receives += count
        return self.receives - count

    def outbox(self, *wholes):
        self.sends += 1
        self.owed.append((self.sends - 1, wholes))
        return self.sends - 1

    def copy(self, src, dst, device, out, slot):
        return pltpu.make_async_remote_copy(
            src_ref=src,
            dst_ref=dst,
            send_sem=self.send_sem.at[out],
            recv_sem=self.recv_sem.at[slot],
            device_id=device,
            device_id_type=MESH,
        )

    def send(self, src, dst, device, out, slot):
        self.copy(src, dst, device, out, slot).start()

    def arrive(self, whole, slot):
        self.copy(whole, whole, self.device(), 0, slot).wait_recv()

    def drain(self):
        for out, wholes in self.owed:
            for whole in wholes:
                self.copy(whole, whole, self.device(), out, 0).wait_send()
        self.owed = []


def spot(lead, c=None, tail=(), **at):
    index = list(lead) + [slice(None) if c is None else c]
    for axis in "zyx":
        value = at.get(axis)
        half = isinstance(value, tuple)
        if axis == "y":
            index.append(pl.ds(2 * value[1], 2) if half else slice(None) if value is None else value)
        elif half:
            index += [value[1], slice(None)]
        elif value is None:
            index += [slice(None), slice(None)]
        else:
            index += [lax.div(value, 2), lax.rem(value, 2)]
    return tuple(index) + tail


def strip(sub):
    return (pl.ds(16 * sub, 16), slice(None))


def spread(index, count, width):
    row = lax.broadcasted_iota(jnp.int32, (128, width), 0)
    column = lax.broadcasted_iota(jnp.int32, (128, width), 1)
    return jnp.where((column == count * index + row) & (row < count), 1.0, 0.0)


def gather_phase(place, w, part, lean):
    c = place.c
    here = {"x": place.x, "y": place.y, "z": place.z}
    sibling = place.device(c=1 - c)
    blocks = {3: w.at[part, 0, 0, 0, 0:3, 0, 0], 12: w.at[part, 0, 0, 0, 0:3], 16: w.at[part, 0, 0, 0], 48: w.at[part, 0, :, :, 0:3], 64: w.at[part, 0]}
    passing, passed = place.outbox(blocks[64]), place.slot()

    def piece(sub, **at):
        return w.at[spot((part,), c, strip(sub), **at)]

    def pass_on(sub, **at):
        place.send(piece(sub, **at), piece(sub, **at), sibling, passing, passed)

    for stage, count in ((0, 3), (1, 12)):
        out, slot = place.outbox(blocks[count]), place.slot()
        for sub in range(3):
            axis, done = ORDERS[sub][stage], ORDERS[sub][:stage]
            own = piece(sub, **{a: here[a] for a in "xyz" if a not in done})
            for step in (1, 2, 3):
                place.send(own, own, place.device(**{axis: place.along(axis, step)}), out, slot)
        yield
        place.arrive(blocks[count], slot)
    out, sides, last = place.outbox(blocks[48]), place.slot(6), place.slot()

    def toward(axis, side):
        return place.device(**{axis: place.along(axis, 3 if side else 1)})

    for sub in range(3):
        axis = ORDERS[sub][2]
        own = piece(sub, **{axis: here[axis]})
        for side in range(2):
            place.send(own, own, toward(axis, side), out, sides + 2 * sub + side)
    for sub in range(3):
        axis = ORDERS[sub][2]
        pass_on(sub, **{axis: here[axis]})
    yield
    for side in range(2):
        for sub in range(3):
            axis, whole = ORDERS[sub][2], ORDERS[sub][0]
            came = {axis: place.along(axis, 1 if side else 3)}
            place.arrive(piece(sub, **came), sides + 2 * sub + side)
            down_only = lean and axis == "z"
            if not down_only or side == 1:
                half = piece(sub, **came) if down_only else piece(sub, **came, **{whole: ("half", side)})
                place.send(half, half, toward(axis, side), out, last)
            pass_on(sub, **came)
    yield
    place.arrive(blocks[16], last)
    for sub in range(3):
        axis = ORDERS[sub][2]
        pass_on(sub, **{axis: place.along(axis, 2)})
    yield
    place.arrive(blocks[64], passed)


HALF = {"z": "y", "x": "z", "y": "x"}
HALVES = {"z": (2, 2, 2), "x": (2, 4), "y": (2, 2, 2)}


def half_of(axis, h):
    return {"z": (pl.ds(2 * h, 2),), "x": (h,), "y": (slice(None), slice(None), h)}[axis]


def scatter_phase(place, g, lead, tails, arrivals, landed, lands, finish, relayed, lean):
    c = place.c
    here = {"x": place.x, "y": place.y, "z": place.z}
    tail = (slice(None), tails[0][1])
    corner = lead + (0, 0, 0)
    blocks = {
        3: g.at[corner + (pl.ds(0, 3), 0, 0) + tail],
        12: g.at[corner + (pl.ds(0, 3), slice(None), slice(None)) + tail],
        48: g.at[lead + (0, slice(None), slice(None), pl.ds(0, 3), slice(None), slice(None)) + tail],
    }

    def at(sub, **where):
        return spot(lead, c, tails[sub], **where)

    for index, slot in arrivals:
        place.arrive(landed.at[index], slot)
        g[lead + (c,) + index] = g[lead + (c,) + index] + landed[index]
    out = place.outbox(blocks[48])

    def ways(sub):
        axis = BACK[sub][0]
        way = [(t, place.device(**{axis: t})) for t in (place.along(axis, 1), place.along(axis, 3))]
        return axis, HALF[axis], way, (0, 0) if lean and axis == "z" else (0, 1)

    if relayed:
        relays, sides = place.slot(6), place.slot(3)
        for sub in range(3):
            axis, whole, way, course = ways(sub)
            across = place.along(axis, 2)
            for k in range(2):
                src = g.at[at(sub, **{axis: across, whole: ("half", k)})]
                place.send(src, lands[sub][0].at[k], way[course[k]][1], out, relays + 2 * sub + k)
        for sub in range(3):
            axis, whole, way, course = ways(sub)
            for k in range(2):
                toward = 1 - course[k]
                coordinate, device = way[toward]
                src = g.at[at(sub, **{axis: coordinate, whole: ("half", k)})]
                place.send(src, lands[sub][1].at[(toward,) + half_of(axis, k)], device, out, sides + sub)
        yield
        for sub in range(3):
            axis, whole, way, course = ways(sub)
            relay, side = lands[sub][:2]
            for k in range(2):
                coordinate, device = way[course[k]]
                place.arrive(relay.at[k], relays + 2 * sub + k)
                index = at(sub, **{axis: coordinate, whole: ("half", k)})
                g[index] = g[index] + relay[k]
                place.send(g.at[index], side.at[(course[k],) + half_of(axis, k)], device, out, sides + sub)
        yield
    else:
        sides = place.slot(3)
        for step in (2, 1, 3):
            for sub in range(3):
                axis = BACK[sub][0]
                there = place.along(axis, step)
                src = g.at[at(sub, **{axis: there})]
                place.send(src, lands[sub][1].at[step - 1], place.device(**{axis: there}), out, sides + sub)
        yield
    out, slot = place.outbox(blocks[12]), place.slot()
    for sub in range(3):
        axis, second = BACK[sub][0], BACK[sub][1]
        side = lands[sub][1]
        place.arrive(side, sides + sub)
        index = at(sub, **{axis: here[axis]})
        total = g[index].astype(F32)
        for k in range(side.shape[0]):
            total = total + side[k].astype(F32)
        g[index] = total.astype(BF16)
        for step in (1, 2, 3):
            there = place.along(second, step)
            src = g.at[at(sub, **{axis: here[axis], second: there})]
            place.send(src, lands[sub][2].at[step - 1], place.device(**{second: there}), out, slot)
    yield
    place.arrive(blocks[12], slot)
    out, slot = place.outbox(blocks[3]), place.slot()
    for sub in range(3):
        own = {a: here[a] for a in BACK[sub][:2]}
        third = BACK[sub][2]
        index = at(sub, **own)
        total = g[index].astype(F32)
        for step in range(3):
            total = total + lands[sub][2][step].astype(F32)
        g[index] = total.astype(BF16)
        for step in (1, 2, 3):
            there = place.along(third, step)
            src = g.at[at(sub, **own, **{third: there})]
            place.send(src, lands[sub][3].at[step - 1], place.device(**{third: there}), out, slot)
    yield
    place.arrive(blocks[3], slot)
    for sub in range(3):
        total = g[at(sub, **here)].astype(F32)
        for step in range(3):
            total = total + lands[sub][3][step].astype(F32)
        finish(sub, total)


def advance(*steps):
    for step in steps:
        next(step, None)


def remainder(value, count):
    value = value.astype(F32)
    whole = jnp.floor((value + 0.5) * (1.0 / count))
    return value - whole * count, whole


def gather_vectors(place, few, tiles, landed, vec):
    sublane = lax.broadcasted_iota(jnp.int32, (8, 128), 0)
    mine = place.c * 4 + place.x
    landed[3] = jnp.where(sublane == mine, few[...], 0.0)
    yield
    out, slot = place.outbox(landed.at[0:3]), place.slot()
    for step in (1, 2, 3):
        place.send(landed.at[3], landed.at[step - 1], place.device(x=place.along("x", step)), out, slot)
    yield
    place.arrive(landed.at[0:3], slot)
    landed[4] = landed[0] + landed[1] + landed[2] + landed[3]
    out, slot = place.outbox(landed.at[4]), place.slot()
    place.send(landed.at[4], landed.at[5], place.device(c=1 - place.c), out, slot)
    yield
    place.arrive(landed.at[5], slot)
    tiles[place.z, place.y] = landed[4] + landed[5]
    here = tiles.at[place.z, place.y]
    out, slot = place.outbox(landed.at[0:3]), place.slot()
    for step in (1, 2, 3):
        place.send(here, here, place.device(y=place.along("y", step)), out, slot)
    yield
    place.arrive(landed.at[0:3], slot)
    out, slot = place.outbox(tiles.at[0:3]), place.slot()
    for step in (1, 2, 3):
        place.send(tiles.at[place.z], tiles.at[place.z], place.device(z=place.along("z", step)), out, slot)
    yield
    place.arrive(tiles.at[0:3], slot)
    table = tiles[...].reshape(128, 128).astype(BF16)
    row = lax.broadcasted_iota(jnp.int32, (128, 1), 0)
    z, y, core, x = row // 32, (row // 8) % 4, (row // 4) % 2, row % 4
    device = ((z // 2) * 64 + y * 16 + x * 4 + core * 2 + z % 2).astype(F32)
    for count, width, firsts in ((6, D, (0, 6)), (18, 3 * D, (12, 30, 48))):
        part, owner = remainder(lax.broadcasted_iota(jnp.int32, (1, width), 1), count)
        lane = lax.broadcasted_iota(jnp.int32, (128, 1), 0).astype(F32)
        for first in firsts:
            choose = jnp.where(lane - first == part, 1.0, 0.0).astype(BF16)
            spread_out = nn(table, choose)
            vector = jnp.sum(jnp.where(device == owner, spread_out, 0.0), axis=0, keepdims=True)
            base = first if count == 6 else first
            for k in range(width // 128):
                vec[base + k:base + k + 1, :] = vector[:, 128 * k:128 * (k + 1)]


def sum_vectors(place, vec, incoming):
    for stage, axis in enumerate("cxyz"):
        steps = (1,) if axis == "c" else (1, 2, 3)
        whole = incoming.at[stage, 0:len(steps)]
        out, slot = place.outbox(whole), place.slot()
        for k, step in enumerate(steps):
            device = place.device(c=1 - place.c) if axis == "c" else place.device(**{axis: place.along(axis, step)})
            place.send(vec.at[stage], incoming.at[stage, k], device, out, slot)
        yield
        place.arrive(whole, slot)
        total = vec[stage]
        for k in range(len(steps)):
            total = total + incoming[stage, k]
        vec[stage + 1] = total


def nt(left, right):
    return lax.dot_general(left, right, (((1,), (1,)), ((), ())), preferred_element_type=F32)


def tn(left, right):
    return lax.dot_general(left, right, (((0,), (0,)), ((), ())), preferred_element_type=F32)


def nn(left, right):
    return jnp.dot(left, right, preferred_element_type=F32)


def columns(ref, part, jp):
    halves = [ref[part, lax.rem(jp, 2), :, zl, :, :, lax.div(jp, 2)].reshape(D, 384) for zl in range(2)]
    return jnp.concatenate(halves, axis=1)


def tile_at(t):
    j, q = READY.index(t) % 8, READY.index(t) // 8
    xl, c, zl = j // 4, j // 2 % 2, j % 2
    every = slice(None)
    return (c, every, zl, every, every, xl, every, pl.ds(128 * q, 128))


def tiles_of(w, wanted):
    return jnp.concatenate([w[(0,) + tile_at(t)].reshape(D, 128) for t in wanted], axis=1)


def put_tiles(g, wanted, value):
    low = value.astype(BF16)
    for k, t in enumerate(wanted):
        g[tile_at(t)] = low[:, 128 * k:128 * (k + 1)].reshape(2, 4, 2, 48, 128)


def put_columns(ref, part, jp, value):
    for zl in range(2):
        ref[part, lax.rem(jp, 2), :, zl, :, :, lax.div(jp, 2)] = (
            value[:, zl * 384:(zl + 1) * 384].astype(BF16).reshape(2, 4, 2, 48, 384)
        )


def row_pieces():
    return [(y, xh, xl, c) for y in range(2) for xh in range(2) for xl in range(2) for c in range(2)]


def rows(ref, jp):
    zh, y0 = lax.div(jp, 2), lax.rem(jp, 2) * 2
    halves = [
        jnp.concatenate([ref[2, c, zh, zl, y0 + y, xh, xl] for y, xh, xl, c in row_pieces()], axis=0) for zl in range(2)
    ]
    return jnp.concatenate(halves, axis=1)


def put_rows(ref, jp, value):
    zh, y0 = lax.div(jp, 2), lax.rem(jp, 2) * 2
    low = value.astype(BF16)
    for zl in range(2):
        for k, (y, xh, xl, c) in enumerate(row_pieces()):
            ref[2, c, zh, zl, y0 + y, xh, xl] = low[48 * k:48 * k + 48, zl * 384:(zl + 1) * 384]


def normalize(values):
    mean = jnp.mean(values, axis=-1, keepdims=True)
    centred = values - mean
    inverse = lax.rsqrt(jnp.mean(centred * centred, axis=-1, keepdims=True) + EPS)
    return centred * inverse, inverse


def norm_back(grad, normed, inverse):
    first = jnp.mean(grad, axis=-1, keepdims=True)
    second = jnp.mean(grad * normed, axis=-1, keepdims=True)
    return inverse * (grad - first - normed * second)


def shifted(values, steps):
    count = values.shape[0]
    row = lax.broadcasted_iota(jnp.int32, values.shape, 0)
    rolled = pltpu.roll(values, steps % count, 0)
    return jnp.where(row >= steps if steps > 0 else row < count + steps, rolled, 0.0)


def layer_kernel(tok, cot, wq, wo, wu, wd, ga, gf, taps, out, gtok, gq, go, gu, gd, gga, ggf, gtap, *scratch):
    (w, g0, h1t, h2t, from_core, to_peer, from_peer, pile, down_s, down, few, tiles, few_landed, vec, prev, h1, raw, mixed, bias,
     probs, att, h2, act, gup, gh2, gatt, acc, contrib, got, gvec, incoming, sums) = scratch[:32]
    lands, (send_sem, recv_sem) = scratch[32:-2], scratch[-2:]
    place = Place(send_sem, recv_sem)
    c, zl, rank = place.c, place.zl, place.zl
    ready = place.greet()
    for number in range(8):
        for q in range(3):
            t = READY[8 * q + number]
            source = wq[:, t * 128:(t + 1) * 128] if t < 18 else wo[:, (t - 18) * 128:(t - 17) * 128]
            to_peer[0, number, 0:6, q * 128:(q + 1) * 128] = source.astype(F32)
        to_peer[1, number, 0:6, :] = wu[:, number * 384:(number + 1) * 384].astype(F32)
    left, right = wd[:, 0:384].astype(F32), wd[:, 384:768].astype(F32)
    down_s[...] = jnp.where(zl == 0, right, left)
    down[pl.ds(pl.multiple_of(zl * 24, 8), 24), :] = jnp.where(zl == 0, left, right)
    few[...] = jnp.zeros_like(few)
    few[0:1, 0:6] = ga[...].astype(F32)
    few[0:1, 6:12] = gf[...].astype(F32)
    for j in range(3):
        few[0:1, 12 + 18 * j:30 + 18 * j] = taps[j:j + 1, :].astype(F32)
    few[...] = jnp.broadcast_to(few[0:1, :], (8, 128))
    vectors = gather_vectors(place, few, tiles, few_landed, vec)
    advance(vectors)
    ready()

    other = place.device(z=place.flip(place.z, 1))
    trades, trade_down, token_slot, back_slot = place.slot(2), place.slot(), place.slot(), place.slot()
    out_trades, out_down = [place.outbox(from_peer.at[0, 0:7]) for _ in range(2)], place.outbox(down_s)
    out_tokens = place.outbox()
    _, mine = place.member(0)
    def trade(k):
        for d in range(1, 8):
            device, number = place.member(d)
            place.send(to_peer.at[k, number], from_peer.at[k, mine], device, out_trades[k], trades + k)

    def send_tokens(k):
        piece = pl.ds(64 * k, 64)

        @pl.when(zl == 0)
        def _():
            place.send(tok.at[piece], prev.at[piece], other, out_tokens, token_slot)

    trade(0)
    trade(1)
    place.send(down_s, down.at[pl.ds(pl.multiple_of(zl * 24, 8), 24)], other, out_down, trade_down)
    next(vectors)

    for k in range(2):
        from_peer[k, mine] = to_peer[k, mine]

    def normalize_half(half):
        return normalize((prev if half == 0 else tok)[...].astype(F32))

    send_tokens(0)
    place.arrive(down_s, trade_down)
    at = (c, lax.div(place.z, 2), zl, place.y, lax.div(place.x, 2), lax.rem(place.x, 2))
    for k in range(2):
        place.arrive(from_peer.at[k, 0:7], trades + k)
        for number in range(8):
            pile[k, 6 * number:6 * number + 8, :] = from_peer[k, number]
        w[(k,) + at] = pile[k, 0:48, :].astype(BF16)
    w[(2,) + at] = down[...].astype(BF16)
    phase = [gather_phase(place, w, part, LEAN_IN[part]) for part in range(3)]
    advance(vectors)
    for k in range(3):
        advance(*phase)
        send_tokens(k + 1)
        advance(vectors)

    advance(*phase)

    @pl.when(zl == 1)
    def _():
        place.arrive(prev, token_slot)

    @pl.when(zl == 0)
    def _():
        prev[...] = jnp.zeros_like(prev)

    gain_one = jnp.concatenate([vec[r:r + 1, :] for r in range(6)], axis=1)
    gain_two = jnp.concatenate([vec[r:r + 1, :] for r in range(6, 12)], axis=1)
    for half in range(2):
        h1[half * ROWS:(half + 1) * ROWS, :] = (normalize_half(half)[0] * gain_one).astype(BF16)
    h1t[...] = h1[...].T
    row = lax.broadcasted_iota(jnp.int32, (ROWS, EXT), 0)
    column = lax.broadcasted_iota(jnp.int32, (ROWS, EXT), 1)
    behind = jnp.where(column < ROWS, (1 - rank) * EXT, column - ROWS)
    bias[...] = jnp.where(behind <= row, 0.0, -1e30)
    first = lax.broadcasted_iota(jnp.int32, (ROWS, 128), 1) < 64
    gvec[0] = jnp.zeros((VEC, 128), F32)
    advance(phase[0], phase[0])

    def tap(j, t):
        return vec[pl.ds(12 + TILES * j + t, 1), :]

    for jp in range(3):
        block = nn(h1[...], tiles_of(w, range(6 * jp, 6 * jp + 6))).astype(BF16)
        for k in range(6):
            t = 6 * jp + k
            tile = block[:, 128 * k:128 * (k + 1)]
            raw[t] = tile
            value = tile.astype(F32)
            conv = tap(0, t) * value + tap(1, t) * shifted(value, 1) + tap(2, t) * shifted(value, 2)
            mixed[t] = conv.astype(BF16)

    def both(value):
        zero = jnp.zeros_like(value)
        return jnp.concatenate([jnp.where(first, value, zero), jnp.where(first, zero, value)], axis=0)

    def pick(value):
        return jnp.where(first, value[:ROWS], value[ROWS:])

    def attend(p):
        query = both(mixed[p, ROWS:, :])
        key, value = mixed[PAIRS + p], mixed[2 * PAIRS + p]
        scores = nt(query, key) * 0.125 + jnp.concatenate([bias[...], bias[...]], axis=0)
        weights = jnp.exp(scores - jnp.max(scores, axis=-1, keepdims=True))
        exact = weights * (1.0 / jnp.sum(weights, axis=-1, keepdims=True))
        probs[p] = exact
        att[p] = pick(nn(exact.astype(BF16), value)).astype(BF16)

    advance(phase[1])
    for p in range(PAIRS):
        attend(p)
        if p == 0:
            advance(phase[2])

    attended = jnp.concatenate([att[p] for p in range(PAIRS)], axis=1)
    resid = tok[...].astype(F32) + nn(attended, tiles_of(w, range(18, 24)))
    normed_two, inverse_two = normalize(resid)
    h2[...] = (normed_two * gain_two).astype(BF16)
    h2t[...] = h2[...].T
    acc[...] = resid
    advance(phase[1], phase[1], phase[1])

    @pl.loop(0, 4)
    def _(jp):
        rect = jnp.maximum(nn(h2[...], columns(w, 1, jp)), 0.0)
        act[jp] = (rect * rect).astype(BF16)
        gup[jp] = rect.astype(BF16)

    for _ in range(6):
        advance(phase[2])
    place.drain()

    @pl.when(zl == 0)
    def _():
        place.copy(tok, tok, other, out_tokens, 0).wait_send()

    sibling = place.device(c=1 - c)
    across = [place.slot(3), place.slot(2), place.slot(4)]
    out_across = [place.outbox(w.at[part, 0]) for part in range(3)]
    every = slice(None)

    @pl.loop(0, 4)
    def _(jp):
        low = rows(w, jp)
        gup[jp] = (nt(cot[...], low) * 2.0 * gup[jp].astype(F32)).astype(BF16)
        acc[...] += nn(act[jp], low)
        put_rows(w, jp, tn(act[jp], cot[...]))
        some = (lax.div(jp, 2), slice(None), pl.ds(lax.rem(jp, 2) * 2, 2))
        place.send(w.at[(2, 1 - c) + some], from_core.at[(2,) + some], sibling, out_across[2], across[2] + jp)

    gh2[...] = jnp.zeros_like(gh2)

    def widen(jp):
        gh2[...] += nt(gup[jp], columns(w, 1, jp))
        put_columns(w, 1, jp, nn(h2t[...], gup[jp]))

        @pl.when(lax.rem(jp, 2) == 1 - c)
        def _():
            xl = lax.div(jp, 2)
            src, dst = w.at[1, 1 - c, :, :, :, :, xl], from_core.at[1, :, :, :, :, xl]
            place.send(src, dst, sibling, out_across[1], across[1] + xl)

    strips = [strip(sub) for sub in range(3)]

    def finish(part):
        def store(sub, total):
            sums[part, 16 * sub:16 * sub + 16, :] = total
        return store

    def finish_chunk(first, width):
        def store(sub, total):
            sums[0, 16 * sub:16 * sub + 16, first:first + width] = total
        return store

    def land(k):
        return [lands[12 * k + 4 * sub:12 * k + 4 * sub + 4] for sub in range(3)]

    def cross(k):
        cut = (1 - c,) + (every,) * 6 + (pl.ds(*CHUNKS[k]),)
        place.send(g0.at[cut], from_core.at[(0,) + cut[1:]], sibling, out_across[0], across[0] + k)

    up_ready = [((every,) * 4 + (xl,), across[1] + xl) for xl in range(2)]
    down_ready = [((jp // 2, every, pl.ds(jp % 2 * 2, 2)), across[2] + jp) for jp in range(4)]
    ups = scatter_phase(place, w, (1,), strips, up_ready, from_core.at[1], land(2), finish(1), True, LEAN_OUT[1])
    downs = scatter_phase(place, w, (2,), strips, down_ready, from_core.at[2], land(3), finish(2), True, LEAN_OUT[2])
    chunks = []
    for k, (start, width) in enumerate(CHUNKS):
        cut = (pl.ds(start, width),)
        came = [((every,) * 6 + cut, across[0] + k)]
        tails = [(pl.ds(16 * sub, 16),) + cut for sub in range(3)]
        chunks.append(scatter_phase(place, g0, (), tails, came, from_core.at[0], land(k), finish_chunk(start, width), k == 0, LEAN_OUT[0]))
    pl.loop(0, 2)(widen)
    advance(downs)
    pl.loop(2, 4)(widen)
    out[...] = acc[...].astype(BF16)
    grad_two = gh2[...]
    summed = jnp.sum(grad_two * normed_two, axis=0, keepdims=True)
    for r in range(6):
        gvec[0, 6 + r:7 + r, :] = summed[:, 128 * r:128 * (r + 1)]
    grad_resid = cot[...].astype(F32) + norm_back(grad_two * gain_two, normed_two, inverse_two)
    acc[...] = grad_resid
    gproj = grad_resid.astype(BF16)
    gback = nt(gproj, tiles_of(w, range(18, 24))).astype(BF16)
    for p in range(PAIRS):
        gatt[p] = gback[:, 128 * p:128 * (p + 1)]
    put_tiles(g0, range(18, 24), tn(attended, gproj))

    def attend_back(p):
        query = both(mixed[p, ROWS:, :])
        key, value = mixed[PAIRS + p], mixed[2 * PAIRS + p]
        grad = both(gatt[p])
        exact = probs[p]
        gvalue = tn(exact.astype(BF16), grad)
        gprobs = nt(grad, value)
        centred = gprobs - jnp.sum(gprobs * exact, axis=-1, keepdims=True)
        gscores = (exact * centred).astype(BF16)
        gquery = pick(nn(gscores, key)) * 0.125
        gkey = tn(gscores, query) * 0.125
        for k, tile in enumerate((jnp.concatenate([jnp.zeros_like(gquery), gquery], axis=0), gkey, gvalue)):
            t = PAIRS * k + p
            back = tap(0, t) * tile + tap(1, t) * shifted(tile, -1) + tap(2, t) * shifted(tile, -2)
            mixed[t] = back.astype(BF16)
            value_in = raw[t].astype(F32)
            for j in range(3):
                delayed = value_in if j == 0 else shifted(value_in, j)
                gvec[0, pl.ds(12 + TILES * j + t, 1), :] = jnp.sum(tile * delayed, axis=0, keepdims=True)

    def weigh(wanted):
        put_tiles(g0, wanted, nn(h1t[...], jnp.concatenate([mixed[t] for t in wanted], axis=1)))

    attend_back(0)
    advance(ups)
    attend_back(1)
    attend_back(2)
    attend_back(3)
    weigh(READY[6:16])
    cross(0)
    advance(downs)
    attend_back(4)
    attend_back(5)
    advance(chunks[0])
    weigh(READY[16:24])
    cross(1)
    out_back = place.outbox()

    def through_norm(half):
        here = pl.ds(half * ROWS, ROWS)
        grad_one = jnp.zeros((ROWS, D), F32)
        for jp in range(3):
            grad = jnp.concatenate([mixed[6 * jp + k, here, :] for k in range(6)], axis=1)
            grad_one = grad_one + nt(grad, tiles_of(w, range(6 * jp, 6 * jp + 6)))
        normed, inverse = normalize_half(half)
        return jnp.sum(grad_one * normed, axis=0, keepdims=True), norm_back(grad_one * gain_one, normed, inverse)

    def send_back(k):
        piece = pl.ds(64 * k, 64)

        @pl.when(zl == 1)
        def _():
            place.send(contrib.at[piece], got.at[piece], other, out_back, back_slot)

    advance(ups)
    total, back = through_norm(0)
    contrib[...] = back.astype(BF16)
    send_back(0)
    gain, back = through_norm(1)
    acc[...] += back
    total = total + gain
    for r in range(6):
        gvec[0, r:r + 1, :] = total[:, 128 * r:128 * (r + 1)]
    small = sum_vectors(place, gvec, incoming)
    advance(small)
    advance(chunks[1])
    advance(small)
    send_back(1)
    advance(chunks[0], downs, ups, chunks[1])
    advance(small)
    send_back(2)
    advance(chunks[0], downs, ups, chunks[1])
    advance(small)
    send_back(3)
    advance(chunks[0], downs, ups)

    trades, trade_down = place.slot(2), place.slot()
    back_from, arrived = pile.at[0, pl.ds(0, 24)], from_peer
    out_trades, out_down = [place.outbox(from_peer.at[0, 0:7]) for _ in range(2)], place.outbox(back_from)

    def hand_back(k):
        for number in range(8):
            to_peer[k, number, 0:6, :] = sums[k, 6 * number:6 * number + 6, :]
        for d in range(1, 8):
            device, number = place.member(d)
            place.send(to_peer.at[k, number], arrived.at[k, mine], device, out_trades[k], trades + k)
        arrived[k, mine] = to_peer[k, mine]

    hand_back(1)
    place.send(sums.at[2, pl.ds(pl.multiple_of((1 - zl) * 24, 8), 24)], back_from, other, out_down, trade_down)
    advance(chunks[1], chunks[0])
    hand_back(0)
    advance(small, small)
    summed = gvec[4]
    gains = [jnp.concatenate([summed[r:r + 1] for r in range(6 * k, 6 * k + 6)], axis=1) for k in range(2)]
    tapped = [jnp.concatenate([summed[r:r + 1] for r in range(12 + TILES * j, 12 + TILES * j + TILES)], axis=1) for j in range(3)]
    gain_rows = jnp.concatenate(gains + [jnp.zeros((6, D), F32)], axis=0)
    tap_rows = jnp.concatenate(tapped + [jnp.zeros((5, 3 * D), F32)], axis=0)
    exactly = functools.partial(
        lax.dot_general,
        dimension_numbers=(((1,), (1,)), ((), ())),
        preferred_element_type=F32,
        precision=lax.Precision.HIGHEST,
    )
    gain_own = exactly(gain_rows, spread(place.index, 6, D))
    gga[...] = gain_own[0:1, 0:6]
    ggf[...] = gain_own[1:2, 0:6]
    gtap[...] = exactly(tap_rows, spread(place.index, 18, 3 * D))[0:3, 0:18]

    @pl.when(zl == 0)
    def _():
        place.arrive(got, back_slot)

    @pl.when(zl == 1)
    def _():
        got[...] = jnp.zeros_like(got)

    gtok[...] = (acc[...] + got[...].astype(F32)).astype(BF16)
    for k in range(2):
        place.arrive(arrived.at[k, 0:7], trades + k)
    place.arrive(back_from, trade_down)
    for number in range(8):
        for q in range(3):
            t = READY[8 * q + number]
            tile = arrived[0, number, 0:6, 128 * q:128 * (q + 1)]
            if t < 18:
                gq[:, 128 * t:128 * (t + 1)] = tile
            else:
                go[:, 128 * (t - 18):128 * (t - 17)] = tile
        gu[:, 384 * number:384 * (number + 1)] = arrived[1, number, 0:6, :]
    own = sums[2, pl.ds(pl.multiple_of(zl * 24, 8), 24), :]
    theirs = pile[0, 0:24, :]
    gd[:, 0:384] = jnp.where(zl == 0, own, theirs)
    gd[:, 384:768] = jnp.where(zl == 0, theirs, own)
    place.drain()

    @pl.when(zl == 1)
    def _():
        place.copy(contrib, contrib, other, out_back, 0).wait_send()


def kept(axes):
    grid = []
    for axis in "zyx":
        if axis not in axes:
            grid += {"z": [2, 2], "y": [4], "x": [2, 2]}[axis]
    return tuple(grid)


RESULTS = (
    ((ROWS, D), BF16),
    ((ROWS, D), BF16),
    ((6, 2304), F32),
    ((6, 768), F32),
    ((6, 3072), F32),
    ((24, 768), F32),
    ((1, 6), F32),
    ((1, 6), F32),
    ((3, 18), F32),
)


def layer(*args):
    vmem = pl.BlockSpec(memory_space=pltpu.VMEM)
    lands = []
    for k in range(4):
        for sub in range(3):
            order = BACK[sub]
            grids = [(2,) + HALVES[order[0]], (2,) + kept(order[:1]), (3,) + kept(order[:2]), (3,)]
            if k == 1:
                grids[:2] = [(1,), (3,) + kept(order[:1])]
            lands += [pltpu.VMEM(grid + (16, CHUNKS[k][1] if k < 2 else 384), BF16) for grid in grids]
    return pl.pallas_call(
        layer_kernel,
        out_shape=tuple(jax.ShapeDtypeStruct(*result) for result in RESULTS),
        in_specs=[vmem] * 9,
        out_specs=(vmem,) * 9,
        scratch_shapes=[
            pltpu.VMEM((3,) + GRID + BLOCK, BF16),
            pltpu.VMEM(GRID + BLOCK, BF16),
            pltpu.VMEM((D, EXT), BF16),
            pltpu.VMEM((D, ROWS), BF16),
            pltpu.VMEM((3,) + GRID[1:] + BLOCK, BF16),
            pltpu.VMEM((2, 8, 8, 384), F32),
            pltpu.VMEM((2, 8, 8, 384), F32),
            pltpu.VMEM((2, 56, 384), F32),
            pltpu.VMEM((24, 384), F32),
            pltpu.VMEM((48, 384), F32),
            pltpu.VMEM((8, 128), F32),
            pltpu.VMEM((4, 4, 8, 128), F32),
            pltpu.VMEM((8, 8, 128), F32),
            pltpu.VMEM((VEC, 128), F32),
            pltpu.VMEM((ROWS, D), BF16),
            pltpu.VMEM((EXT, D), BF16),
            pltpu.VMEM((TILES, EXT, 128), BF16),
            pltpu.VMEM((TILES, EXT, 128), BF16),
            pltpu.VMEM((ROWS, EXT), F32),
            pltpu.VMEM((PAIRS, EXT, EXT), F32),
            pltpu.VMEM((PAIRS, ROWS, 128), BF16),
            pltpu.VMEM((ROWS, D), BF16),
            pltpu.VMEM((4, ROWS, D), BF16),
            pltpu.VMEM((4, ROWS, D), BF16),
            pltpu.VMEM((ROWS, D), F32),
            pltpu.VMEM((PAIRS, ROWS, 128), BF16),
            pltpu.VMEM((ROWS, D), F32),
            pltpu.VMEM((ROWS, D), BF16),
            pltpu.VMEM((ROWS, D), BF16),
            pltpu.VMEM((5, VEC, 128), F32),
            pltpu.VMEM((4, 3, VEC, 128), F32),
            pltpu.VMEM((3,) + BLOCK, F32),
            *lands,
            pltpu.SemaphoreType.DMA((64,)),
            pltpu.SemaphoreType.DMA((120,)),
        ],
        compiler_params=pltpu.CompilerParams(collective_id=0, has_side_effects=True, vmem_limit_bytes=LIMIT),
    )(*args)


def copy_kernel(*refs):
    for source, target in zip(refs[:len(RESULTS)], refs[len(RESULTS):]):
        target[...] = source[...]


def copied(*args):
    vmem = pl.BlockSpec(memory_space=pltpu.VMEM)
    return pl.pallas_call(
        copy_kernel,
        out_shape=tuple(jax.ShapeDtypeStruct(*result) for result in RESULTS),
        in_specs=[vmem] * len(RESULTS),
        out_specs=(vmem,) * len(RESULTS),
    )(*args)


def per_device(tokens, w_qkv, w_out, w_up, w_down, gain_attn, gain_ffn, conv_taps, cotangent):
    results = copied(*layer(
        tokens, cotangent, w_qkv, w_out, w_up, w_down, gain_attn.reshape(1, 6), gain_ffn.reshape(1, 6), conv_taps
    ))
    return results[:6] + (results[6].reshape(6), results[7].reshape(6), results[8])


def solution(mesh):
    both = ("grp", "seq")
    row, one, column = P(both, None), P(both), P(None, both)
    return jax.shard_map(
        per_device,
        mesh=mesh,
        in_specs=(row, row, row, row, row, one, one, column, row),
        out_specs=(row, row, row, row, row, row, one, one, column),
        check_vma=False,
    )
```

```python
import functools

import jax
import jax.numpy as jnp
from jax import lax
from jax.experimental import pallas as pl
from jax.experimental.pallas import tpu as pltpu
from jax.sharding import PartitionSpec as P

MESH = pl.DeviceIdType.MESH
F32 = jnp.float32
BF16 = jnp.bfloat16
EPS = 1e-05
D = 768
ROWS = 256
EXT = 512
PAIRS = 6
TILES = 18
BLOCK = (48, 384)
GRID = (2, 2, 2, 4, 2, 2)
VEC = 80
ORDERS = (("x", "y", "z"), ("y", "z", "x"), ("z", "x", "y"))
BACK = (("z", "y", "x"), ("x", "z", "y"), ("y", "x", "z"))
LIMIT = 60 * 2**20
READY = tuple(range(18, 24)) + tuple(t for p in range(6) for t in (p, 6 + p, 12 + p))
CHUNKS = ((0, 256), (256, 128))

LEAN_IN = (False, True, True)
LEAN_OUT = (True, True, True)


class Place:
    def __init__(self, send_sem, recv_sem):
        grp, seq = lax.axis_index("grp"), lax.axis_index("seq")
        self.c = lax.rem(grp, 2)
        self.x = lax.rem(lax.div(grp, 2), 4)
        self.y = lax.rem(lax.div(grp, 8), 4)
        self.z = lax.div(grp, 32) * 2 + seq
        self.zl = seq
        self.index = grp * 2 + seq
        self.send_sem, self.recv_sem = send_sem, recv_sem
        self.sends = self.receives = 0
        self.owed = []

    def device(self, **new):
        at = {"x": self.x, "y": self.y, "z": self.z, "c": self.c}
        at.update(new)
        grp = ((lax.div(at["z"], 2) * 4 + at["y"]) * 4 + at["x"]) * 2 + at["c"]
        return (grp, lax.rem(at["z"], 2))

    def along(self, axis, delta):
        return lax.rem(getattr(self, axis) + delta, 4)

    def flip(self, value, bit):
        return value + bit * (1 - 2 * lax.rem(value, 2))

    def member(self, d):
        x, c, z = self.flip(self.x, d // 4), self.flip(self.c, (d // 2) % 2), self.flip(self.z, d % 2)
        number = lax.rem(x, 2) * 4 + c * 2 + lax.rem(z, 2)
        return self.device(x=x, c=c, z=z), number

    def greet(self):
        barrier = pltpu.get_barrier_semaphore()
        partners = [self.device(**{a: self.along(a, d)}) for a in "xyz" for d in (1, 2, 3)]
        partners += [self.member(d)[0] for d in (2, 3, 5, 6, 7)]
        for partner in partners:
            pl.semaphore_signal(barrier, inc=1, device_id=partner, device_id_type=MESH)
        return lambda: pl.semaphore_wait(barrier, len(partners))

    def slot(self, count=1):
        self.receives += count
        return self.receives - count

    def outbox(self, *wholes):
        self.sends += 1
        self.owed.append((self.sends - 1, wholes))
        return self.sends - 1

    def copy(self, src, dst, device, out, slot):
        return pltpu.make_async_remote_copy(
            src_ref=src,
            dst_ref=dst,
            send_sem=self.send_sem.at[out],
            recv_sem=self.recv_sem.at[slot],
            device_id=device,
            device_id_type=MESH,
        )

    def send(self, src, dst, device, out, slot):
        self.copy(src, dst, device, out, slot).start()

    def arrive(self, whole, slot):
        self.copy(whole, whole, self.device(), 0, slot).wait_recv()

    def drain(self):
        for out, wholes in self.owed:
            for whole in wholes:
                self.copy(whole, whole, self.device(), out, 0).wait_send()
        self.owed = []


def spot(lead, c=None, tail=(), **at):
    index = list(lead) + [slice(None) if c is None else c]
    for axis in "zyx":
        value = at.get(axis)
        half = isinstance(value, tuple)
        if axis == "y":
            index.append(pl.ds(2 * value[1], 2) if half else slice(None) if value is None else value)
        elif half:
            index += [value[1], slice(None)]
        elif value is None:
            index += [slice(None), slice(None)]
        else:
            index += [lax.div(value, 2), lax.rem(value, 2)]
    return tuple(index) + tail


def strip(sub):
    return (pl.ds(16 * sub, 16), slice(None))


def spread(index, count, width):
    row = lax.broadcasted_iota(jnp.int32, (128, width), 0)
    column = lax.broadcasted_iota(jnp.int32, (128, width), 1)
    return jnp.where((column == count * index + row) & (row < count), 1.0, 0.0)


def gather_phase(place, w, part, lean):
    c = place.c
    here = {"x": place.x, "y": place.y, "z": place.z}
    sibling = place.device(c=1 - c)
    blocks = {3: w.at[part, 0, 0, 0, 0:3, 0, 0], 12: w.at[part, 0, 0, 0, 0:3], 16: w.at[part, 0, 0, 0], 48: w.at[part, 0, :, :, 0:3], 64: w.at[part, 0]}
    passing, passed = place.outbox(blocks[64]), place.slot()

    def piece(sub, **at):
        return w.at[spot((part,), c, strip(sub), **at)]

    def pass_on(sub, **at):
        place.send(piece(sub, **at), piece(sub, **at), sibling, passing, passed)

    for stage, count in ((0, 3), (1, 12)):
        out, slot = place.outbox(blocks[count]), place.slot()
        for sub in range(3):
            axis, done = ORDERS[sub][stage], ORDERS[sub][:stage]
            own = piece(sub, **{a: here[a] for a in "xyz" if a not in done})
            for step in (1, 2, 3):
                place.send(own, own, place.device(**{axis: place.along(axis, step)}), out, slot)
        yield
        place.arrive(blocks[count], slot)
    out, sides, last = place.outbox(blocks[48]), place.slot(6), place.slot()

    def toward(axis, side):
        return place.device(**{axis: place.along(axis, 3 if side else 1)})

    for sub in range(3):
        axis = ORDERS[sub][2]
        own = piece(sub, **{axis: here[axis]})
        for side in range(2):
            place.send(own, own, toward(axis, side), out, sides + 2 * sub + side)
    for sub in range(3):
        axis = ORDERS[sub][2]
        pass_on(sub, **{axis: here[axis]})
    yield
    for side in range(2):
        for sub in range(3):
            axis, whole = ORDERS[sub][2], ORDERS[sub][0]
            came = {axis: place.along(axis, 1 if side else 3)}
            place.arrive(piece(sub, **came), sides + 2 * sub + side)
            down_only = lean and axis == "z"
            if not down_only or side == 1:
                half = piece(sub, **came) if down_only else piece(sub, **came, **{whole: ("half", side)})
                place.send(half, half, toward(axis, side), out, last)
            pass_on(sub, **came)
    yield
    place.arrive(blocks[16], last)
    for sub in range(3):
        axis = ORDERS[sub][2]
        pass_on(sub, **{axis: place.along(axis, 2)})
    yield
    place.arrive(blocks[64], passed)


HALF = {"z": "y", "x": "z", "y": "x"}
HALVES = {"z": (2, 2, 2), "x": (2, 4), "y": (2, 2, 2)}


def half_of(axis, h):
    return {"z": (pl.ds(2 * h, 2),), "x": (h,), "y": (slice(None), slice(None), h)}[axis]


def scatter_phase(place, g, lead, tails, arrivals, landed, lands, finish, relayed, lean):
    c = place.c
    here = {"x": place.x, "y": place.y, "z": place.z}
    tail = (slice(None), tails[0][1])
    corner = lead + (0, 0, 0)
    blocks = {
        3: g.at[corner + (pl.ds(0, 3), 0, 0) + tail],
        12: g.at[corner + (pl.ds(0, 3), slice(None), slice(None)) + tail],
        48: g.at[lead + (0, slice(None), slice(None), pl.ds(0, 3), slice(None), slice(None)) + tail],
    }

    def at(sub, **where):
        return spot(lead, c, tails[sub], **where)

    for index, slot in arrivals:
        place.arrive(landed.at[index], slot)
        g[lead + (c,) + index] = g[lead + (c,) + index] + landed[index]
    out = place.outbox(blocks[48])

    def ways(sub):
        axis = BACK[sub][0]
        way = [(t, place.device(**{axis: t})) for t in (place.along(axis, 1), place.along(axis, 3))]
        return axis, HALF[axis], way, (0, 0) if lean and axis == "z" else (0, 1)

    if relayed:
        relays, sides = place.slot(6), place.slot(3)
        for sub in range(3):
            axis, whole, way, course = ways(sub)
            across = place.along(axis, 2)
            for k in range(2):
                src = g.at[at(sub, **{axis: across, whole: ("half", k)})]
                place.send(src, lands[sub][0].at[k], way[course[k]][1], out, relays + 2 * sub + k)
        for sub in range(3):
            axis, whole, way, course = ways(sub)
            for k in range(2):
                toward = 1 - course[k]
                coordinate, device = way[toward]
                src = g.at[at(sub, **{axis: coordinate, whole: ("half", k)})]
                place.send(src, lands[sub][1].at[(toward,) + half_of(axis, k)], device, out, sides + sub)
        yield
        for sub in range(3):
            axis, whole, way, course = ways(sub)
            relay, side = lands[sub][:2]
            for k in range(2):
                coordinate, device = way[course[k]]
                place.arrive(relay.at[k], relays + 2 * sub + k)
                index = at(sub, **{axis: coordinate, whole: ("half", k)})
                g[index] = g[index] + relay[k]
                place.send(g.at[index], side.at[(course[k],) + half_of(axis, k)], device, out, sides + sub)
        yield
    else:
        sides = place.slot(3)
        for step in (2, 1, 3):
            for sub in range(3):
                axis = BACK[sub][0]
                there = place.along(axis, step)
                src = g.at[at(sub, **{axis: there})]
                place.send(src, lands[sub][1].at[step - 1], place.device(**{axis: there}), out, sides + sub)
        yield
    out, slot = place.outbox(blocks[12]), place.slot()
    for sub in range(3):
        axis, second = BACK[sub][0], BACK[sub][1]
        side = lands[sub][1]
        place.arrive(side, sides + sub)
        index = at(sub, **{axis: here[axis]})
        total = g[index].astype(F32)
        for k in range(side.shape[0]):
            total = total + side[k].astype(F32)
        g[index] = total.astype(BF16)
        for step in (1, 2, 3):
            there = place.along(second, step)
            src = g.at[at(sub, **{axis: here[axis], second: there})]
            place.send(src, lands[sub][2].at[step - 1], place.device(**{second: there}), out, slot)
    yield
    place.arrive(blocks[12], slot)
    out, slot = place.outbox(blocks[3]), place.slot()
    for sub in range(3):
        own = {a: here[a] for a in BACK[sub][:2]}
        third = BACK[sub][2]
        index = at(sub, **own)
        total = g[index].astype(F32)
        for step in range(3):
            total = total + lands[sub][2][step].astype(F32)
        g[index] = total.astype(BF16)
        for step in (1, 2, 3):
            there = place.along(third, step)
            src = g.at[at(sub, **own, **{third: there})]
            place.send(src, lands[sub][3].at[step - 1], place.device(**{third: there}), out, slot)
    yield
    place.arrive(blocks[3], slot)
    for sub in range(3):
        total = g[at(sub, **here)].astype(F32)
        for step in range(3):
            total = total + lands[sub][3][step].astype(F32)
        finish(sub, total)


def advance(*steps):
    for step in steps:
        next(step, None)


def remainder(value, count):
    value = value.astype(F32)
    whole = jnp.floor((value + 0.5) * (1.0 / count))
    return value - whole * count, whole


def gather_vectors(place, few, tiles, landed, vec):
    sublane = lax.broadcasted_iota(jnp.int32, (8, 128), 0)
    mine = place.c * 4 + place.x
    landed[3] = jnp.where(sublane == mine, few[...], 0.0)
    yield
    out, slot = place.outbox(landed.at[0:3]), place.slot()
    for step in (1, 2, 3):
        place.send(landed.at[3], landed.at[step - 1], place.device(x=place.along("x", step)), out, slot)
    yield
    place.arrive(landed.at[0:3], slot)
    landed[4] = landed[0] + landed[1] + landed[2] + landed[3]
    out, slot = place.outbox(landed.at[4]), place.slot()
    place.send(landed.at[4], landed.at[5], place.device(c=1 - place.c), out, slot)
    yield
    place.arrive(landed.at[5], slot)
    tiles[place.z, place.y] = landed[4] + landed[5]
    here = tiles.at[place.z, place.y]
    out, slot = place.outbox(landed.at[0:3]), place.slot()
    for step in (1, 2, 3):
        place.send(here, here, place.device(y=place.along("y", step)), out, slot)
    yield
    place.arrive(landed.at[0:3], slot)
    out, slot = place.outbox(tiles.at[0:3]), place.slot()
    for step in (1, 2, 3):
        place.send(tiles.at[place.z], tiles.at[place.z], place.device(z=place.along("z", step)), out, slot)
    yield
    place.arrive(tiles.at[0:3], slot)
    table = tiles[...].reshape(128, 128).astype(BF16)
    row = lax.broadcasted_iota(jnp.int32, (128, 1), 0)
    z, y, core, x = row // 32, (row // 8) % 4, (row // 4) % 2, row % 4
    device = ((z // 2) * 64 + y * 16 + x * 4 + core * 2 + z % 2).astype(F32)
    for count, width, firsts in ((6, D, (0, 6)), (18, 3 * D, (12, 30, 48))):
        part, owner = remainder(lax.broadcasted_iota(jnp.int32, (1, width), 1), count)
        lane = lax.broadcasted_iota(jnp.int32, (128, 1), 0).astype(F32)
        for first in firsts:
            choose = jnp.where(lane - first == part, 1.0, 0.0).astype(BF16)
            spread_out = nn(table, choose)
            vector = jnp.sum(jnp.where(device == owner, spread_out, 0.0), axis=0, keepdims=True)
            base = first if count == 6 else first
            for k in range(width // 128):
                vec[base + k:base + k + 1, :] = vector[:, 128 * k:128 * (k + 1)]


def sum_vectors(place, vec, incoming):
    for stage, axis in enumerate("cxyz"):
        steps = (1,) if axis == "c" else (1, 2, 3)
        whole = incoming.at[stage, 0:len(steps)]
        out, slot = place.outbox(whole), place.slot()
        for k, step in enumerate(steps):
            device = place.device(c=1 - place.c) if axis == "c" else place.device(**{axis: place.along(axis, step)})
            place.send(vec.at[stage], incoming.at[stage, k], device, out, slot)
        yield
        place.arrive(whole, slot)
        total = vec[stage]
        for k in range(len(steps)):
            total = total + incoming[stage, k]
        vec[stage + 1] = total


def nt(left, right):
    return lax.dot_general(left, right, (((1,), (1,)), ((), ())), preferred_element_type=F32)


def tn(left, right):
    return lax.dot_general(left, right, (((0,), (0,)), ((), ())), preferred_element_type=F32)


def nn(left, right):
    return jnp.dot(left, right, preferred_element_type=F32)


def columns(ref, part, jp):
    halves = [ref[part, lax.rem(jp, 2), :, zl, :, :, lax.div(jp, 2)].reshape(D, 384) for zl in range(2)]
    return jnp.concatenate(halves, axis=1)


def tile_at(t):
    j, q = READY.index(t) % 8, READY.index(t) // 8
    xl, c, zl = j // 4, j // 2 % 2, j % 2
    every = slice(None)
    return (c, every, zl, every, every, xl, every, pl.ds(128 * q, 128))


def tiles_of(w, wanted):
    return jnp.concatenate([w[(0,) + tile_at(t)].reshape(D, 128) for t in wanted], axis=1)


def put_tiles(g, wanted, value):
    low = value.astype(BF16)
    for k, t in enumerate(wanted):
        g[(2,) + tile_at(t)] = low[:, 128 * k:128 * (k + 1)].reshape(2, 4, 2, 48, 128)


def put_columns(ref, part, jp, value):
    for zl in range(2):
        ref[part, lax.rem(jp, 2), :, zl, :, :, lax.div(jp, 2)] = (
            value[:, zl * 384:(zl + 1) * 384].astype(BF16).reshape(2, 4, 2, 48, 384)
        )


def row_pieces():
    return [(y, xh, xl, c) for y in range(2) for xh in range(2) for xl in range(2) for c in range(2)]


def rows(ref, jp):
    zh, y0 = lax.div(jp, 2), lax.rem(jp, 2) * 2
    halves = [
        jnp.concatenate([ref[2, c, zh, zl, y0 + y, xh, xl] for y, xh, xl, c in row_pieces()], axis=0) for zl in range(2)
    ]
    return jnp.concatenate(halves, axis=1)


def put_rows(ref, jp, value):
    zh, y0 = lax.div(jp, 2), lax.rem(jp, 2) * 2
    low = value.astype(BF16)
    for zl in range(2):
        for k, (y, xh, xl, c) in enumerate(row_pieces()):
            ref[c, zh, zl, y0 + y, xh, xl] = low[48 * k:48 * k + 48, zl * 384:(zl + 1) * 384]


def normalize(values):
    mean = jnp.mean(values, axis=-1, keepdims=True)
    centred = values - mean
    inverse = lax.rsqrt(jnp.mean(centred * centred, axis=-1, keepdims=True) + EPS)
    return centred * inverse, inverse


def norm_back(grad, normed, inverse):
    first = jnp.mean(grad, axis=-1, keepdims=True)
    second = jnp.mean(grad * normed, axis=-1, keepdims=True)
    return inverse * (grad - first - normed * second)


def shifted(values, steps):
    count = values.shape[0]
    row = lax.broadcasted_iota(jnp.int32, values.shape, 0)
    rolled = pltpu.roll(values, steps % count, 0)
    return jnp.where(row >= steps if steps > 0 else row < count + steps, rolled, 0.0)


def layer_kernel(tok, cot, wq, wo, wu, wd, ga, gf, taps, out, gtok, gq, go, gu, gd, gga, ggf, gtap, *scratch):
    (w, g0, h1t, h2t, from_core, to_peer, from_peer, pile, down_s, down, few, tiles, few_landed, vec, prev, h1, raw, mixed, bias,
     probs, att, h2, act, gup, gh2, gatt, acc, contrib, got, gvec, incoming, sums) = scratch[:32]
    lands, (send_sem, recv_sem) = scratch[32:-2], scratch[-2:]
    place = Place(send_sem, recv_sem)
    c, zl, rank = place.c, place.zl, place.zl
    ready = place.greet()
    for number in range(8):
        for q in range(3):
            t = READY[8 * q + number]
            source = wq[:, t * 128:(t + 1) * 128] if t < 18 else wo[:, (t - 18) * 128:(t - 17) * 128]
            to_peer[0, number, 0:6, q * 128:(q + 1) * 128] = source.astype(F32)
        to_peer[1, number, 0:6, :] = wu[:, number * 384:(number + 1) * 384].astype(F32)
    left, right = wd[:, 0:384].astype(F32), wd[:, 384:768].astype(F32)
    down_s[...] = jnp.where(zl == 0, right, left)
    down[pl.ds(pl.multiple_of(zl * 24, 8), 24), :] = jnp.where(zl == 0, left, right)
    few[...] = jnp.zeros_like(few)
    few[0:1, 0:6] = ga[...].astype(F32)
    few[0:1, 6:12] = gf[...].astype(F32)
    for j in range(3):
        few[0:1, 12 + 18 * j:30 + 18 * j] = taps[j:j + 1, :].astype(F32)
    few[...] = jnp.broadcast_to(few[0:1, :], (8, 128))
    vectors = gather_vectors(place, few, tiles, few_landed, vec)
    advance(vectors)
    ready()

    other = place.device(z=place.flip(place.z, 1))
    trades, trade_down, token_slot, back_slot = place.slot(2), place.slot(), place.slot(), place.slot()
    out_trades, out_down = [place.outbox(from_peer.at[0, 0:7]) for _ in range(2)], place.outbox(down_s)
    out_tokens = place.outbox()
    _, mine = place.member(0)
    def trade(k):
        for d in range(1, 8):
            device, number = place.member(d)
            place.send(to_peer.at[k, number], from_peer.at[k, mine], device, out_trades[k], trades + k)

    def send_tokens(k):
        piece = pl.ds(64 * k, 64)

        @pl.when(zl == 0)
        def _():
            place.send(tok.at[piece], prev.at[piece], other, out_tokens, token_slot)

    trade(0)
    trade(1)
    place.send(down_s, down.at[pl.ds(pl.multiple_of(zl * 24, 8), 24)], other, out_down, trade_down)
    next(vectors)

    for k in range(2):
        from_peer[k, mine] = to_peer[k, mine]

    def normalize_half(half):
        return normalize((prev if half == 0 else tok)[...].astype(F32))

    send_tokens(0)
    place.arrive(down_s, trade_down)
    at = (c, lax.div(place.z, 2), zl, place.y, lax.div(place.x, 2), lax.rem(place.x, 2))
    for k in range(2):
        place.arrive(from_peer.at[k, 0:7], trades + k)
        for number in range(8):
            pile[k, 6 * number:6 * number + 8, :] = from_peer[k, number]
        w[(k,) + at] = pile[k, 0:48, :].astype(BF16)
    w[(2,) + at] = down[...].astype(BF16)
    phase = [gather_phase(place, w, part, LEAN_IN[part]) for part in range(3)]
    advance(vectors)
    for k in range(2):
        advance(*phase)
        send_tokens(k + 1)
        advance(vectors)
    advance(phase[0], phase[1])
    send_tokens(3)
    advance(vectors)

    advance(phase[0], phase[2], phase[1])

    @pl.when(zl == 1)
    def _():
        place.arrive(prev, token_slot)

    @pl.when(zl == 0)
    def _():
        prev[...] = jnp.zeros_like(prev)

    gain_one = jnp.concatenate([vec[r:r + 1, :] for r in range(6)], axis=1)
    gain_two = jnp.concatenate([vec[r:r + 1, :] for r in range(6, 12)], axis=1)
    for half in range(2):
        h1[half * ROWS:(half + 1) * ROWS, :] = (normalize_half(half)[0] * gain_one).astype(BF16)
    h1t[...] = h1[...].T
    row = lax.broadcasted_iota(jnp.int32, (ROWS, EXT), 0)
    column = lax.broadcasted_iota(jnp.int32, (ROWS, EXT), 1)
    behind = jnp.where(column < ROWS, (1 - rank) * EXT, column - ROWS)
    bias[...] = jnp.where(behind <= row, 0.0, -1e30)
    first = lax.broadcasted_iota(jnp.int32, (ROWS, 128), 1) < 64
    gvec[0] = jnp.zeros((VEC, 128), F32)
    advance(phase[0], phase[2], phase[0])

    def tap(j, t):
        return vec[pl.ds(12 + TILES * j + t, 1), :]

    for jp in range(3):
        block = nn(h1[...], tiles_of(w, range(6 * jp, 6 * jp + 6))).astype(BF16)
        for k in range(6):
            t = 6 * jp + k
            tile = block[:, 128 * k:128 * (k + 1)]
            raw[t] = tile
            value = tile.astype(F32)
            conv = tap(0, t) * value + tap(1, t) * shifted(value, 1) + tap(2, t) * shifted(value, 2)
            mixed[t] = conv.astype(BF16)

    def both(value):
        zero = jnp.zeros_like(value)
        return jnp.concatenate([jnp.where(first, value, zero), jnp.where(first, zero, value)], axis=0)

    def pick(value):
        return jnp.where(first, value[:ROWS], value[ROWS:])

    def attend(p):
        query = both(mixed[p, ROWS:, :])
        key, value = mixed[PAIRS + p], mixed[2 * PAIRS + p]
        scores = nt(query, key) * 0.125 + jnp.concatenate([bias[...], bias[...]], axis=0)
        weights = jnp.exp(scores - jnp.max(scores, axis=-1, keepdims=True))
        exact = weights * (1.0 / jnp.sum(weights, axis=-1, keepdims=True))
        probs[p] = exact
        att[p] = pick(nn(exact.astype(BF16), value)).astype(BF16)

    advance(phase[1])
    for p in range(PAIRS):
        attend(p)
        if p == 0:
            advance(phase[2])

    attended = jnp.concatenate([att[p] for p in range(PAIRS)], axis=1)
    resid = tok[...].astype(F32) + nn(attended, tiles_of(w, range(18, 24)))
    normed_two, inverse_two = normalize(resid)
    h2[...] = (normed_two * gain_two).astype(BF16)
    h2t[...] = h2[...].T
    acc[...] = resid
    advance(phase[1], phase[1], phase[1])
    inward, place.owed = place.owed, []
    sibling = place.device(c=1 - c)
    across = [place.slot(3), place.slot(2), place.slot(4)]
    out_across = [place.outbox(w.at[part, 0]) for part in range(3)]
    every = slice(None)
    strips = [strip(sub) for sub in range(3)]

    def finish(part):
        def store(sub, total):
            sums[part, 16 * sub:16 * sub + 16, :] = total
        return store

    def finish_chunk(first, width):
        def store(sub, total):
            sums[0, 16 * sub:16 * sub + 16, first:first + width] = total
        return store

    def land(k):
        return [lands[12 * k + 4 * sub:12 * k + 4 * sub + 4] for sub in range(3)]

    def cross(k):
        cut = (1 - c,) + (every,) * 6 + (pl.ds(*CHUNKS[k]),)
        place.send(w.at[(2,) + cut], from_core.at[(0,) + cut[1:]], sibling, out_across[0], across[0] + k)

    up_ready = [((every,) * 4 + (xl,), across[1] + xl) for xl in range(2)]
    down_ready = [((jp // 2, every, pl.ds(jp % 2 * 2, 2)), across[2] + jp) for jp in range(4)]
    ups = scatter_phase(place, w, (1,), strips, up_ready, from_core.at[1], land(2), finish(1), True, LEAN_OUT[1])
    downs = scatter_phase(place, g0, (), strips, down_ready, from_core.at[2], land(3), finish(2), True, LEAN_OUT[2])
    chunks = []
    for k, (start, width) in enumerate(CHUNKS):
        cut = (pl.ds(start, width),)
        came = [((every,) * 6 + cut, across[0] + k)]
        tails = [(pl.ds(16 * sub, 16),) + cut for sub in range(3)]
        chunks.append(scatter_phase(place, w, (2,), tails, came, from_core.at[0], land(k), finish_chunk(start, width), k == 0, LEAN_OUT[0]))

    @pl.loop(0, 4)
    def _(jp):
        rect = jnp.maximum(nn(h2[...], columns(w, 1, jp)), 0.0)
        act[jp] = (rect * rect).astype(BF16)
        gup[jp] = rect.astype(BF16)
        put_rows(g0, jp, tn(act[jp], cot[...]))
        some = (lax.div(jp, 2), slice(None), pl.ds(lax.rem(jp, 2) * 2, 2))
        place.send(g0.at[(1 - c,) + some], from_core.at[(2,) + some], sibling, out_across[2], across[2] + jp)

    for _ in range(6):
        advance(phase[2])
    place.owed, outward = inward, place.owed
    place.drain()
    place.owed = outward

    @pl.when(zl == 0)
    def _():
        place.copy(tok, tok, other, out_tokens, 0).wait_send()

    def narrow(jp):
        low = rows(w, jp)
        gup[jp] = (nt(cot[...], low) * 2.0 * gup[jp].astype(F32)).astype(BF16)
        acc[...] += nn(act[jp], low)

    pl.loop(0, 2)(narrow)
    advance(downs)
    pl.loop(2, 4)(narrow)
    gh2[...] = jnp.zeros_like(gh2)

    def widen(jp):
        gh2[...] += nt(gup[jp], columns(w, 1, jp))
        put_columns(w, 1, jp, nn(h2t[...], gup[jp]))

        @pl.when(lax.rem(jp, 2) == 1 - c)
        def _():
            xl = lax.div(jp, 2)
            src, dst = w.at[1, 1 - c, :, :, :, :, xl], from_core.at[1, :, :, :, :, xl]
            place.send(src, dst, sibling, out_across[1], across[1] + xl)

    pl.loop(0, 4)(widen)
    out[...] = acc[...].astype(BF16)
    grad_two = gh2[...]
    summed = jnp.sum(grad_two * normed_two, axis=0, keepdims=True)
    for r in range(6):
        gvec[0, 6 + r:7 + r, :] = summed[:, 128 * r:128 * (r + 1)]
    grad_resid = cot[...].astype(F32) + norm_back(grad_two * gain_two, normed_two, inverse_two)
    acc[...] = grad_resid
    gproj = grad_resid.astype(BF16)
    gback = nt(gproj, tiles_of(w, range(18, 24))).astype(BF16)
    for p in range(PAIRS):
        gatt[p] = gback[:, 128 * p:128 * (p + 1)]
    put_tiles(w, range(18, 24), tn(attended, gproj))

    def attend_back(p):
        query = both(mixed[p, ROWS:, :])
        key, value = mixed[PAIRS + p], mixed[2 * PAIRS + p]
        grad = both(gatt[p])
        exact = probs[p]
        gvalue = tn(exact.astype(BF16), grad)
        gprobs = nt(grad, value)
        centred = gprobs - jnp.sum(gprobs * exact, axis=-1, keepdims=True)
        gscores = (exact * centred).astype(BF16)
        gquery = pick(nn(gscores, key)) * 0.125
        gkey = tn(gscores, query) * 0.125
        for k, tile in enumerate((jnp.concatenate([jnp.zeros_like(gquery), gquery], axis=0), gkey, gvalue)):
            t = PAIRS * k + p
            back = tap(0, t) * tile + tap(1, t) * shifted(tile, -1) + tap(2, t) * shifted(tile, -2)
            mixed[t] = back.astype(BF16)
            value_in = raw[t].astype(F32)
            for j in range(3):
                delayed = value_in if j == 0 else shifted(value_in, j)
                gvec[0, pl.ds(12 + TILES * j + t, 1), :] = jnp.sum(tile * delayed, axis=0, keepdims=True)

    def weigh(wanted):
        put_tiles(w, wanted, nn(h1t[...], jnp.concatenate([mixed[t] for t in wanted], axis=1)))

    attend_back(0)
    advance(ups)
    attend_back(1)
    attend_back(2)
    attend_back(3)
    weigh(READY[6:16])
    cross(0)
    advance(downs)
    attend_back(4)
    attend_back(5)
    advance(chunks[0])
    weigh(READY[16:24])
    cross(1)
    out_back = place.outbox()

    def through_norm(half):
        here = pl.ds(half * ROWS, ROWS)
        grad_one = jnp.zeros((ROWS, D), F32)
        for jp in range(3):
            grad = jnp.concatenate([mixed[6 * jp + k, here, :] for k in range(6)], axis=1)
            grad_one = grad_one + nt(grad, tiles_of(w, range(6 * jp, 6 * jp + 6)))
        normed, inverse = normalize_half(half)
        return jnp.sum(grad_one * normed, axis=0, keepdims=True), norm_back(grad_one * gain_one, normed, inverse)

    def send_back(k):
        piece = pl.ds(64 * k, 64)

        @pl.when(zl == 1)
        def _():
            place.send(contrib.at[piece], got.at[piece], other, out_back, back_slot)

    advance(ups)
    total, back = through_norm(0)
    contrib[...] = back.astype(BF16)
    send_back(0)
    gain, back = through_norm(1)
    acc[...] += back
    total = total + gain
    for r in range(6):
        gvec[0, r:r + 1, :] = total[:, 128 * r:128 * (r + 1)]
    small = sum_vectors(place, gvec, incoming)
    advance(small)
    advance(chunks[1])
    advance(small)
    send_back(1)
    advance(chunks[0], downs, ups, chunks[1])
    advance(small)
    send_back(2)
    advance(chunks[0], downs, ups, chunks[1])
    advance(small)
    send_back(3)
    advance(chunks[0], downs, ups)

    trades, trade_down = place.slot(2), place.slot()
    back_from, arrived = pile.at[0, pl.ds(0, 24)], from_peer
    out_trades, out_down = [place.outbox(from_peer.at[0, 0:7]) for _ in range(2)], place.outbox(back_from)

    def hand_back(k):
        for number in range(8):
            to_peer[k, number, 0:6, :] = sums[k, 6 * number:6 * number + 6, :]
        for d in range(1, 8):
            device, number = place.member(d)
            place.send(to_peer.at[k, number], arrived.at[k, mine], device, out_trades[k], trades + k)
        arrived[k, mine] = to_peer[k, mine]

    hand_back(1)
    place.send(sums.at[2, pl.ds(pl.multiple_of((1 - zl) * 24, 8), 24)], back_from, other, out_down, trade_down)
    advance(chunks[1], chunks[0])
    hand_back(0)
    advance(small, small)
    summed = gvec[4]
    gains = [jnp.concatenate([summed[r:r + 1] for r in range(6 * k, 6 * k + 6)], axis=1) for k in range(2)]
    tapped = [jnp.concatenate([summed[r:r + 1] for r in range(12 + TILES * j, 12 + TILES * j + TILES)], axis=1) for j in range(3)]
    gain_rows = jnp.concatenate(gains + [jnp.zeros((6, D), F32)], axis=0)
    tap_rows = jnp.concatenate(tapped + [jnp.zeros((5, 3 * D), F32)], axis=0)
    exactly = functools.partial(
        lax.dot_general,
        dimension_numbers=(((1,), (1,)), ((), ())),
        preferred_element_type=F32,
        precision=lax.Precision.HIGHEST,
    )
    gain_own = exactly(gain_rows, spread(place.index, 6, D))
    gga[...] = gain_own[0:1, 0:6]
    ggf[...] = gain_own[1:2, 0:6]
    gtap[...] = exactly(tap_rows, spread(place.index, 18, 3 * D))[0:3, 0:18]

    @pl.when(zl == 0)
    def _():
        place.arrive(got, back_slot)

    @pl.when(zl == 1)
    def _():
        got[...] = jnp.zeros_like(got)

    gtok[...] = (acc[...] + got[...].astype(F32)).astype(BF16)
    for k in range(2):
        place.arrive(arrived.at[k, 0:7], trades + k)
    place.arrive(back_from, trade_down)
    for number in range(8):
        for q in range(3):
            t = READY[8 * q + number]
            tile = arrived[0, number, 0:6, 128 * q:128 * (q + 1)]
            if t < 18:
                gq[:, 128 * t:128 * (t + 1)] = tile
            else:
                go[:, 128 * (t - 18):128 * (t - 17)] = tile
        gu[:, 384 * number:384 * (number + 1)] = arrived[1, number, 0:6, :]
    own = sums[2, pl.ds(pl.multiple_of(zl * 24, 8), 24), :]
    theirs = pile[0, 0:24, :]
    gd[:, 0:384] = jnp.where(zl == 0, own, theirs)
    gd[:, 384:768] = jnp.where(zl == 0, theirs, own)
    place.drain()

    @pl.when(zl == 1)
    def _():
        place.copy(contrib, contrib, other, out_back, 0).wait_send()


def kept(axes):
    grid = []
    for axis in "zyx":
        if axis not in axes:
            grid += {"z": [2, 2], "y": [4], "x": [2, 2]}[axis]
    return tuple(grid)


RESULTS = (
    ((ROWS, D), BF16),
    ((ROWS, D), BF16),
    ((6, 2304), F32),
    ((6, 768), F32),
    ((6, 3072), F32),
    ((24, 768), F32),
    ((1, 6), F32),
    ((1, 6), F32),
    ((3, 18), F32),
)


def layer(*args):
    vmem = pl.BlockSpec(memory_space=pltpu.VMEM)
    lands = []
    for k in range(4):
        for sub in range(3):
            order = BACK[sub]
            grids = [(2,) + HALVES[order[0]], (2,) + kept(order[:1]), (3,) + kept(order[:2]), (3,)]
            if k == 1:
                grids[:2] = [(1,), (3,) + kept(order[:1])]
            lands += [pltpu.VMEM(grid + (16, CHUNKS[k][1] if k < 2 else 384), BF16) for grid in grids]
    return pl.pallas_call(
        layer_kernel,
        out_shape=tuple(jax.ShapeDtypeStruct(*result) for result in RESULTS),
        in_specs=[vmem] * 9,
        out_specs=(vmem,) * 9,
        scratch_shapes=[
            pltpu.VMEM((3,) + GRID + BLOCK, BF16),
            pltpu.VMEM(GRID + BLOCK, BF16),
            pltpu.VMEM((D, EXT), BF16),
            pltpu.VMEM((D, ROWS), BF16),
            pltpu.VMEM((3,) + GRID[1:] + BLOCK, BF16),
            pltpu.VMEM((2, 8, 8, 384), F32),
            pltpu.VMEM((2, 8, 8, 384), F32),
            pltpu.VMEM((2, 56, 384), F32),
            pltpu.VMEM((24, 384), F32),
            pltpu.VMEM((48, 384), F32),
            pltpu.VMEM((8, 128), F32),
            pltpu.VMEM((4, 4, 8, 128), F32),
            pltpu.VMEM((8, 8, 128), F32),
            pltpu.VMEM((VEC, 128), F32),
            pltpu.VMEM((ROWS, D), BF16),
            pltpu.VMEM((EXT, D), BF16),
            pltpu.VMEM((TILES, EXT, 128), BF16),
            pltpu.VMEM((TILES, EXT, 128), BF16),
            pltpu.VMEM((ROWS, EXT), F32),
            pltpu.VMEM((PAIRS, EXT, EXT), F32),
            pltpu.VMEM((PAIRS, ROWS, 128), BF16),
            pltpu.VMEM((ROWS, D), BF16),
            pltpu.VMEM((4, ROWS, D), BF16),
            pltpu.VMEM((4, ROWS, D), BF16),
            pltpu.VMEM((ROWS, D), F32),
            pltpu.VMEM((PAIRS, ROWS, 128), BF16),
            pltpu.VMEM((ROWS, D), F32),
            pltpu.VMEM((ROWS, D), BF16),
            pltpu.VMEM((ROWS, D), BF16),
            pltpu.VMEM((5, VEC, 128), F32),
            pltpu.VMEM((4, 3, VEC, 128), F32),
            pltpu.VMEM((3,) + BLOCK, F32),
            *lands,
            pltpu.SemaphoreType.DMA((43,)),
            pltpu.SemaphoreType.DMA((93,)),
        ],
        compiler_params=pltpu.CompilerParams(collective_id=0, has_side_effects=True, vmem_limit_bytes=LIMIT),
    )(*args)


def copy_kernel(*refs):
    for source, target in zip(refs[:len(RESULTS)], refs[len(RESULTS):]):
        target[...] = source[...]


def copied(*args):
    vmem = pl.BlockSpec(memory_space=pltpu.VMEM)
    return pl.pallas_call(
        copy_kernel,
        out_shape=tuple(jax.ShapeDtypeStruct(*result) for result in RESULTS),
        in_specs=[vmem] * len(RESULTS),
        out_specs=(vmem,) * len(RESULTS),
    )(*args)


def per_device(tokens, w_qkv, w_out, w_up, w_down, gain_attn, gain_ffn, conv_taps, cotangent):
    results = copied(*layer(
        tokens, cotangent, w_qkv, w_out, w_up, w_down, gain_attn.reshape(1, 6), gain_ffn.reshape(1, 6), conv_taps
    ))
    return results[:6] + (results[6].reshape(6), results[7].reshape(6), results[8])


def solution(mesh):
    both = ("grp", "seq")
    row, one, column = P(both, None), P(both), P(None, both)
    return jax.shard_map(
        per_device,
        mesh=mesh,
        in_specs=(row, row, row, row, row, one, one, column, row),
        out_specs=(row, row, row, row, row, row, one, one, column),
        check_vma=False,
    )
```

```python
import functools

import jax
import jax.numpy as jnp
from jax import lax
from jax.experimental import pallas as pl
from jax.experimental.pallas import tpu as pltpu
from jax.sharding import PartitionSpec as P

MESH = pl.DeviceIdType.MESH
F32 = jnp.float32
BF16 = jnp.bfloat16
EPS = 1e-05
D = 768
ROWS = 256
EXT = 512
PAIRS = 6
TILES = 18
BLOCK = (48, 384)
GRID = (2, 2, 2, 4, 2, 2)
VEC = 80
ORDERS = (("x", "y", "z"), ("y", "z", "x"), ("z", "x", "y"))
BACK = (("z", "y", "x"), ("x", "z", "y"), ("y", "x", "z"))
LIMIT = 60 * 2**20
READY = tuple(range(18, 24)) + tuple(t for p in range(6) for t in (p, 6 + p, 12 + p))
CHUNKS = ((0, 256), (256, 128))

LEAN_IN = (False, True, True)
LEAN_OUT = (True, True, True)


class Place:
    def __init__(self, send_sem, recv_sem):
        grp, seq = lax.axis_index("grp"), lax.axis_index("seq")
        self.c = lax.rem(grp, 2)
        self.x = lax.rem(lax.div(grp, 2), 4)
        self.y = lax.rem(lax.div(grp, 8), 4)
        self.z = lax.div(grp, 32) * 2 + seq
        self.zl = seq
        self.index = grp * 2 + seq
        self.send_sem, self.recv_sem = send_sem, recv_sem
        self.sends = self.receives = 0
        self.owed = []

    def device(self, **new):
        at = {"x": self.x, "y": self.y, "z": self.z, "c": self.c}
        at.update(new)
        grp = ((lax.div(at["z"], 2) * 4 + at["y"]) * 4 + at["x"]) * 2 + at["c"]
        return (grp, lax.rem(at["z"], 2))

    def along(self, axis, delta):
        return lax.rem(getattr(self, axis) + delta, 4)

    def flip(self, value, bit):
        return value + bit * (1 - 2 * lax.rem(value, 2))

    def member(self, d):
        x, c, z = self.flip(self.x, d // 4), self.flip(self.c, (d // 2) % 2), self.flip(self.z, d % 2)
        number = lax.rem(x, 2) * 4 + c * 2 + lax.rem(z, 2)
        return self.device(x=x, c=c, z=z), number

    def greet(self):
        barrier = pltpu.get_barrier_semaphore()
        partners = [self.device(**{a: self.along(a, d)}) for a in "xyz" for d in (1, 2, 3)]
        partners += [self.member(d)[0] for d in (2, 3, 5, 6, 7)]
        for partner in partners:
            pl.semaphore_signal(barrier, inc=1, device_id=partner, device_id_type=MESH)
        return lambda: pl.semaphore_wait(barrier, len(partners))

    def slot(self, count=1):
        self.receives += count
        return self.receives - count

    def outbox(self, *wholes):
        self.sends += 1
        self.owed.append((self.sends - 1, wholes))
        return self.sends - 1

    def copy(self, src, dst, device, out, slot):
        return pltpu.make_async_remote_copy(
            src_ref=src,
            dst_ref=dst,
            send_sem=self.send_sem.at[out],
            recv_sem=self.recv_sem.at[slot],
            device_id=device,
            device_id_type=MESH,
        )

    def send(self, src, dst, device, out, slot):
        self.copy(src, dst, device, out, slot).start()

    def arrive(self, whole, slot):
        self.copy(whole, whole, self.device(), 0, slot).wait_recv()

    def drain(self):
        for out, wholes in self.owed:
            for whole in wholes:
                self.copy(whole, whole, self.device(), out, 0).wait_send()
        self.owed = []


def spot(lead, c=None, tail=(), **at):
    index = list(lead) + [slice(None) if c is None else c]
    for axis in "zyx":
        value = at.get(axis)
        half = isinstance(value, tuple)
        if axis == "y":
            index.append(pl.ds(2 * value[1], 2) if half else slice(None) if value is None else value)
        elif half:
            index += [value[1], slice(None)]
        elif value is None:
            index += [slice(None), slice(None)]
        else:
            index += [lax.div(value, 2), lax.rem(value, 2)]
    return tuple(index) + tail


def strip(sub):
    return (pl.ds(16 * sub, 16), slice(None))


def spread(index, count, width):
    row = lax.broadcasted_iota(jnp.int32, (128, width), 0)
    column = lax.broadcasted_iota(jnp.int32, (128, width), 1)
    return jnp.where((column == count * index + row) & (row < count), 1.0, 0.0)


def gather_phase(place, w, part, lean):
    c = place.c
    here = {"x": place.x, "y": place.y, "z": place.z}
    sibling = place.device(c=1 - c)
    blocks = {3: w.at[part, 0, 0, 0, 0:3, 0, 0], 12: w.at[part, 0, 0, 0, 0:3], 16: w.at[part, 0, 0, 0], 48: w.at[part, 0, :, :, 0:3], 64: w.at[part, 0]}
    passing, passed = place.outbox(blocks[64]), place.slot()

    def piece(sub, **at):
        return w.at[spot((part,), c, strip(sub), **at)]

    def pass_on(sub, **at):
        place.send(piece(sub, **at), piece(sub, **at), sibling, passing, passed)

    for stage, count in ((0, 3), (1, 12)):
        out, slot = place.outbox(blocks[count]), place.slot()
        for sub in range(3):
            axis, done = ORDERS[sub][stage], ORDERS[sub][:stage]
            own = piece(sub, **{a: here[a] for a in "xyz" if a not in done})
            for step in (1, 2, 3):
                place.send(own, own, place.device(**{axis: place.along(axis, step)}), out, slot)
        yield
        place.arrive(blocks[count], slot)
    out, sides, last = place.outbox(blocks[48]), place.slot(6), place.slot()

    def toward(axis, side):
        return place.device(**{axis: place.along(axis, 3 if side else 1)})

    for sub in range(3):
        axis = ORDERS[sub][2]
        own = piece(sub, **{axis: here[axis]})
        for side in range(2):
            place.send(own, own, toward(axis, side), out, sides + 2 * sub + side)
    for sub in range(3):
        axis = ORDERS[sub][2]
        pass_on(sub, **{axis: here[axis]})
    yield
    for side in range(2):
        for sub in range(3):
            axis, whole = ORDERS[sub][2], ORDERS[sub][0]
            came = {axis: place.along(axis, 1 if side else 3)}
            place.arrive(piece(sub, **came), sides + 2 * sub + side)
            down_only = lean and axis == "z"
            if not down_only or side == 1:
                half = piece(sub, **came) if down_only else piece(sub, **came, **{whole: ("half", side)})
                place.send(half, half, toward(axis, side), out, last)
            pass_on(sub, **came)
    yield
    place.arrive(blocks[16], last)
    for sub in range(3):
        axis = ORDERS[sub][2]
        pass_on(sub, **{axis: place.along(axis, 2)})
    yield
    place.arrive(blocks[64], passed)


HALF = {"z": "y", "x": "z", "y": "x"}
HALVES = {"z": (2, 2, 2), "x": (2, 4), "y": (2, 2, 2)}


def half_of(axis, h):
    return {"z": (pl.ds(2 * h, 2),), "x": (h,), "y": (slice(None), slice(None), h)}[axis]


def scatter_phase(place, g, lead, tails, arrivals, landed, lands, finish, relayed, lean):
    c = place.c
    here = {"x": place.x, "y": place.y, "z": place.z}
    tail = (slice(None), tails[0][1])
    corner = lead + (0, 0, 0)
    blocks = {
        3: g.at[corner + (pl.ds(0, 3), 0, 0) + tail],
        12: g.at[corner + (pl.ds(0, 3), slice(None), slice(None)) + tail],
        48: g.at[lead + (0, slice(None), slice(None), pl.ds(0, 3), slice(None), slice(None)) + tail],
    }

    def at(sub, **where):
        return spot(lead, c, tails[sub], **where)

    for index, slot in arrivals:
        place.arrive(landed.at[index], slot)
        g[lead + (c,) + index] = g[lead + (c,) + index] + landed[index]
    out = place.outbox(blocks[48])

    def ways(sub):
        axis = BACK[sub][0]
        way = [(t, place.device(**{axis: t})) for t in (place.along(axis, 1), place.along(axis, 3))]
        return axis, HALF[axis], way, (0, 0) if lean and axis == "z" else (0, 1)

    if relayed:
        relays, sides = place.slot(6), place.slot(3)
        for sub in range(3):
            axis, whole, way, course = ways(sub)
            across = place.along(axis, 2)
            for k in range(2):
                src = g.at[at(sub, **{axis: across, whole: ("half", k)})]
                place.send(src, lands[sub][0].at[k], way[course[k]][1], out, relays + 2 * sub + k)
        for sub in range(3):
            axis, whole, way, course = ways(sub)
            for k in range(2):
                toward = 1 - course[k]
                coordinate, device = way[toward]
                src = g.at[at(sub, **{axis: coordinate, whole: ("half", k)})]
                place.send(src, lands[sub][1].at[(toward,) + half_of(axis, k)], device, out, sides + sub)
        yield
        for sub in range(3):
            axis, whole, way, course = ways(sub)
            relay, side = lands[sub][:2]
            for k in range(2):
                coordinate, device = way[course[k]]
                place.arrive(relay.at[k], relays + 2 * sub + k)
                index = at(sub, **{axis: coordinate, whole: ("half", k)})
                g[index] = g[index] + relay[k]
                place.send(g.at[index], side.at[(course[k],) + half_of(axis, k)], device, out, sides + sub)
        yield
    else:
        sides = place.slot(3)
        for step in (2, 1, 3):
            for sub in range(3):
                axis = BACK[sub][0]
                there = place.along(axis, step)
                src = g.at[at(sub, **{axis: there})]
                place.send(src, lands[sub][1].at[step - 1], place.device(**{axis: there}), out, sides + sub)
        yield
    out, slot = place.outbox(blocks[12]), place.slot()
    for sub in range(3):
        axis, second = BACK[sub][0], BACK[sub][1]
        side = lands[sub][1]
        place.arrive(side, sides + sub)
        index = at(sub, **{axis: here[axis]})
        total = g[index].astype(F32)
        for k in range(side.shape[0]):
            total = total + side[k].astype(F32)
        g[index] = total.astype(BF16)
        for step in (1, 2, 3):
            there = place.along(second, step)
            src = g.at[at(sub, **{axis: here[axis], second: there})]
            place.send(src, lands[sub][2].at[step - 1], place.device(**{second: there}), out, slot)
    yield
    place.arrive(blocks[12], slot)
    out, slot = place.outbox(blocks[3]), place.slot()
    for sub in range(3):
        own = {a: here[a] for a in BACK[sub][:2]}
        third = BACK[sub][2]
        index = at(sub, **own)
        total = g[index].astype(F32)
        for step in range(3):
            total = total + lands[sub][2][step].astype(F32)
        g[index] = total.astype(BF16)
        for step in (1, 2, 3):
            there = place.along(third, step)
            src = g.at[at(sub, **own, **{third: there})]
            place.send(src, lands[sub][3].at[step - 1], place.device(**{third: there}), out, slot)
    yield
    place.arrive(blocks[3], slot)
    for sub in range(3):
        total = g[at(sub, **here)].astype(F32)
        for step in range(3):
            total = total + lands[sub][3][step].astype(F32)
        finish(sub, total)


def advance(*steps):
    for step in steps:
        next(step, None)


def remainder(value, count):
    value = value.astype(F32)
    whole = jnp.floor((value + 0.5) * (1.0 / count))
    return value - whole * count, whole


def gather_vectors(place, few, tiles, landed, vec):
    sublane = lax.broadcasted_iota(jnp.int32, (8, 128), 0)
    mine = place.c * 4 + place.x
    landed[3] = jnp.where(sublane == mine, few[...], 0.0)
    yield
    out, slot = place.outbox(landed.at[0:3]), place.slot()
    for step in (1, 2, 3):
        place.send(landed.at[3], landed.at[step - 1], place.device(x=place.along("x", step)), out, slot)
    yield
    place.arrive(landed.at[0:3], slot)
    landed[4] = landed[0] + landed[1] + landed[2] + landed[3]
    out, slot = place.outbox(landed.at[4]), place.slot()
    place.send(landed.at[4], landed.at[5], place.device(c=1 - place.c), out, slot)
    yield
    place.arrive(landed.at[5], slot)
    tiles[place.z, place.y] = landed[4] + landed[5]
    here = tiles.at[place.z, place.y]
    out, slot = place.outbox(landed.at[0:3]), place.slot()
    for step in (1, 2, 3):
        place.send(here, here, place.device(y=place.along("y", step)), out, slot)
    yield
    place.arrive(landed.at[0:3], slot)
    out, slot = place.outbox(tiles.at[0:3]), place.slot()
    for step in (1, 2, 3):
        place.send(tiles.at[place.z], tiles.at[place.z], place.device(z=place.along("z", step)), out, slot)
    yield
    place.arrive(tiles.at[0:3], slot)
    table = tiles[...].reshape(128, 128).astype(BF16)
    row = lax.broadcasted_iota(jnp.int32, (128, 1), 0)
    z, y, core, x = row // 32, (row // 8) % 4, (row // 4) % 2, row % 4
    device = ((z // 2) * 64 + y * 16 + x * 4 + core * 2 + z % 2).astype(F32)
    for count, width, firsts in ((6, D, (0, 6)), (18, 3 * D, (12, 30, 48))):
        part, owner = remainder(lax.broadcasted_iota(jnp.int32, (1, width), 1), count)
        lane = lax.broadcasted_iota(jnp.int32, (128, 1), 0).astype(F32)
        for first in firsts:
            choose = jnp.where(lane - first == part, 1.0, 0.0).astype(BF16)
            spread_out = nn(table, choose)
            vector = jnp.sum(jnp.where(device == owner, spread_out, 0.0), axis=0, keepdims=True)
            base = first if count == 6 else first
            for k in range(width // 128):
                vec[base + k:base + k + 1, :] = vector[:, 128 * k:128 * (k + 1)]


def sum_vectors(place, vec, incoming):
    for stage, axis in enumerate("cxyz"):
        steps = (1,) if axis == "c" else (1, 2, 3)
        whole = incoming.at[stage, 0:len(steps)]
        out, slot = place.outbox(whole), place.slot()
        for k, step in enumerate(steps):
            device = place.device(c=1 - place.c) if axis == "c" else place.device(**{axis: place.along(axis, step)})
            place.send(vec.at[stage], incoming.at[stage, k], device, out, slot)
        yield
        place.arrive(whole, slot)
        total = vec[stage]
        for k in range(len(steps)):
            total = total + incoming[stage, k]
        vec[stage + 1] = total


def nt(left, right):
    return lax.dot_general(left, right, (((1,), (1,)), ((), ())), preferred_element_type=F32)


def tn(left, right):
    return lax.dot_general(left, right, (((0,), (0,)), ((), ())), preferred_element_type=F32)


def nn(left, right):
    return jnp.dot(left, right, preferred_element_type=F32)


def columns(ref, part, jp):
    halves = [ref[part, lax.rem(jp, 2), :, zl, :, :, lax.div(jp, 2)].reshape(D, 384) for zl in range(2)]
    return jnp.concatenate(halves, axis=1)


def tile_at(t):
    j, q = READY.index(t) % 8, READY.index(t) // 8
    xl, c, zl = j // 4, j // 2 % 2, j % 2
    every = slice(None)
    return (c, every, zl, every, every, xl, every, pl.ds(128 * q, 128))


def tiles_of(w, wanted):
    return jnp.concatenate([w[(0,) + tile_at(t)].reshape(D, 128) for t in wanted], axis=1)


def put_tiles(g, wanted, value):
    low = value.astype(BF16)
    for k, t in enumerate(wanted):
        g[(2,) + tile_at(t)] = low[:, 128 * k:128 * (k + 1)].reshape(2, 4, 2, 48, 128)


def put_columns(ref, part, jp, value):
    for zl in range(2):
        ref[part, lax.rem(jp, 2), :, zl, :, :, lax.div(jp, 2)] = (
            value[:, zl * 384:(zl + 1) * 384].astype(BF16).reshape(2, 4, 2, 48, 384)
        )


def row_pieces():
    return [(y, xh, xl, c) for y in range(2) for xh in range(2) for xl in range(2) for c in range(2)]


def rows(ref, jp):
    zh, y0 = lax.div(jp, 2), lax.rem(jp, 2) * 2
    halves = [
        jnp.concatenate([ref[2, c, zh, zl, y0 + y, xh, xl] for y, xh, xl, c in row_pieces()], axis=0) for zl in range(2)
    ]
    return jnp.concatenate(halves, axis=1)


def put_rows(ref, jp, value):
    zh, y0 = lax.div(jp, 2), lax.rem(jp, 2) * 2
    low = value.astype(BF16)
    for zl in range(2):
        for k, (y, xh, xl, c) in enumerate(row_pieces()):
            ref[c, zh, zl, y0 + y, xh, xl] = low[48 * k:48 * k + 48, zl * 384:(zl + 1) * 384]


def normalize(values):
    mean = jnp.mean(values, axis=-1, keepdims=True)
    centred = values - mean
    inverse = lax.rsqrt(jnp.mean(centred * centred, axis=-1, keepdims=True) + EPS)
    return centred * inverse, inverse


def norm_back(grad, normed, inverse):
    first = jnp.mean(grad, axis=-1, keepdims=True)
    second = jnp.mean(grad * normed, axis=-1, keepdims=True)
    return inverse * (grad - first - normed * second)


def shifted(values, steps):
    count = values.shape[0]
    row = lax.broadcasted_iota(jnp.int32, values.shape, 0)
    rolled = pltpu.roll(values, steps % count, 0)
    return jnp.where(row >= steps if steps > 0 else row < count + steps, rolled, 0.0)


def layer_kernel(tok, cot, wq, wo, wu, wd, ga, gf, taps, out, gtok, gq, go, gu, gd, gga, ggf, gtap, *scratch):
    (w, g0, h1t, h2t, from_core, to_peer, from_peer, pile, down_s, down, few, tiles, few_landed, vec, prev, h1, raw, mixed, bias,
     probs, att, h2, act, gup, gh2, gatt, acc, contrib, got, gvec, incoming, sums) = scratch[:32]
    lands, (send_sem, recv_sem) = scratch[32:-2], scratch[-2:]
    place = Place(send_sem, recv_sem)
    c, zl, rank = place.c, place.zl, place.zl
    ready = place.greet()
    for number in range(8):
        for q in range(3):
            t = READY[8 * q + number]
            source = wq[:, t * 128:(t + 1) * 128] if t < 18 else wo[:, (t - 18) * 128:(t - 17) * 128]
            to_peer[0, number, 0:6, q * 128:(q + 1) * 128] = source.astype(F32)
        to_peer[1, number, 0:6, :] = wu[:, number * 384:(number + 1) * 384].astype(F32)
    left, right = wd[:, 0:384].astype(F32), wd[:, 384:768].astype(F32)
    down_s[...] = jnp.where(zl == 0, right, left)
    down[pl.ds(pl.multiple_of(zl * 24, 8), 24), :] = jnp.where(zl == 0, left, right)
    few[...] = jnp.zeros_like(few)
    few[0:1, 0:6] = ga[...].astype(F32)
    few[0:1, 6:12] = gf[...].astype(F32)
    for j in range(3):
        few[0:1, 12 + 18 * j:30 + 18 * j] = taps[j:j + 1, :].astype(F32)
    few[...] = jnp.broadcast_to(few[0:1, :], (8, 128))
    vectors = gather_vectors(place, few, tiles, few_landed, vec)
    advance(vectors)
    ready()

    other = place.device(z=place.flip(place.z, 1))
    trades, trade_down, token_slot, back_slot = place.slot(2), place.slot(), place.slot(), place.slot()
    out_trades, out_down = [place.outbox(from_peer.at[0, 0:7]) for _ in range(2)], place.outbox(down_s)
    out_tokens = place.outbox()
    _, mine = place.member(0)
    def trade(k):
        for d in range(1, 8):
            device, number = place.member(d)
            place.send(to_peer.at[k, number], from_peer.at[k, mine], device, out_trades[k], trades + k)

    def send_tokens(k):
        piece = pl.ds(64 * k, 64)

        @pl.when(zl == 0)
        def _():
            place.send(tok.at[piece], prev.at[piece], other, out_tokens, token_slot)

    trade(0)
    trade(1)
    place.send(down_s, down.at[pl.ds(pl.multiple_of(zl * 24, 8), 24)], other, out_down, trade_down)
    next(vectors)

    for k in range(2):
        from_peer[k, mine] = to_peer[k, mine]

    def normalize_half(half):
        return normalize((prev if half == 0 else tok)[...].astype(F32))

    send_tokens(0)
    place.arrive(down_s, trade_down)
    at = (c, lax.div(place.z, 2), zl, place.y, lax.div(place.x, 2), lax.rem(place.x, 2))
    for k in range(2):
        place.arrive(from_peer.at[k, 0:7], trades + k)
        for number in range(8):
            pile[k, 6 * number:6 * number + 8, :] = from_peer[k, number]
        w[(k,) + at] = pile[k, 0:48, :].astype(BF16)
    w[(2,) + at] = down[...].astype(BF16)
    phase = [gather_phase(place, w, part, LEAN_IN[part]) for part in range(3)]
    advance(vectors)
    for k in range(2):
        advance(*phase)
        send_tokens(k + 1)
        advance(vectors)
    advance(phase[0], phase[1])
    send_tokens(3)
    advance(vectors)

    advance(phase[0], phase[2], phase[1])

    @pl.when(zl == 1)
    def _():
        place.arrive(prev, token_slot)

    @pl.when(zl == 0)
    def _():
        prev[...] = jnp.zeros_like(prev)

    gain_one = jnp.concatenate([vec[r:r + 1, :] for r in range(6)], axis=1)
    gain_two = jnp.concatenate([vec[r:r + 1, :] for r in range(6, 12)], axis=1)
    for half in range(2):
        h1[half * ROWS:(half + 1) * ROWS, :] = (normalize_half(half)[0] * gain_one).astype(BF16)
    h1t[...] = h1[...].T
    row = lax.broadcasted_iota(jnp.int32, (ROWS, EXT), 0)
    column = lax.broadcasted_iota(jnp.int32, (ROWS, EXT), 1)
    behind = jnp.where(column < ROWS, (1 - rank) * EXT, column - ROWS)
    bias[...] = jnp.where(behind <= row, 0.0, -1e30)
    first = lax.broadcasted_iota(jnp.int32, (ROWS, 128), 1) < 64
    gvec[0] = jnp.zeros((VEC, 128), F32)
    advance(phase[0], phase[2], phase[0])

    def tap(j, t):
        return vec[pl.ds(12 + TILES * j + t, 1), :]

    for jp in range(3):
        block = nn(h1[...], tiles_of(w, range(6 * jp, 6 * jp + 6))).astype(BF16)
        for k in range(6):
            t = 6 * jp + k
            tile = block[:, 128 * k:128 * (k + 1)]
            raw[t] = tile
            value = tile.astype(F32)
            conv = tap(0, t) * value + tap(1, t) * shifted(value, 1) + tap(2, t) * shifted(value, 2)
            mixed[t] = conv.astype(BF16)

    def both(value):
        zero = jnp.zeros_like(value)
        return jnp.concatenate([jnp.where(first, value, zero), jnp.where(first, zero, value)], axis=0)

    def pick(value):
        return jnp.where(first, value[:ROWS], value[ROWS:])

    def attend(p):
        query = both(mixed[p, ROWS:, :])
        key, value = mixed[PAIRS + p], mixed[2 * PAIRS + p]
        scores = nt(query, key) * 0.125 + jnp.concatenate([bias[...], bias[...]], axis=0)
        weights = jnp.exp(scores - jnp.max(scores, axis=-1, keepdims=True))
        exact = weights * (1.0 / jnp.sum(weights, axis=-1, keepdims=True))
        probs[p] = exact
        att[p] = pick(nn(exact.astype(BF16), value)).astype(BF16)

    advance(phase[1])
    for p in range(PAIRS):
        attend(p)
        if p == 0:
            advance(phase[2])

    attended = jnp.concatenate([att[p] for p in range(PAIRS)], axis=1)
    resid = tok[...].astype(F32) + nn(attended, tiles_of(w, range(18, 24)))
    normed_two, inverse_two = normalize(resid)
    h2[...] = (normed_two * gain_two).astype(BF16)
    h2t[...] = h2[...].T
    acc[...] = resid
    advance(phase[1], phase[1], phase[1])
    inward, place.owed = place.owed, []
    sibling = place.device(c=1 - c)
    across = [place.slot(3), place.slot(2), place.slot(4)]
    out_across = [place.outbox(w.at[part, 0]) for part in range(3)]
    every = slice(None)
    strips = [strip(sub) for sub in range(3)]

    def finish(part):
        def store(sub, total):
            sums[part, 16 * sub:16 * sub + 16, :] = total
        return store

    def finish_chunk(first, width):
        def store(sub, total):
            sums[0, 16 * sub:16 * sub + 16, first:first + width] = total
        return store

    def land(k):
        return [lands[12 * k + 4 * sub:12 * k + 4 * sub + 4] for sub in range(3)]

    def cross(k):
        cut = (1 - c,) + (every,) * 6 + (pl.ds(*CHUNKS[k]),)
        place.send(w.at[(2,) + cut], from_core.at[(0,) + cut[1:]], sibling, out_across[0], across[0] + k)

    up_ready = [((every,) * 4 + (xl,), across[1] + xl) for xl in range(2)]
    down_ready = [((jp // 2, every, pl.ds(jp % 2 * 2, 2)), across[2] + jp) for jp in range(4)]
    ups = scatter_phase(place, w, (1,), strips, up_ready, from_core.at[1], land(2), finish(1), True, LEAN_OUT[1])
    downs = scatter_phase(place, g0, (), strips, down_ready, from_core.at[2], land(3), finish(2), True, LEAN_OUT[2])
    chunks = []
    for k, (start, width) in enumerate(CHUNKS):
        cut = (pl.ds(start, width),)
        came = [((every,) * 6 + cut, across[0] + k)]
        tails = [(pl.ds(16 * sub, 16),) + cut for sub in range(3)]
        chunks.append(scatter_phase(place, w, (2,), tails, came, from_core.at[0], land(k), finish_chunk(start, width), k == 0, LEAN_OUT[0]))

    @pl.loop(0, 4)
    def _(jp):
        rect = jnp.maximum(nn(h2[...], columns(w, 1, jp)), 0.0)
        act[jp] = (rect * rect).astype(BF16)
        gup[jp] = rect.astype(BF16)
        put_rows(g0, jp, tn(act[jp], cot[...]))
        some = (lax.div(jp, 2), slice(None), pl.ds(lax.rem(jp, 2) * 2, 2))
        place.send(g0.at[(1 - c,) + some], from_core.at[(2,) + some], sibling, out_across[2], across[2] + jp)

    for _ in range(6):
        advance(phase[2])
    place.owed, outward = inward, place.owed
    place.drain()
    place.owed = outward

    @pl.when(zl == 0)
    def _():
        place.copy(tok, tok, other, out_tokens, 0).wait_send()

    def narrow(jp):
        low = rows(w, jp)
        gup[jp] = (nt(cot[...], low) * 2.0 * gup[jp].astype(F32)).astype(BF16)
        acc[...] += nn(act[jp], low)

    pl.loop(0, 2)(narrow)
    advance(downs)
    pl.loop(2, 4)(narrow)
    gh2[...] = jnp.zeros_like(gh2)

    def widen(jp):
        gh2[...] += nt(gup[jp], columns(w, 1, jp))
        put_columns(w, 1, jp, nn(h2t[...], gup[jp]))

        @pl.when(lax.rem(jp, 2) == 1 - c)
        def _():
            xl = lax.div(jp, 2)
            src, dst = w.at[1, 1 - c, :, :, :, :, xl], from_core.at[1, :, :, :, :, xl]
            place.send(src, dst, sibling, out_across[1], across[1] + xl)

    pl.loop(0, 4)(widen)
    out[...] = acc[...].astype(BF16)
    grad_two = gh2[...]
    summed = jnp.sum(grad_two * normed_two, axis=0, keepdims=True)
    for r in range(6):
        gvec[0, 6 + r:7 + r, :] = summed[:, 128 * r:128 * (r + 1)]
    grad_resid = cot[...].astype(F32) + norm_back(grad_two * gain_two, normed_two, inverse_two)
    acc[...] = grad_resid
    gproj = grad_resid.astype(BF16)
    gback = nt(gproj, tiles_of(w, range(18, 24))).astype(BF16)
    for p in range(PAIRS):
        gatt[p] = gback[:, 128 * p:128 * (p + 1)]
    put_tiles(w, range(18, 24), tn(attended, gproj))

    def attend_back(p):
        query = both(mixed[p, ROWS:, :])
        key, value = mixed[PAIRS + p], mixed[2 * PAIRS + p]
        grad = both(gatt[p])
        exact = probs[p]
        gvalue = tn(exact.astype(BF16), grad)
        gprobs = nt(grad, value)
        centred = gprobs - jnp.sum(gprobs * exact, axis=-1, keepdims=True)
        gscores = (exact * centred).astype(BF16)
        gquery = pick(nn(gscores, key)) * 0.125
        gkey = tn(gscores, query) * 0.125
        for k, tile in enumerate((jnp.concatenate([jnp.zeros_like(gquery), gquery], axis=0), gkey, gvalue)):
            t = PAIRS * k + p
            back = tap(0, t) * tile + tap(1, t) * shifted(tile, -1) + tap(2, t) * shifted(tile, -2)
            mixed[t] = back.astype(BF16)
            value_in = raw[t].astype(F32)
            for j in range(3):
                delayed = value_in if j == 0 else shifted(value_in, j)
                gvec[0, pl.ds(12 + TILES * j + t, 1), :] = jnp.sum(tile * delayed, axis=0, keepdims=True)

    def weigh(wanted):
        put_tiles(w, wanted, nn(h1t[...], jnp.concatenate([mixed[t] for t in wanted], axis=1)))

    attend_back(0)
    advance(ups)
    attend_back(1)
    attend_back(2)
    attend_back(3)
    weigh(READY[6:16])
    cross(0)
    advance(downs)
    attend_back(4)
    attend_back(5)
    advance(chunks[0])
    weigh(READY[16:24])
    cross(1)
    out_back = place.outbox()

    def through_norm(half):
        here = pl.ds(half * ROWS, ROWS)
        grad_one = jnp.zeros((ROWS, D), F32)
        for jp in range(3):
            grad = jnp.concatenate([mixed[6 * jp + k, here, :] for k in range(6)], axis=1)
            grad_one = grad_one + nt(grad, tiles_of(w, range(6 * jp, 6 * jp + 6)))
        normed, inverse = normalize_half(half)
        return jnp.sum(grad_one * normed, axis=0, keepdims=True), norm_back(grad_one * gain_one, normed, inverse)

    def send_back(k):
        piece = pl.ds(64 * k, 64)

        @pl.when(zl == 1)
        def _():
            place.send(contrib.at[piece], got.at[piece], other, out_back, back_slot)

    advance(ups)
    total, back = through_norm(0)
    contrib[...] = back.astype(BF16)
    send_back(0)
    gain, back = through_norm(1)
    acc[...] += back
    total = total + gain
    for r in range(6):
        gvec[0, r:r + 1, :] = total[:, 128 * r:128 * (r + 1)]
    small = sum_vectors(place, gvec, incoming)
    advance(small)
    advance(chunks[1])
    advance(small)
    advance(chunks[0])
    send_back(1)
    advance(downs, ups, chunks[1])
    advance(small)
    advance(chunks[0])
    send_back(2)
    advance(downs, ups, chunks[1])
    advance(small)
    advance(chunks[0])
    send_back(3)
    advance(downs, ups)

    trades, trade_down = place.slot(2), place.slot()
    back_from, arrived = pile.at[0, pl.ds(0, 24)], from_peer
    out_trades, out_down = [place.outbox(from_peer.at[0, 0:7]) for _ in range(2)], place.outbox(back_from)

    def hand_back(k):
        for number in range(8):
            to_peer[k, number, 0:6, :] = sums[k, 6 * number:6 * number + 6, :]
        for d in range(1, 8):
            device, number = place.member(d)
            place.send(to_peer.at[k, number], arrived.at[k, mine], device, out_trades[k], trades + k)
        arrived[k, mine] = to_peer[k, mine]

    hand_back(1)
    place.send(sums.at[2, pl.ds(pl.multiple_of((1 - zl) * 24, 8), 24)], back_from, other, out_down, trade_down)
    advance(chunks[1], chunks[0])
    hand_back(0)
    advance(small, small)
    summed = gvec[4]
    gains = [jnp.concatenate([summed[r:r + 1] for r in range(6 * k, 6 * k + 6)], axis=1) for k in range(2)]
    tapped = [jnp.concatenate([summed[r:r + 1] for r in range(12 + TILES * j, 12 + TILES * j + TILES)], axis=1) for j in range(3)]
    gain_rows = jnp.concatenate(gains + [jnp.zeros((6, D), F32)], axis=0)
    tap_rows = jnp.concatenate(tapped + [jnp.zeros((5, 3 * D), F32)], axis=0)
    exactly = functools.partial(
        lax.dot_general,
        dimension_numbers=(((1,), (1,)), ((), ())),
        preferred_element_type=F32,
        precision=lax.Precision.HIGHEST,
    )
    gain_own = exactly(gain_rows, spread(place.index, 6, D))
    gga[...] = gain_own[0:1, 0:6]
    ggf[...] = gain_own[1:2, 0:6]
    gtap[...] = exactly(tap_rows, spread(place.index, 18, 3 * D))[0:3, 0:18]

    @pl.when(zl == 0)
    def _():
        place.arrive(got, back_slot)

    @pl.when(zl == 1)
    def _():
        got[...] = jnp.zeros_like(got)

    gtok[...] = (acc[...] + got[...].astype(F32)).astype(BF16)
    for k in range(2):
        place.arrive(arrived.at[k, 0:7], trades + k)
    place.arrive(back_from, trade_down)
    for number in range(8):
        for q in range(3):
            t = READY[8 * q + number]
            tile = arrived[0, number, 0:6, 128 * q:128 * (q + 1)]
            if t < 18:
                gq[:, 128 * t:128 * (t + 1)] = tile
            else:
                go[:, 128 * (t - 18):128 * (t - 17)] = tile
        gu[:, 384 * number:384 * (number + 1)] = arrived[1, number, 0:6, :]
    own = sums[2, pl.ds(pl.multiple_of(zl * 24, 8), 24), :]
    theirs = pile[0, 0:24, :]
    gd[:, 0:384] = jnp.where(zl == 0, own, theirs)
    gd[:, 384:768] = jnp.where(zl == 0, theirs, own)
    place.drain()

    @pl.when(zl == 1)
    def _():
        place.copy(contrib, contrib, other, out_back, 0).wait_send()


def kept(axes):
    grid = []
    for axis in "zyx":
        if axis not in axes:
            grid += {"z": [2, 2], "y": [4], "x": [2, 2]}[axis]
    return tuple(grid)


RESULTS = (
    ((ROWS, D), BF16),
    ((ROWS, D), BF16),
    ((6, 2304), F32),
    ((6, 768), F32),
    ((6, 3072), F32),
    ((24, 768), F32),
    ((1, 6), F32),
    ((1, 6), F32),
    ((3, 18), F32),
)


def layer(*args):
    vmem = pl.BlockSpec(memory_space=pltpu.VMEM)
    lands = []
    for k in range(4):
        for sub in range(3):
            order = BACK[sub]
            grids = [(2,) + HALVES[order[0]], (2,) + kept(order[:1]), (3,) + kept(order[:2]), (3,)]
            if k == 1:
                grids[:2] = [(1,), (3,) + kept(order[:1])]
            lands += [pltpu.VMEM(grid + (16, CHUNKS[k][1] if k < 2 else 384), BF16) for grid in grids]
    return pl.pallas_call(
        layer_kernel,
        out_shape=tuple(jax.ShapeDtypeStruct(*result) for result in RESULTS),
        in_specs=[vmem] * 9,
        out_specs=(vmem,) * 9,
        scratch_shapes=[
            pltpu.VMEM((3,) + GRID + BLOCK, BF16),
            pltpu.VMEM(GRID + BLOCK, BF16),
            pltpu.VMEM((D, EXT), BF16),
            pltpu.VMEM((D, ROWS), BF16),
            pltpu.VMEM((3,) + GRID[1:] + BLOCK, BF16),
            pltpu.VMEM((2, 8, 8, 384), F32),
            pltpu.VMEM((2, 8, 8, 384), F32),
            pltpu.VMEM((2, 56, 384), F32),
            pltpu.VMEM((24, 384), F32),
            pltpu.VMEM((48, 384), F32),
            pltpu.VMEM((8, 128), F32),
            pltpu.VMEM((4, 4, 8, 128), F32),
            pltpu.VMEM((8, 8, 128), F32),
            pltpu.VMEM((VEC, 128), F32),
            pltpu.VMEM((ROWS, D), BF16),
            pltpu.VMEM((EXT, D), BF16),
            pltpu.VMEM((TILES, EXT, 128), BF16),
            pltpu.VMEM((TILES, EXT, 128), BF16),
            pltpu.VMEM((ROWS, EXT), F32),
            pltpu.VMEM((PAIRS, EXT, EXT), F32),
            pltpu.VMEM((PAIRS, ROWS, 128), BF16),
            pltpu.VMEM((ROWS, D), BF16),
            pltpu.VMEM((4, ROWS, D), BF16),
            pltpu.VMEM((4, ROWS, D), BF16),
            pltpu.VMEM((ROWS, D), F32),
            pltpu.VMEM((PAIRS, ROWS, 128), BF16),
            pltpu.VMEM((ROWS, D), F32),
            pltpu.VMEM((ROWS, D), BF16),
            pltpu.VMEM((ROWS, D), BF16),
            pltpu.VMEM((5, VEC, 128), F32),
            pltpu.VMEM((4, 3, VEC, 128), F32),
            pltpu.VMEM((3,) + BLOCK, F32),
            *lands,
            pltpu.SemaphoreType.DMA((43,)),
            pltpu.SemaphoreType.DMA((93,)),
        ],
        compiler_params=pltpu.CompilerParams(collective_id=0, has_side_effects=True, vmem_limit_bytes=LIMIT),
    )(*args)


def copy_kernel(*refs):
    for source, target in zip(refs[:len(RESULTS)], refs[len(RESULTS):]):
        target[...] = source[...]


def copied(*args):
    vmem = pl.BlockSpec(memory_space=pltpu.VMEM)
    return pl.pallas_call(
        copy_kernel,
        out_shape=tuple(jax.ShapeDtypeStruct(*result) for result in RESULTS),
        in_specs=[vmem] * len(RESULTS),
        out_specs=(vmem,) * len(RESULTS),
    )(*args)


def per_device(tokens, w_qkv, w_out, w_up, w_down, gain_attn, gain_ffn, conv_taps, cotangent):
    results = copied(*layer(
        tokens, cotangent, w_qkv, w_out, w_up, w_down, gain_attn.reshape(1, 6), gain_ffn.reshape(1, 6), conv_taps
    ))
    return results[:6] + (results[6].reshape(6), results[7].reshape(6), results[8])


def solution(mesh):
    both = ("grp", "seq")
    row, one, column = P(both, None), P(both), P(None, both)
    return jax.shard_map(
        per_device,
        mesh=mesh,
        in_specs=(row, row, row, row, row, one, one, column, row),
        out_specs=(row, row, row, row, row, row, one, one, column),
        check_vma=False,
    )
```
